256 devices in a mesh: blk: 8 (over x, y_lo), rep: 32 (over y_hi, z, core).
Axes of the slice: x: 4, y: 4 (y_hi: 2, y_lo: 2; y = y_hi * 2 + y_lo), z: 8, core: 2. Of those that a mesh axis runs over, the one named last changes fastest.
Arguments:
- tokens: bfloat16 [65536, 4096], P(('blk', 'rep'))
- grad_attended: bfloat16 [65536, 1024], P(('blk', 'rep'))
- doc_ids: int32 [256, 256], P(('blk', 'rep')), may hold values from 0 to 3, never falling along the last dimension, each value on 1 to 128 neighbouring positions
- w_qkv: bfloat16 [4096, 1280], P('blk')
Outputs:
- d_tokens: bfloat16 [65536, 4096], P(('blk', 'rep'))
- grad_qkv: bfloat16 [4096, 1280], P('blk')
The draws below stay inside these ranges and needn't reach their ends.
Inputs may be any that keep to these rules, and one draw needn't show every extreme that they name: `doc_ids`: along each row ids never fall; every document holds 1 to 128 tokens.
All inputs are finite; a program needn't handle non-finite values.
Results may differ from the reference program's by a relative error of at most 0.035.
Values may be sent and summed in bfloat16 or wider, within the bound.
No kernel may reach another device: no remote copies, remote signals or barrier semaphores. Data moves between devices by JAX's collectives and lax.ppermute only.
A program may use at most 128 MiB of HBM per device.

```python
import math
import jax
import jax.numpy as jnp
import numpy as np
from jax import lax

D = 4096
HD = 128
QH = 8
TOK_DEV = 256
QKV = 1280
OUTW = 1024
SEQS = 256
TOKENS = 65536


def draw_tokens(key, part):
    key = jax.random.fold_in(key, 11)
    k_base, k_rows = jax.random.split(key)
    cols = jnp.exp(jnp.log(10.0) * jnp.arange(D, dtype=jnp.float32) / (D - 1))
    rows = jnp.exp(jax.random.uniform(k_rows, (TOKENS, 1), jnp.float32, jnp.log(0.1), 0.0))
    base = jax.random.normal(k_base, (TOKENS, D), jnp.float32)
    return (base * rows * cols).astype(jnp.bfloat16)


def draw_grad_attended(key, part):
    key = jax.random.fold_in(key, 13)
    k_base, k_rows = jax.random.split(key)
    cols = jnp.exp(jnp.log(3.0) * jnp.arange(OUTW, dtype=jnp.float32) / (OUTW - 1))
    rows = jnp.exp(jax.random.uniform(k_rows, (TOKENS, 1), jnp.float32, jnp.log(0.3), jnp.log(3.0)))
    base = jax.random.normal(k_base, (TOKENS, OUTW), jnp.float32)
    return (base * rows * cols).astype(jnp.bfloat16)


def draw_w_qkv(key, part):
    key = jax.random.fold_in(key, 17)
    base = jax.random.normal(key, (D, QKV), jnp.float32) / jnp.sqrt(1.0 * D)
    return base.astype(jnp.bfloat16)


def split_up(count, total, bound, skew):
    weights = [(1 << 20) // math.isqrt(standing ** skew) + 1 for standing in range(2, count + 1)]
    surplus, holding = total - bound - (count - 1), [1] * (count - 1)
    while surplus > 0:
        movable = [i for i in range(count - 1) if holding[i] < bound]
        whole, remaining = sum([weights[i] for i in movable]), surplus
        for i in movable:
            more = min(bound - holding[i], max(1, remaining * weights[i] // whole), surplus)
            holding[i] = holding[i] + more
            surplus = surplus - more
    return np.array([bound] + holding)


def uneven_parts(own_key, number_of, total, bound, skew):
    if number_of == 2:
        one = jax.random.randint(own_key, (), max(1, total - bound), min(bound, total - 1) + 1)
        return jnp.stack([one, total - one])
    lengths = jnp.asarray(split_up(number_of, total, bound, skew), jnp.int32)
    twos = (number_of - 1) // 2
    donor, sink = lengths[1:1 + 2 * twos:2], lengths[2:2 + 2 * twos:2]
    room = jnp.minimum(donor - 1, bound - sink)
    passed = jax.random.randint(jax.random.fold_in(own_key, 1), (twos,), 0, 1 << 20) % (room + 1)
    lengths = lengths.at[1:1 + 2 * twos:2].set(donor - passed).at[2:2 + 2 * twos:2].set(sink + passed)
    return lengths[jax.random.permutation(jax.random.fold_in(own_key, 2), number_of)]


def setup_inputs(seed: int = 0) -> dict:
    seeds = jax.random.split(jax.random.key(seed), 5)
    tokens = draw_tokens(jax.random.fold_in(seeds[4], 71), 0)
    grad_attended = draw_grad_attended(jax.random.fold_in(seeds[4], 71), 0)
    doc_ids = jax.vmap(lambda own: jnp.searchsorted(jnp.cumsum(uneven_parts(own, 4, TOK_DEV, TOK_DEV // 2, 0)), jnp.arange(TOK_DEV), side="right"))(jax.random.split(seeds[2], SEQS)).reshape((SEQS, TOK_DEV)).astype(jnp.int32)
    w_qkv = draw_w_qkv(jax.random.fold_in(seeds[4], 71), 0)
    return {"tokens": tokens, "grad_attended": grad_attended, "doc_ids": doc_ids, "w_qkv": w_qkv}


target_rms = 0.5
rope_base = 500000.0

def rounded(value):
    return lax.optimization_barrier(value.astype(jnp.bfloat16)).astype(jnp.float32)

def tables(count, head):
    position = jnp.arange(count, dtype=jnp.float32)
    freq = jnp.exp(-jnp.log(rope_base) * 2.0 * jnp.arange(head // 2, dtype=jnp.float32) / head)
    angle = position[:, None] * freq[None, :]
    return (jnp.cos(angle), jnp.sin(angle))

def rotate(value, cosine, sine, sign):
    half = value.shape[-1] // 2
    first = value[..., :half]
    second = value[..., half:]
    return jnp.concatenate([first * cosine - sign * second * sine, second * cosine + sign * first * sine], axis=-1)

def attention_grads(tokens, grad_attended, doc, w_qkv, heads, head):
    count = tokens.shape[0]
    width = heads * head
    full = tokens.astype(jnp.float32)
    scale_r = lax.rsqrt(lax.optimization_barrier(jnp.mean(full * full, axis=1, keepdims=True)) + 1e-05)
    normed = (full * scale_r).astype(jnp.bfloat16)
    qkv = jnp.dot(normed, w_qkv, preferred_element_type=jnp.float32)
    query = qkv[:, :width].reshape(count, heads, head)
    keys = qkv[:, width:width + head]
    values = qkv[:, width + head:]
    cosine, sine = tables(count, head)
    q_rot = rotate(query, cosine[:, None, :], sine[:, None, :], 1.0).astype(jnp.bfloat16).astype(jnp.float32)
    k_rot = rotate(keys, cosine, sine, 1.0).astype(jnp.bfloat16).astype(jnp.float32)
    v_rnd = values.astype(jnp.bfloat16).astype(jnp.float32)
    factor = head ** (-0.5)
    scores = jnp.einsum('thd,ud->htu', q_rot, k_rot) * factor
    position = jnp.arange(count)
    allowed = (position[None, :] <= position[:, None]) & (doc[:, None] == doc[None, :])
    scores = jnp.where(allowed[None], scores, -1e+30)
    top = lax.optimization_barrier(jnp.max(scores, axis=-1, keepdims=True))
    expo = jnp.exp(scores - top)
    probs = expo / lax.optimization_barrier(jnp.sum(expo, axis=-1, keepdims=True))
    probs_b = rounded(probs)
    d_heads = grad_attended.astype(jnp.float32).reshape(count, heads, head)
    d_probs = jnp.einsum('thd,ud->htu', d_heads, v_rnd)
    d_v = jnp.einsum('htu,thd->ud', probs_b, d_heads)
    d_scores = probs * (d_probs - lax.optimization_barrier(jnp.sum(d_probs * probs, axis=-1, keepdims=True))) * factor
    d_scores = rounded(d_scores)
    d_qrot = jnp.einsum('htu,ud->thd', d_scores, k_rot)
    d_krot = jnp.einsum('htu,thd->ud', d_scores, q_rot)
    d_q = rotate(d_qrot, cosine[:, None, :], sine[:, None, :], -1.0).reshape(count, width)
    d_k = rotate(d_krot, cosine, sine, -1.0)
    d_qkv = jnp.concatenate([d_q, d_k, d_v], axis=1).astype(jnp.bfloat16)
    d_normed = lax.dot_general(d_qkv, w_qkv, (((1,), (1,)), ((), ())), preferred_element_type=jnp.float32)
    d_norm = scale_r * d_normed - full * scale_r ** 3 * lax.optimization_barrier(jnp.mean(d_normed * full, axis=1, keepdims=True))
    d_tokens = d_norm.astype(jnp.bfloat16)
    return (d_tokens, normed, d_qkv)

def grad_term(normed, d_qkv, start, count):
    normed_cols = lax.dynamic_slice_in_dim(normed, start, count, 1)
    first = lax.dot_general(normed_cols, d_qkv, (((0,), (0,)), ((), ())), preferred_element_type=jnp.float32)
    return rounded(first)

def rescale_factor(squares, entries):
    return target_rms * lax.rsqrt(squares / entries + 1e-06)

def reference(tokens, grad_attended, doc_ids, w_qkv):
    seq_count = doc_ids.shape[0]
    length = doc_ids.shape[1]
    token_blocks = tokens.reshape(seq_count, length, D)
    grad_blocks = grad_attended.reshape(seq_count, length, OUTW)

    def step(total, item):
        block_tok, block_grad, doc = item
        d_tok, normed, d_qkv = attention_grads(block_tok, block_grad, doc, w_qkv, QH, HD)
        term = grad_term(normed, d_qkv, 0, D)
        return (total + term, d_tok)
    start = jnp.zeros((D, QKV), jnp.float32)
    total, d_blocks = lax.scan(step, start, (token_blocks, grad_blocks, doc_ids))
    factor = rescale_factor(jnp.sum(total * total), D * QKV)
    rescaled = (total * factor).astype(jnp.bfloat16)
    return (d_blocks.reshape(seq_count * length, D), rescaled)
```

```python
import jax
import jax.numpy as jnp
from jax import lax
from jax.experimental import pallas as pl
from jax.experimental.pallas import tpu as pltpu
from jax.sharding import PartitionSpec as P

D = 4096
HD = 128
QH = 8
QKV = 1280
TOK = 256
BLK = D // 8
HALF = BLK // 2
QUART = HALF // 2
PIECE = QUART // 8
COLS = QKV // 2
OUTW = QH * HD

AXES = ("blk", "rep")
target_rms = 0.5
rope_base = 500000.0
F32 = jnp.float32
BF16 = jnp.bfloat16


def place():
    blk, rep = lax.axis_index("blk"), lax.axis_index("rep")
    x, y = blk // 2, (rep // 16) * 2 + blk % 2
    return x, y, (rep // 2) % 8, rep % 2


def flat(x, y, z, c):
    return (x * 2 + y % 2) * 32 + (y // 2) * 16 + z * 2 + c


def swap(value, partner):
    pairs = []
    for x in range(4):
        for y in range(4):
            for z in range(8):
                for c in range(2):
                    pairs.append((flat(x, y, z, c), flat(*partner(x, y, z, c))))
    return lax.ppermute(value, AXES, pairs)


def near(c):
    return 1 if c == 0 else 3


def gray(place_z):
    return place_z ^ (place_z >> 1)


def ungray(code):
    return code ^ (code >> 1) ^ (code >> 2)


def other_core(x, y, z, c):
    return x, y, z, 1 - c


def gather_x1(x, y, z, c):
    return x ^ near(c ^ (z & 1)), y, z, c


def gather_x2(x, y, z, c):
    return x ^ (4 - near(c ^ (z & 1))), y, z, c


def flip_y(x, y, z, c):
    return x, y ^ near(c), z, c


def pair_z(x, y, z, c):
    return x, y, (z ^ 1) if c == 0 else ((z + 1) % 8 if z % 2 else (z - 1) % 8), c


def x_1(x, y, z, c):
    return x ^ near(c), y, z, c


def x_2(x, y, z, c):
    return x ^ (4 - near(c)), y, z, c


def y_1(x, y, z, c):
    return x, y ^ near(c), z, c


def y_2(x, y, z, c):
    return x, y ^ (4 - near(c)), z, c


def y_far(x, y, z, c):
    return x, y ^ 2, z, c


def z_bit(bit):
    def partner(x, y, z, c):
        return x, y, (ungray(gray((z + c) % 8) ^ (1 << bit)) - c) % 8, c

    return partner


VM = pl.BlockSpec(memory_space=pltpu.VMEM)
SM = pl.BlockSpec(memory_space=pltpu.SMEM)
ANY = pl.BlockSpec(memory_space=pl.ANY)


def dot(a, b, dims):
    return lax.dot_general(a, b, (dims, ((), ())), preferred_element_type=F32)


def part_body(count, *refs):
    at, normed, old = refs[0], refs[1], refs[2]
    pieces, out = refs[3 : 3 + count], refs[3 + count]
    total = old[...]
    for i in range(count):
        cols = pl.ds(pl.multiple_of(at[i], HALF), HALF)
        total = total + dot(normed[:, cols], pieces[i][...], ((1,), (0,)))
    out[...] = total


def part_qkv(at, normed, old, pieces):
    count = len(pieces)
    return pl.pallas_call(
        lambda *refs: part_body(count, *refs),
        out_shape=jax.ShapeDtypeStruct((TOK, QKV), F32),
        in_specs=[SM] + [VM] * (2 + count),
        out_specs=VM,
        compiler_params=pltpu.CompilerParams(vmem_limit_bytes=24 << 20),
        cost_estimate=pl.CostEstimate(
            flops=2 * TOK * HALF * QKV * count, bytes_accessed=count * HALF * QKV * 2, transcendentals=0
        ),
        name="qkv_part",
    )(at, normed, old, *pieces)


def attend_body(qkv, grad, doc_row, doc_col, cosine, sine, out):
    cos, sin = cosine[...], sine[...]
    key = qkv[:, OUTW : OUTW + HD]
    k_rot = (key * cos + pltpu.roll(key, HD // 2, 1) * sin).astype(BF16)
    val = qkv[:, OUTW + HD :].astype(BF16)
    rows = lax.broadcasted_iota(jnp.int32, (TOK, TOK), 0)
    cols = lax.broadcasted_iota(jnp.int32, (TOK, TOK), 1)
    seen = (cols <= rows) & (doc_col[...] == doc_row[...])
    scale = HD**-0.5
    d_key = jnp.zeros((TOK, HD), F32)
    d_val = jnp.zeros((TOK, HD), F32)
    for h in range(QH):
        at = slice(h * HD, (h + 1) * HD)
        query = qkv[:, at]
        q_rot = (query * cos + pltpu.roll(query, HD // 2, 1) * sin).astype(BF16)
        g = grad[:, at]
        scores = jnp.where(seen, dot(q_rot, k_rot, ((1,), (1,))), -1e30)
        expo = jnp.exp((scores - jnp.max(scores, axis=1, keepdims=True)) * scale)
        probs = expo * (1.0 / jnp.sum(expo, axis=1, keepdims=True))
        d_probs = dot(g, val, ((1,), (1,)))
        delta = jnp.sum(d_probs * probs, axis=1, keepdims=True)
        d_scores = (probs * (d_probs - delta)).astype(BF16)
        d_val = d_val + dot(probs.astype(BF16), g, ((0,), (0,)))
        d_query = dot(d_scores, k_rot, ((1,), (0,))) * scale
        d_key = d_key + dot(d_scores, q_rot, ((0,), (0,)))
        out[:, at] = (d_query * cos - pltpu.roll(d_query, HD // 2, 1) * sin).astype(BF16)
    d_key = d_key * scale
    out[:, OUTW : OUTW + HD] = (d_key * cos - pltpu.roll(d_key, HD // 2, 1) * sin).astype(BF16)
    out[:, OUTW + HD :] = d_val.astype(BF16)


def attend(qkv, grad, doc, cosine, sine):
    return pl.pallas_call(
        attend_body,
        out_shape=jax.ShapeDtypeStruct((TOK, QKV), BF16),
        in_specs=[VM] * 6,
        out_specs=VM,
        compiler_params=pltpu.CompilerParams(vmem_limit_bytes=24 << 20),
        cost_estimate=pl.CostEstimate(
            flops=10 * TOK * TOK * OUTW, bytes_accessed=3 << 20, transcendentals=TOK * TOK * QH
        ),
        name="attend",
    )(qkv, grad, doc, doc.reshape(TOK, 1), cosine, sine)


def tokens_body(count, *refs):
    at, d_qkv, tokens, scale_r = refs[:4]
    pieces, out, hold = refs[4 : 4 + count], refs[4 + count], refs[5 + count]
    dq = d_qkv[...]
    total = jnp.zeros((TOK, HALF), F32)
    for i in range(count):
        cols = pl.ds(pl.multiple_of(at[i], HALF), HALF)
        part = dot(dq, pieces[i][...], ((1,), (1,)))
        hold[:, cols] = part
        total = total + part * tokens[:, cols].astype(F32)
    r = scale_r[...]
    mean = jnp.sum(total, axis=1, keepdims=True) * (1.0 / D)
    back = r * r * r * mean
    for i in range(count):
        cols = slice(i * HALF, (i + 1) * HALF)
        out[:, cols] = (r * hold[:, cols] - tokens[:, cols].astype(F32) * back).astype(BF16)


def tokens_grad(at, d_qkv, tokens, scale_r, pieces):
    count = len(pieces)
    return pl.pallas_call(
        lambda *refs: tokens_body(count, *refs),
        out_shape=jax.ShapeDtypeStruct((TOK, D), BF16),
        in_specs=[SM] + [VM] * (3 + count),
        out_specs=VM,
        scratch_shapes=[pltpu.VMEM((TOK, D), F32)],
        compiler_params=pltpu.CompilerParams(vmem_limit_bytes=40 << 20),
        cost_estimate=pl.CostEstimate(flops=2 * TOK * D * QKV, bytes_accessed=16 << 20, transcendentals=0),
        name="tokens_grad",
    )(at, d_qkv, tokens, scale_r, *pieces)


def term_body(count, at, feats, d_qkv, out_x, out_y):
    low, high = d_qkv[:, :COLS], d_qkv[:, COLS:]
    for i in range(count):
        rows = pl.ds(pl.multiple_of(at[0, i], QUART), QUART)
        out_x[i] = dot(feats[rows, :], low, ((1,), (0,))).astype(BF16)
        rows = pl.ds(pl.multiple_of(at[1, i], QUART), QUART)
        out_y[i] = dot(feats[rows, :], high, ((1,), (0,))).astype(BF16)


def terms(at, feats, d_qkv):
    count = at.shape[1]
    shape = jax.ShapeDtypeStruct((count, QUART, COLS), BF16)
    return pl.pallas_call(
        lambda *refs: term_body(count, *refs),
        out_shape=(shape, shape),
        in_specs=[SM, VM, VM],
        out_specs=(VM, VM),
        compiler_params=pltpu.CompilerParams(vmem_limit_bytes=24 << 20),
        cost_estimate=pl.CostEstimate(
            flops=4 * count * QUART * COLS * 2 * TOK, bytes_accessed=6 << 20, transcendentals=0
        ),
        name="terms",
    )(at, feats, d_qkv)


def rescale_body(factor, at, mine, theirs, out):
    for i in range(16):
        rows = pl.ds(pl.multiple_of(at[0, i], PIECE), PIECE)
        out[rows, :] = (mine[i].astype(F32) * factor[0]).astype(BF16)
        rows = pl.ds(pl.multiple_of(at[1, i], PIECE), PIECE)
        out[rows, :] = (theirs[i].astype(F32) * factor[0]).astype(BF16)


def rescale(factor, at, mine, theirs):
    return pl.pallas_call(
        rescale_body,
        out_shape=jax.ShapeDtypeStruct((BLK, QKV), BF16),
        in_specs=[SM, SM, VM, VM],
        out_specs=VM,
        compiler_params=pltpu.CompilerParams(vmem_limit_bytes=16 << 20),
        name="rescale",
    )(factor.reshape(1), at, mine, theirs)


def tables():
    position = jnp.arange(TOK, dtype=F32)
    freq = jnp.exp(-jnp.log(rope_base) * 2.0 * jnp.arange(HD // 2, dtype=F32) / HD)
    angle = position[:, None] * freq[None, :]
    cos, sin = jnp.cos(angle), jnp.sin(angle)
    return jnp.concatenate([cos, cos], axis=1), jnp.concatenate([-sin, sin], axis=1)


def add(kept, came):
    return (kept.astype(F32) + came.astype(F32)).astype(BF16)


def on_device(tokens, grad_attended, doc_ids, w_own):
    x, y, z, c = place()
    cosine, sine = tables()

    w00 = lax.dynamic_slice_in_dim(w_own, c * HALF, HALF, 0)
    wa0 = swap(w00, gather_x1)
    w01 = swap(w00, flip_y)

    full = tokens.astype(F32)
    scale_r = lax.rsqrt(jnp.mean(full * full, axis=1, keepdims=True) + 1e-05)
    normed = (full * scale_r).astype(BF16)
    turned = normed.T.reshape(8, 2, HALF, TOK)
    mine = lax.dynamic_index_in_dim(turned, c, 1, False)
    theirs = swap(lax.dynamic_index_in_dim(turned, 1 - c, 1, False), other_core)
    feats = jnp.concatenate([mine, theirs], axis=2).reshape(D // 2, 2 * TOK)

    wo0 = swap(wa0, gather_x2)
    wa1 = swap(wa0, flip_y)
    wb0 = swap(wa0, pair_z)
    v01 = swap(w01, other_core)
    vb0 = swap(wa0, other_core)
    wo1 = swap(wo0, flip_y)
    wb1 = swap(wa1, pair_z)
    vo0 = swap(wo0, other_core)
    vb1 = swap(wa1, other_core)
    va0 = swap(wb0, other_core)
    vo1 = swap(wo1, other_core)
    va1 = swap(wb1, other_core)
    v00 = lax.dynamic_slice_in_dim(w_own, (1 - c) * HALF, HALF, 0)

    turn = c ^ (z & 1)
    p1 = 1 + 2 * turn
    p2 = 4 - p1
    step = {"0": 0, "a": p1, "b": p2, "o": 2}

    def column(name, flip, half):
        return ((x ^ step[name]) * 2 + ((y & 1) ^ flip)) * BLK + half * HALF

    early = [
        (w00, column("0", 0, c)),
        (v00, column("0", 0, 1 - c)),
        (w01, column("0", 1, c)),
        (v01, column("0", 1, 1 - c)),
        (wa0, column("a", 0, c)),
        (vb0, column("b", 0, 1 - c)),
    ]
    middle = [
        (wo0, column("o", 0, c)),
        (wa1, column("a", 1, c)),
        (wb0, column("b", 0, c)),
        (vo0, column("o", 0, 1 - c)),
        (vb1, column("b", 1, 1 - c)),
        (va0, column("a", 0, 1 - c)),
    ]
    late = [
        (wo1, column("o", 1, c)),
        (wb1, column("b", 1, c)),
        (vo1, column("o", 1, 1 - c)),
        (va1, column("a", 1, 1 - c)),
    ]

    def spots(group):
        return jnp.stack([spot for _, spot in group]).astype(jnp.int32)

    qkv = jnp.zeros((TOK, QKV), F32)
    for group in (early, middle, late):
        qkv = part_qkv(spots(group), normed, qkv, [piece for piece, _ in group])

    d_qkv = attend(qkv, grad_attended, doc_ids, cosine, sine)

    d_other = swap(d_qkv, other_core)
    both = jnp.concatenate([d_qkv, d_other], axis=0)
    q1 = 1 + 2 * c
    order = [0, 4 - q1, q1, 2]

    def row(xm, ym):
        yy = y ^ ym
        return ((x ^ xm) * 2 + (yy & 1)) * HALF + (yy >> 1) * QUART

    def rows(first, second):
        along_x = [row(order[i], order[j]) for i in (first, second) for j in range(4)]
        along_y = [row(order[i], order[j]) for j in (first, second) for i in range(4)]
        return jnp.stack([jnp.stack(along_x), jnp.stack(along_y)]).astype(jnp.int32)

    sent_x, sent_y = terms(rows(2, 3), feats, both)
    came_x = swap(sent_x, x_1)
    came_y = swap(sent_y, y_1)
    kept_x, kept_y = terms(rows(0, 1), feats, both)
    every = early + middle + late
    d_tokens = tokens_grad(spots(every), d_qkv, tokens, scale_r, [piece for piece, _ in every])

    sum_x, sum_y = add(kept_x, came_x), add(kept_y, came_y)
    for count, step_x, step_y in ((4, x_2, y_2), (2, y_1, x_1), (1, y_2, x_2)):
        came_x, came_y = swap(sum_x[count:], step_x), swap(sum_y[count:], step_y)
        sum_x, sum_y = add(sum_x[:count], came_x), add(sum_y[:count], came_y)

    code = gray((z + c) % 8)
    total = jnp.concatenate([sum_x[0], sum_y[0]], axis=1).reshape(2, 2, 2, PIECE, QKV)
    for bit in range(3):
        axis = 2 - bit
        own = (code >> bit) & 1
        came = swap(lax.dynamic_index_in_dim(total, 1 - own, axis, False), z_bit(bit))
        kept = lax.dynamic_index_in_dim(total, own, axis, False)
        total = kept.astype(F32) + came.astype(F32)
        if bit < 2:
            total = total.astype(BF16)

    square = jnp.broadcast_to(jnp.sum(total * total), (8, 128))
    for steps in ((other_core,), (x_1, x_2, lambda x, y, z, c: (x ^ 2, y, z, c)), (y_1, y_2, y_far)):
        square = square + sum([swap(square, s) for s in steps])
    for bit in range(3):
        square = square + swap(square, z_bit(bit))
    factor = target_rms * lax.rsqrt(square[0, 0] / (D * QKV) + 1e-06)

    got = total.astype(BF16)[None]
    for partner in (y_far, z_bit(2), z_bit(1), z_bit(0)):
        got = jnp.concatenate([got, swap(got, partner)], axis=0)
    got_other = swap(got, other_core)

    def homes(core):
        own = gray((z + core) % 8)
        out = []
        for i in range(16):
            mask = ((i >> 3) & 1) | (((i >> 2) & 1) << 1) | (((i >> 1) & 1) << 2)
            out.append(core * HALF + ((y >> 1) ^ (i & 1)) * QUART + (own ^ mask) * PIECE)
        return jnp.stack(out)

    spots_out = jnp.stack([homes(c), homes(1 - c)]).astype(jnp.int32)
    return d_tokens, rescale(factor, spots_out, got, got_other)


def solution(mesh):
    spread = P(("blk", "rep"), None)
    return jax.shard_map(
        on_device,
        mesh=mesh,
        in_specs=(spread, spread, spread, P("blk", None)),
        out_specs=(spread, P("blk", None)),
        check_vma=False,
    )
```

```python
import jax
import jax.numpy as jnp
from jax import lax
from jax.experimental import pallas as pl
from jax.experimental.pallas import tpu as pltpu
from jax.sharding import PartitionSpec as P

D = 4096
HD = 128
QH = 8
QKV = 1280
TOK = 256
BLK = D // 8
HALF = BLK // 2
QUART = HALF // 2
PIECE = QUART // 8
COLS = QKV // 2
OUTW = QH * HD

AXES = ("blk", "rep")
target_rms = 0.5
rope_base = 500000.0
F32 = jnp.float32
BF16 = jnp.bfloat16


def place():
    blk, rep = lax.axis_index("blk"), lax.axis_index("rep")
    x, y = blk // 2, (rep // 16) * 2 + blk % 2
    return x, y, (rep // 2) % 8, rep % 2


def flat(x, y, z, c):
    return (x * 2 + y % 2) * 32 + (y // 2) * 16 + z * 2 + c


def swap(value, partner):
    pairs = []
    for x in range(4):
        for y in range(4):
            for z in range(8):
                for c in range(2):
                    pairs.append((flat(x, y, z, c), flat(*partner(x, y, z, c))))
    return lax.ppermute(value, AXES, pairs)


def near(c):
    return 1 if c == 0 else 3


def gray(place_z):
    return place_z ^ (place_z >> 1)


def ungray(code):
    return code ^ (code >> 1) ^ (code >> 2)


def other_core(x, y, z, c):
    return x, y, z, 1 - c


def gather_x1(x, y, z, c):
    return x ^ near(c ^ (z & 1)), y, z, c


def gather_x2(x, y, z, c):
    return x ^ (4 - near(c ^ (z & 1))), y, z, c


def flip_y(x, y, z, c):
    return x, y ^ near(c), z, c


def pair_z(x, y, z, c):
    return x, y, (z ^ 1) if c == 0 else ((z + 1) % 8 if z % 2 else (z - 1) % 8), c


def x_1(x, y, z, c):
    return x ^ near(c), y, z, c


def x_2(x, y, z, c):
    return x ^ (4 - near(c)), y, z, c


def y_1(x, y, z, c):
    return x, y ^ near(c), z, c


def y_2(x, y, z, c):
    return x, y ^ (4 - near(c)), z, c


def y_far(x, y, z, c):
    return x, y ^ 2, z, c


def z_shift(shift):
    return lambda x, y, z, c: (x, y, (z + shift) % 8, c)


def z_bit(bit):
    def partner(x, y, z, c):
        return x, y, (ungray(gray((z + c) % 8) ^ (1 << bit)) - c) % 8, c

    return partner


VM = pl.BlockSpec(memory_space=pltpu.VMEM)
SM = pl.BlockSpec(memory_space=pltpu.SMEM)
ANY = pl.BlockSpec(memory_space=pl.ANY)


def dot(a, b, dims):
    return lax.dot_general(a, b, (dims, ((), ())), preferred_element_type=F32)


def norm_body(c, tokens, normed, scale_r, mine, theirs):
    full = tokens[...].astype(F32)
    r = lax.rsqrt(jnp.sum(full * full, axis=1, keepdims=True) * (1.0 / D) + 1e-05)
    scale_r[...] = r
    normed[...] = (full * r).astype(BF16)
    for b in range(8):
        for half, out in ((c[0], mine), (1 - c[0], theirs)):
            cols = pl.ds(pl.multiple_of(b * BLK + half * HALF, HALF), HALF)
            out[b * HALF : (b + 1) * HALF, :] = normed[:, cols].T


def norm(c, tokens):
    turned = jax.ShapeDtypeStruct((D // 2, TOK), BF16)
    return pl.pallas_call(
        norm_body,
        out_shape=(
            jax.ShapeDtypeStruct((TOK, D), BF16),
            jax.ShapeDtypeStruct((TOK, 1), F32),
            turned,
            turned,
        ),
        in_specs=[SM, VM],
        out_specs=(VM, VM, VM, VM),
        compiler_params=pltpu.CompilerParams(vmem_limit_bytes=24 << 20),
        cost_estimate=pl.CostEstimate(flops=10 * TOK * D, bytes_accessed=6 << 20, transcendentals=0),
        name="norm",
    )(c.reshape(1).astype(jnp.int32), tokens)


def project(total, at, normed, pieces):
    for i, piece in enumerate(pieces):
        cols = pl.ds(pl.multiple_of(at[i], HALF), HALF)
        part = dot(normed[:, cols], piece[...], ((1,), (0,)))
        total = part if total is None else total + part
    return total


def part_body(count, *refs):
    at, normed, pieces, out = refs[0], refs[1], refs[2 : 2 + count], refs[-1]
    old = refs[2 + count][...] if len(refs) == 4 + count else None
    out[...] = project(old, at, normed, pieces)


def part_qkv(at, normed, pieces, *old):
    count = len(pieces)
    return pl.pallas_call(
        lambda *refs: part_body(count, *refs),
        out_shape=jax.ShapeDtypeStruct((TOK, QKV), F32),
        in_specs=[SM] + [VM] * (1 + count + len(old)),
        out_specs=VM,
        compiler_params=pltpu.CompilerParams(vmem_limit_bytes=24 << 20),
        cost_estimate=pl.CostEstimate(
            flops=2 * TOK * HALF * QKV * count, bytes_accessed=count * HALF * QKV * 2, transcendentals=0
        ),
        name="qkv_part",
    )(at, normed, *pieces, *old)


def attend_body(count, at, normed, *refs):
    pieces = refs[:count]
    old, grad, doc_row, doc_col, cosine, sine, out, qkv = refs[count:]
    qkv[...] = project(old[...], at, normed, pieces)
    cos, sin = cosine[...], sine[...]
    key = qkv[:, OUTW : OUTW + HD]
    k_rot = (key * cos + pltpu.roll(key, HD // 2, 1) * sin).astype(BF16)
    val = qkv[:, OUTW + HD :].astype(BF16)
    rows = lax.broadcasted_iota(jnp.int32, (TOK, TOK), 0)
    cols = lax.broadcasted_iota(jnp.int32, (TOK, TOK), 1)
    seen = (cols <= rows) & (doc_col[...] == doc_row[...])
    scale = HD**-0.5
    d_key = jnp.zeros((TOK, HD), F32)
    d_val = jnp.zeros((TOK, HD), F32)
    for h in range(QH):
        head = slice(h * HD, (h + 1) * HD)
        query = qkv[:, head]
        q_rot = (query * cos + pltpu.roll(query, HD // 2, 1) * sin).astype(BF16)
        g = grad[:, head]
        scores = jnp.where(seen, dot(q_rot, k_rot, ((1,), (1,))), -1e30)
        expo = jnp.exp((scores - jnp.max(scores, axis=1, keepdims=True)) * scale)
        probs = expo * (1.0 / jnp.sum(expo, axis=1, keepdims=True))
        d_probs = dot(g, val, ((1,), (1,)))
        delta = jnp.sum(d_probs * probs, axis=1, keepdims=True)
        d_scores = (probs * (d_probs - delta)).astype(BF16)
        d_val = d_val + dot(probs.astype(BF16), g, ((0,), (0,)))
        d_query = dot(d_scores, k_rot, ((1,), (0,))) * scale
        d_key = d_key + dot(d_scores, q_rot, ((0,), (0,)))
        out[:, head] = (d_query * cos - pltpu.roll(d_query, HD // 2, 1) * sin).astype(BF16)
    d_key = d_key * scale
    out[:, OUTW : OUTW + HD] = (d_key * cos - pltpu.roll(d_key, HD // 2, 1) * sin).astype(BF16)
    out[:, OUTW + HD :] = d_val.astype(BF16)


def attend(at, normed, pieces, old, grad, doc, cosine, sine):
    count = len(pieces)
    return pl.pallas_call(
        lambda *refs: attend_body(count, *refs),
        out_shape=jax.ShapeDtypeStruct((TOK, QKV), BF16),
        in_specs=[SM] + [VM] * (7 + count),
        out_specs=VM,
        scratch_shapes=[pltpu.VMEM((TOK, QKV), F32)],
        compiler_params=pltpu.CompilerParams(vmem_limit_bytes=24 << 20),
        cost_estimate=pl.CostEstimate(
            flops=10 * TOK * TOK * OUTW, bytes_accessed=6 << 20, transcendentals=TOK * TOK * QH
        ),
        name="attend",
    )(at, normed, *pieces, old, grad, doc, doc.reshape(TOK, 1), cosine, sine)


def tokens_body(count, *refs):
    at, d_qkv, tokens, scale_r = refs[:4]
    pieces, out, hold = refs[4 : 4 + count], refs[4 + count], refs[5 + count]
    dq = d_qkv[...]
    total = jnp.zeros((TOK, HALF), F32)
    for i in range(count):
        cols = pl.ds(pl.multiple_of(at[i], HALF), HALF)
        part = dot(dq, pieces[i][...], ((1,), (1,)))
        hold[:, cols] = part
        total = total + part * tokens[:, cols].astype(F32)
    r = scale_r[...]
    mean = jnp.sum(total, axis=1, keepdims=True) * (1.0 / D)
    back = r * r * r * mean
    for i in range(count):
        cols = slice(i * HALF, (i + 1) * HALF)
        out[:, cols] = (r * hold[:, cols] - tokens[:, cols].astype(F32) * back).astype(BF16)


def tokens_grad(at, d_qkv, tokens, scale_r, pieces):
    count = len(pieces)
    return pl.pallas_call(
        lambda *refs: tokens_body(count, *refs),
        out_shape=jax.ShapeDtypeStruct((TOK, D), BF16),
        in_specs=[SM] + [VM] * (3 + count),
        out_specs=VM,
        scratch_shapes=[pltpu.VMEM((TOK, D), F32)],
        compiler_params=pltpu.CompilerParams(vmem_limit_bytes=40 << 20),
        cost_estimate=pl.CostEstimate(flops=2 * TOK * D * QKV, bytes_accessed=16 << 20, transcendentals=0),
        name="tokens_grad",
    )(at, d_qkv, tokens, scale_r, *pieces)


def term_body(count, first, at, feats, feats_other, d_qkv, d_other, out):
    cols = slice(first, first + COLS)
    own, other = d_qkv[:, cols], d_other[:, cols]
    for i in range(count):
        rows = pl.ds(pl.multiple_of(at[i], QUART), QUART)
        part = dot(feats[rows, :], own, ((1,), (0,))) + dot(feats_other[rows, :], other, ((1,), (0,)))
        out[i] = part.astype(BF16)


def terms(first, at, feats, feats_other, d_qkv, d_other):
    count = at.shape[0]
    return pl.pallas_call(
        lambda *refs: term_body(count, first, *refs),
        out_shape=jax.ShapeDtypeStruct((count, QUART, COLS), BF16),
        in_specs=[SM, VM, VM, VM, VM],
        out_specs=VM,
        compiler_params=pltpu.CompilerParams(vmem_limit_bytes=16 << 20),
        cost_estimate=pl.CostEstimate(
            flops=2 * count * QUART * COLS * 2 * TOK, bytes_accessed=5 << 20, transcendentals=0
        ),
        name="terms",
    )(at, feats, feats_other, d_qkv, d_other)


def pack_body(at, kept_x, came_x, kept_y, came_y, *out):
    for i in range(8):
        rows = pl.ds(pl.multiple_of(at[i], PIECE), PIECE)
        out[i][:, :COLS] = (kept_x[rows, :].astype(F32) + came_x[rows, :].astype(F32)).astype(BF16)
        out[i][:, COLS:] = (kept_y[rows, :].astype(F32) + came_y[rows, :].astype(F32)).astype(BF16)


def pack(at, *parts):
    return pl.pallas_call(
        pack_body,
        out_shape=tuple(jax.ShapeDtypeStruct((PIECE, QKV), BF16) for _ in range(8)),
        in_specs=[SM] + [VM] * 4,
        out_specs=(VM,) * 8,
        compiler_params=pltpu.CompilerParams(vmem_limit_bytes=8 << 20),
        name="pack",
    )(at, *parts)


def finish_body(*refs):
    total = sum(ref[...].astype(F32) for ref in refs[:8])
    refs[8][0] = total.astype(BF16)
    squares = jnp.sum(jnp.sum(total * total, axis=1, keepdims=True), axis=0, keepdims=True)
    refs[9][...] = jnp.broadcast_to(squares, (8, 128))


def finish(parts):
    return pl.pallas_call(
        finish_body,
        out_shape=(jax.ShapeDtypeStruct((1, PIECE, QKV), BF16), jax.ShapeDtypeStruct((8, 128), F32)),
        in_specs=[VM] * 8,
        out_specs=(VM, VM),
        compiler_params=pltpu.CompilerParams(vmem_limit_bytes=8 << 20),
        name="finish",
    )(*parts)


def rescale_body(factor, at, mine, theirs, out):
    for i in range(16):
        rows = pl.ds(pl.multiple_of(at[0, i], PIECE), PIECE)
        out[rows, :] = (mine[i].astype(F32) * factor[0]).astype(BF16)
        rows = pl.ds(pl.multiple_of(at[1, i], PIECE), PIECE)
        out[rows, :] = (theirs[i].astype(F32) * factor[0]).astype(BF16)


def rescale(factor, at, mine, theirs):
    return pl.pallas_call(
        rescale_body,
        out_shape=jax.ShapeDtypeStruct((BLK, QKV), BF16),
        in_specs=[SM, SM, VM, VM],
        out_specs=VM,
        compiler_params=pltpu.CompilerParams(vmem_limit_bytes=16 << 20),
        name="rescale",
    )(factor.reshape(1), at, mine, theirs)


def tables():
    position = jnp.arange(TOK, dtype=F32)
    freq = jnp.exp(-jnp.log(rope_base) * 2.0 * jnp.arange(HD // 2, dtype=F32) / HD)
    angle = position[:, None] * freq[None, :]
    cos, sin = jnp.cos(angle), jnp.sin(angle)
    return jnp.concatenate([cos, cos], axis=1), jnp.concatenate([-sin, sin], axis=1)


def add(kept, came):
    return (kept.astype(F32) + came.astype(F32)).astype(BF16)


def on_device(tokens, grad_attended, doc_ids, w_own):
    x, y, z, c = place()
    cosine, sine = tables()

    w00 = lax.dynamic_slice_in_dim(w_own, c * HALF, HALF, 0)
    wa0 = swap(w00, gather_x1)
    w01 = swap(w00, flip_y)

    normed, scale_r, feats, theirs = norm(c, tokens)
    feats_other = swap(theirs, other_core)

    wo0 = swap(wa0, gather_x2)
    wa1 = swap(wa0, flip_y)
    wb0 = swap(wa0, pair_z)
    v01 = swap(w01, other_core)
    vb0 = swap(wa0, other_core)
    wo1 = swap(wo0, flip_y)
    wb1 = swap(wa1, pair_z)
    vo0 = swap(wo0, other_core)
    vb1 = swap(wa1, other_core)
    va0 = swap(wb0, other_core)
    vo1 = swap(wo1, other_core)
    va1 = swap(wb1, other_core)
    v00 = lax.dynamic_slice_in_dim(w_own, (1 - c) * HALF, HALF, 0)

    turn = c ^ (z & 1)
    p1 = 1 + 2 * turn
    p2 = 4 - p1
    step = {"0": 0, "a": p1, "b": p2, "o": 2}

    def column(name, flip, half):
        return ((x ^ step[name]) * 2 + ((y & 1) ^ flip)) * BLK + half * HALF

    early = [
        (w00, column("0", 0, c)),
        (v00, column("0", 0, 1 - c)),
        (w01, column("0", 1, c)),
        (v01, column("0", 1, 1 - c)),
        (wa0, column("a", 0, c)),
        (vb0, column("b", 0, 1 - c)),
    ]
    middle = [
        (wo0, column("o", 0, c)),
        (wa1, column("a", 1, c)),
        (wb0, column("b", 0, c)),
        (vo0, column("o", 0, 1 - c)),
        (vb1, column("b", 1, 1 - c)),
        (va0, column("a", 0, 1 - c)),
    ]
    late = [
        (wo1, column("o", 1, c)),
        (wb1, column("b", 1, c)),
        (vo1, column("o", 1, 1 - c)),
        (va1, column("a", 1, 1 - c)),
    ]

    def spots(group):
        return jnp.stack([spot for _, spot in group]).astype(jnp.int32)

    def pieces(group):
        return [piece for piece, _ in group]

    part = part_qkv(spots(early), normed, pieces(early))
    part = part_qkv(spots(middle), normed, pieces(middle), part)
    d_qkv = attend(spots(late), normed, pieces(late), part, grad_attended, doc_ids, cosine, sine)

    d_other = swap(d_qkv, other_core)
    q1 = 1 + 2 * c
    order = [0, 4 - q1, q1, 2]

    def row(xm, ym):
        yy = y ^ ym
        return ((x ^ xm) * 2 + (yy & 1)) * HALF + (yy >> 1) * QUART

    def along_x(first, second):
        return jnp.stack([row(order[i], order[j]) for i in (first, second) for j in range(4)]).astype(jnp.int32)

    def along_y(first, second):
        return jnp.stack([row(order[i], order[j]) for j in (first, second) for i in range(4)]).astype(jnp.int32)

    made = (feats, feats_other, d_qkv, d_other)
    came_x = swap(terms(0, along_x(2, 3), *made), x_1)
    came_y = swap(terms(COLS, along_y(2, 3), *made), y_1)
    sum_x, sum_y = terms(0, along_x(0, 1), *made), terms(COLS, along_y(0, 1), *made)
    every = early + middle + late
    d_tokens = tokens_grad(spots(every), d_qkv, tokens, scale_r, pieces(every))
    came_x, came_y, d_tokens = lax.optimization_barrier((came_x, came_y, d_tokens))

    for count, step_x, step_y in ((4, x_2, y_2), (2, y_1, x_1), (1, y_2, x_2)):
        sum_x, sum_y = add(sum_x, came_x), add(sum_y, came_y)
        came_x, came_y = swap(sum_x[count:], step_x), swap(sum_y[count:], step_y)
        sum_x, sum_y = sum_x[:count], sum_y[:count]

    shifts = (0, 1, -1, 2, -2, 3, -3, 4)
    parts = pack(
        jnp.stack([((z + k) % 8) * PIECE for k in shifts]).astype(jnp.int32),
        sum_x[0],
        came_x[0],
        sum_y[0],
        came_y[0],
    )
    parts = [parts[0]] + [swap(part, z_shift(k)) for part, k in zip(parts[1:], shifts[1:])]
    got, square = finish(parts)

    for steps in ((other_core,), (x_1, x_2, lambda x, y, z, c: (x ^ 2, y, z, c)), (y_1, y_2, y_far)):
        square = square + sum([swap(square, s) for s in steps])
    for bit in range(3):
        square = square + swap(square, z_bit(bit))
    factor = target_rms * lax.rsqrt(square[0, 0] / (D * QKV) + 1e-06)

    for partner in (y_far, z_bit(2), z_bit(1), z_bit(0)):
        got = jnp.concatenate([got, swap(got, partner)], axis=0)
    got_other = swap(got, other_core)

    def homes(core):
        own = gray((z + core) % 8)
        out = []
        for i in range(16):
            mask = ((i >> 3) & 1) | (((i >> 2) & 1) << 1) | (((i >> 1) & 1) << 2)
            at_z = (ungray(own ^ mask) + 8 - core) % 8
            out.append(core * HALF + ((y >> 1) ^ (i & 1)) * QUART + at_z * PIECE)
        return jnp.stack(out)

    spots_out = jnp.stack([homes(c), homes(1 - c)]).astype(jnp.int32)
    return d_tokens, rescale(factor, spots_out, got, got_other)


def solution(mesh):
    spread = P(("blk", "rep"), None)
    return jax.shard_map(
        on_device,
        mesh=mesh,
        in_specs=(spread, spread, spread, P("blk", None)),
        out_specs=(spread, P("blk", None)),
        check_vma=False,
    )
```

```python
import jax
import jax.numpy as jnp
from jax import lax
from jax.experimental import pallas as pl
from jax.experimental.pallas import tpu as pltpu
from jax.sharding import Mesh
from jax.sharding import PartitionSpec as P

D = 4096
HD = 128
QH = 8
QKV = 1280
TOK = 256
BLK = D // 8
HALF = BLK // 2
QUART = HALF // 2
PIECE = QUART // 8
COLS = QKV // 2
OUTW = QH * HD
LOW = COLS // HD

AXES = ("x", "y_lo", "y_hi", "z", "core")
SIZES = (4, 2, 2, 8, 2)
target_rms = 0.5
rope_base = 500000.0
F32 = jnp.float32
BF16 = jnp.bfloat16


def place():
    x, y_lo, y_hi, z, c = (lax.axis_index(axis) for axis in AXES)
    return x, y_hi * 2 + y_lo, z, c


def flat(x, y, z, c):
    return (x * 2 + y % 2) * 32 + (y // 2) * 16 + z * 2 + c


def swap(value, partner):
    pairs = []
    for x in range(4):
        for y in range(4):
            for z in range(8):
                for c in range(2):
                    pairs.append((flat(x, y, z, c), flat(*partner(x, y, z, c))))
    return lax.ppermute(value, AXES, pairs)


def near(c):
    return 1 if c == 0 else 3


def gray(place_z):
    return place_z ^ (place_z >> 1)


def ungray(code):
    return code ^ (code >> 1) ^ (code >> 2)


def other_core(x, y, z, c):
    return x, y, z, 1 - c


def gather_x1(x, y, z, c):
    return x ^ near(c ^ (z & 1)), y, z, c


def gather_x2(x, y, z, c):
    return x ^ (4 - near(c ^ (z & 1))), y, z, c


def flip_y(x, y, z, c):
    return x, y ^ near(c), z, c


def pair_z(x, y, z, c):
    return x, y, (z ^ 1) if c == 0 else ((z + 1) % 8 if z % 2 else (z - 1) % 8), c


def x_1(x, y, z, c):
    return x ^ near(c), y, z, c


def x_2(x, y, z, c):
    return x ^ (4 - near(c)), y, z, c


def y_1(x, y, z, c):
    return x, y ^ near(c), z, c


def y_2(x, y, z, c):
    return x, y ^ (4 - near(c)), z, c


def y_far(x, y, z, c):
    return x, y ^ 2, z, c


def z_bit(bit):
    def partner(x, y, z, c):
        return x, y, (ungray(gray((z + c) % 8) ^ (1 << bit)) - c) % 8, c

    return partner


VM = pl.BlockSpec(memory_space=pltpu.VMEM)
SM = pl.BlockSpec(memory_space=pltpu.SMEM)
ANY = pl.BlockSpec(memory_space=pl.ANY)


def dot(a, b, dims):
    return lax.dot_general(a, b, (dims, ((), ())), preferred_element_type=F32)


def norm_body(c, tokens, normed, scale_r, mine, theirs):
    full = tokens[...].astype(F32)
    r = lax.rsqrt(jnp.sum(full * full, axis=1, keepdims=True) * (1.0 / D) + 1e-05)
    scale_r[...] = r
    normed[...] = (full * r).astype(BF16)
    for b in range(8):
        for half, out in ((c[0], mine), (1 - c[0], theirs)):
            cols = pl.ds(pl.multiple_of(b * BLK + half * HALF, HALF), HALF)
            out[b * HALF : (b + 1) * HALF, :] = normed[:, cols].T


def norm(c, tokens):
    turned = jax.ShapeDtypeStruct((D // 2, TOK), BF16)
    return pl.pallas_call(
        norm_body,
        out_shape=(
            jax.ShapeDtypeStruct((TOK, D), BF16),
            jax.ShapeDtypeStruct((TOK, 1), F32),
            turned,
            turned,
        ),
        in_specs=[SM, VM],
        out_specs=(VM, VM, VM, VM),
        compiler_params=pltpu.CompilerParams(vmem_limit_bytes=12 << 20),
        cost_estimate=pl.CostEstimate(flops=10 * TOK * D, bytes_accessed=6 << 20, transcendentals=0),
        name="norm",
    )(c.reshape(1).astype(jnp.int32), tokens)


def project(total, at, normed, pieces):
    lhs, rhs = [], []
    for i, piece in enumerate(pieces):
        depth = piece.shape[0]
        lhs.append(normed[:, pl.ds(pl.multiple_of(at[i], HALF), depth)])
        rhs.append(piece[...])
    part = dot(jnp.concatenate(lhs, axis=1), jnp.concatenate(rhs, axis=0), ((1,), (0,)))
    return part if total is None else total + part


def part_body(count, *refs):
    at, normed, pieces, out = refs[0], refs[1], refs[2 : 2 + count], refs[-1]
    old = refs[2 + count][...] if len(refs) == 4 + count else None
    out[...] = project(old, at, normed, pieces)


def part_qkv(at, normed, pieces, *old):
    count = len(pieces)
    return pl.pallas_call(
        lambda *refs: part_body(count, *refs),
        out_shape=jax.ShapeDtypeStruct((TOK, QKV), F32),
        in_specs=[SM] + [VM] * (1 + count + len(old)),
        out_specs=VM,
        compiler_params=pltpu.CompilerParams(vmem_limit_bytes=12 << 20),
        cost_estimate=pl.CostEstimate(
            flops=2 * TOK * HALF * QKV * count, bytes_accessed=count * HALF * QKV * 2, transcendentals=0
        ),
        name="qkv_part",
    )(at, normed, *pieces, *old)


def head_grads(heads, qkv, grad, doc_row, doc_col, cos, sin, out, d_key, d_val):
    key = qkv[:, OUTW : OUTW + HD]
    k_rot = (key * cos + pltpu.roll(key, HD // 2, 1) * sin).astype(BF16)
    val = qkv[:, OUTW + HD :].astype(BF16)
    rows = lax.broadcasted_iota(jnp.int32, (TOK, TOK), 0)
    cols = lax.broadcasted_iota(jnp.int32, (TOK, TOK), 1)
    seen = (cols <= rows) & (doc_col[...] == doc_row[...])
    scale = HD**-0.5
    for place_out, h in enumerate(heads):
        head = slice(h * HD, (h + 1) * HD)
        query = qkv[:, head]
        q_rot = (query * cos + pltpu.roll(query, HD // 2, 1) * sin).astype(BF16)
        g = grad[:, head]
        scores = jnp.where(seen, dot(q_rot, k_rot, ((1,), (1,))), -1e30)
        expo = jnp.exp((scores - jnp.max(scores, axis=1, keepdims=True)) * scale)
        probs = expo * (1.0 / jnp.sum(expo, axis=1, keepdims=True))
        d_probs = dot(g, val, ((1,), (1,)))
        delta = jnp.sum(d_probs * probs, axis=1, keepdims=True)
        d_scores = (probs * (d_probs - delta)).astype(BF16)
        d_val = d_val + dot(probs.astype(BF16), g, ((0,), (0,)))
        d_query = dot(d_scores, k_rot, ((1,), (0,))) * scale
        d_key = d_key + dot(d_scores, q_rot, ((0,), (0,)))
        back = d_query * cos - pltpu.roll(d_query, HD // 2, 1) * sin
        out[:, place_out * HD : (place_out + 1) * HD] = back.astype(BF16)
    return d_key, d_val


def attend_low_body(count, at, normed, *refs):
    pieces = refs[:count]
    old, grad, doc_row, doc_col, cosine, sine, out, qkv, d_key, d_val = refs[count:]
    qkv[...] = project(old[...], at, normed, pieces)
    zero = jnp.zeros((TOK, HD), F32)
    d_key[...], d_val[...] = head_grads(
        range(LOW), qkv, grad, doc_row, doc_col, cosine[...], sine[...], out, zero, zero
    )


def attend_high_body(qkv, key_low, val_low, grad, doc_row, doc_col, cosine, sine, out):
    cos, sin = cosine[...], sine[...]
    d_key, d_val = head_grads(
        range(LOW, QH), qkv, grad, doc_row, doc_col, cos, sin, out, key_low[...], val_low[...]
    )
    d_key = d_key * HD**-0.5
    out[:, COLS - 2 * HD : COLS - HD] = (d_key * cos - pltpu.roll(d_key, HD // 2, 1) * sin).astype(BF16)
    out[:, COLS - HD :] = d_val.astype(BF16)


def attend_cost(heads):
    return pl.CostEstimate(
        flops=10 * TOK * TOK * HD * heads, bytes_accessed=4 << 20, transcendentals=TOK * TOK * heads
    )


def attend_low(at, normed, pieces, old, grad, doc, cosine, sine):
    count = len(pieces)
    half = jax.ShapeDtypeStruct((TOK, HD), F32)
    return pl.pallas_call(
        lambda *refs: attend_low_body(count, *refs),
        out_shape=(
            jax.ShapeDtypeStruct((TOK, COLS), BF16),
            jax.ShapeDtypeStruct((TOK, QKV), F32),
            half,
            half,
        ),
        in_specs=[SM] + [VM] * (7 + count),
        out_specs=(VM,) * 4,
        compiler_params=pltpu.CompilerParams(vmem_limit_bytes=12 << 20),
        cost_estimate=attend_cost(LOW),
        name="attend_low",
    )(at, normed, *pieces, old, grad, doc, doc.reshape(TOK, 1), cosine, sine)


def attend_high(qkv, d_key, d_val, grad, doc, cosine, sine):
    return pl.pallas_call(
        attend_high_body,
        out_shape=jax.ShapeDtypeStruct((TOK, COLS), BF16),
        in_specs=[VM] * 8,
        out_specs=VM,
        compiler_params=pltpu.CompilerParams(vmem_limit_bytes=12 << 20),
        cost_estimate=attend_cost(QH - LOW),
        name="attend_high",
    )(qkv, d_key, d_val, grad, doc, doc.reshape(TOK, 1), cosine, sine)


def normed_body(count, at, d_low, d_high, tokens, *refs):
    pieces, held, sums = refs[:count], refs[count], refs[count + 1]
    d_qkv = jnp.concatenate([d_low[...], d_high[...]], axis=1)
    total = jnp.zeros((TOK, 128), F32)
    first = 0
    for i, piece in enumerate(pieces):
        depth = piece.shape[0]
        part = dot(d_qkv, piece[...], ((1,), (1,)))
        held[:, first : first + depth] = part.astype(held.dtype)
        part = part * tokens[:, pl.ds(pl.multiple_of(at[i], HALF), depth)].astype(F32)
        for k in range(0, depth, 128):
            total = total + part[:, k : k + 128]
        first += depth
    sums[...] = jnp.sum(total, axis=1, keepdims=True)


def normed_grad(at, d_low, d_high, tokens, pieces):
    count = len(pieces)
    width = sum(piece.shape[0] for piece in pieces)
    return pl.pallas_call(
        lambda *refs: normed_body(count, *refs),
        out_shape=(jax.ShapeDtypeStruct((TOK, width), F32), jax.ShapeDtypeStruct((TOK, 1), F32)),
        in_specs=[SM] + [VM] * (3 + count),
        out_specs=(VM, VM),
        compiler_params=pltpu.CompilerParams(vmem_limit_bytes=8 << 20),
        cost_estimate=pl.CostEstimate(
            flops=2 * TOK * width * QKV, bytes_accessed=width * QKV * 2, transcendentals=0
        ),
        name="normed_grad",
    )(at, d_low, d_high, tokens, *pieces)


def tokens_body(widths, at, tokens, scale_r, *refs):
    count = len(widths)
    helds, sums, out = refs[:count], refs[count : 2 * count], refs[-1]
    r = scale_r[...]
    back = r * r * r * (sum(part[...] for part in sums) * (1.0 / D))
    i = 0
    for held, group in zip(helds, widths):
        first = 0
        for depth in group:
            cols = pl.ds(pl.multiple_of(at[i], HALF), depth)
            own = r * held[:, first : first + depth].astype(F32)
            out[:, cols] = (own - tokens[:, cols].astype(F32) * back).astype(BF16)
            first, i = first + depth, i + 1


def tokens_grad(at, widths, tokens, scale_r, helds, sums):
    return pl.pallas_call(
        lambda *refs: tokens_body(widths, *refs),
        out_shape=jax.ShapeDtypeStruct((TOK, D), BF16),
        in_specs=[SM] + [VM] * (2 + 2 * len(widths)),
        out_specs=VM,
        compiler_params=pltpu.CompilerParams(vmem_limit_bytes=8 << 20),
        cost_estimate=pl.CostEstimate(flops=6 * TOK * D, bytes_accessed=8 << 20, transcendentals=0),
        name="tokens_grad",
    )(at, tokens, scale_r, *helds, *sums)


def term_body(count, at, feats, feats_other, d_own, d_other, out):
    own, other = [], []
    for i in range(count):
        rows = pl.ds(pl.multiple_of(at[i], QUART), QUART)
        own.append(feats[rows, :])
        other.append(feats_other[rows, :])
    left = jnp.concatenate([jnp.concatenate(own, axis=0), jnp.concatenate(other, axis=0)], axis=1)
    right = jnp.concatenate([d_own[...], d_other[...]], axis=0)
    part = dot(left, right, ((1,), (0,)))
    out[...] = part.astype(BF16).reshape(count, QUART, COLS)


def terms(at, feats, feats_other, d_own, d_other):
    count = at.shape[0]
    return pl.pallas_call(
        lambda *refs: term_body(count, *refs),
        out_shape=jax.ShapeDtypeStruct((count, QUART, COLS), BF16),
        in_specs=[SM, VM, VM, VM, VM],
        out_specs=VM,
        compiler_params=pltpu.CompilerParams(vmem_limit_bytes=12 << 20),
        cost_estimate=pl.CostEstimate(
            flops=2 * count * QUART * COLS * 2 * TOK, bytes_accessed=4 << 20, transcendentals=0
        ),
        name="terms",
    )(at, feats, feats_other, d_own, d_other)


def finish_body(parts, out, square):
    total = sum(parts[i].astype(F32) for i in range(8))
    out[0] = total.astype(BF16)
    squares = jnp.sum(jnp.sum(total * total, axis=1, keepdims=True), axis=0, keepdims=True)
    square[...] = jnp.broadcast_to(squares, (8, 128))


def finish(parts):
    return pl.pallas_call(
        finish_body,
        out_shape=(jax.ShapeDtypeStruct((1, PIECE, QKV), BF16), jax.ShapeDtypeStruct((8, 128), F32)),
        in_specs=[VM],
        out_specs=(VM, VM),
        compiler_params=pltpu.CompilerParams(vmem_limit_bytes=4 << 20),
        name="finish",
    )(parts)


def rescale_body(factor, at, mine, theirs, out):
    for i in range(16):
        rows = pl.ds(pl.multiple_of(at[0, i], PIECE), PIECE)
        out[rows, :] = (mine[i].astype(F32) * factor[0]).astype(BF16)
        rows = pl.ds(pl.multiple_of(at[1, i], PIECE), PIECE)
        out[rows, :] = (theirs[i].astype(F32) * factor[0]).astype(BF16)


def rescale(factor, at, mine, theirs):
    return pl.pallas_call(
        rescale_body,
        out_shape=jax.ShapeDtypeStruct((BLK, QKV), BF16),
        in_specs=[SM, SM, VM, VM],
        out_specs=VM,
        compiler_params=pltpu.CompilerParams(vmem_limit_bytes=8 << 20),
        name="rescale",
    )(factor.reshape(1), at, mine, theirs)


def tables():
    position = jnp.arange(TOK, dtype=F32)
    freq = jnp.exp(-jnp.log(rope_base) * 2.0 * jnp.arange(HD // 2, dtype=F32) / HD)
    angle = position[:, None] * freq[None, :]
    cos, sin = jnp.cos(angle), jnp.sin(angle)
    return jnp.concatenate([cos, cos], axis=1), jnp.concatenate([-sin, sin], axis=1)


def add(kept, came):
    return (kept.astype(F32) + came.astype(F32)).astype(BF16)


def on_device(tokens, grad_attended, doc_ids, w_own):
    x, y, z, c = place()

    w00 = lax.dynamic_slice_in_dim(w_own, c * HALF, HALF, 0)
    wa0 = swap(w00, gather_x1)
    w01 = swap(w00, flip_y)
    normed, scale_r, feats, theirs = norm(c, tokens)
    cosine, sine = tables()
    wa0, normed, theirs, cosine, sine = lax.optimization_barrier((wa0, normed, theirs, cosine, sine))
    wo0 = swap(wa0, gather_x2)
    wa1 = swap(wa0, flip_y)
    wb0 = swap(wa0, pair_z)
    vb0 = swap(wa0, other_core)
    v01 = swap(w01, other_core)

    turn = c ^ (z & 1)
    p1 = 1 + 2 * turn
    p2 = 4 - p1
    step = {"0": 0, "a": p1, "b": p2, "o": 2}

    def column(name, flip, half):
        return ((x ^ step[name]) * 2 + ((y & 1) ^ flip)) * BLK + half * HALF

    def spots(group):
        return jnp.stack([spot for _, spot in group]).astype(jnp.int32)

    def pieces(group):
        return [piece for piece, _ in group]

    early = [
        (w_own, (x * 2 + (y & 1)) * BLK),
        (w01, column("0", 1, c)),
        (wa0, column("a", 0, c)),
        (vb0, column("b", 0, 1 - c)),
        (v01, column("0", 1, 1 - c)),
    ]
    part = part_qkv(spots(early), normed, pieces(early))
    wo0, wa1, part = lax.optimization_barrier((wo0, wa1, part))
    wo1 = swap(wo0, flip_y)
    wb1 = swap(wa1, pair_z)
    vo0 = swap(wo0, other_core)
    va0 = swap(wb0, other_core)
    vb1 = swap(wa1, other_core)
    feats_other = swap(theirs, other_core)
    middle = [
        (wo0, column("o", 0, c)),
        (wa1, column("a", 1, c)),
        (wb0, column("b", 0, c)),
        (vo0, column("o", 0, 1 - c)),
        (vb1, column("b", 1, 1 - c)),
        (va0, column("a", 0, 1 - c)),
    ]
    part = part_qkv(spots(middle), normed, pieces(middle), part)
    wo1, wb1, part = lax.optimization_barrier((wo1, wb1, part))
    vo1 = swap(wo1, other_core)
    va1 = swap(wb1, other_core)
    late = [
        (wo1, column("o", 1, c)),
        (wb1, column("b", 1, c)),
        (vo1, column("o", 1, 1 - c)),
        (va1, column("a", 1, 1 - c)),
    ]
    d_low, qkv, d_key, d_val = attend_low(
        spots(late), normed, pieces(late), part, grad_attended, doc_ids, cosine, sine
    )

    low_other = swap(d_low, other_core)
    d_high = attend_high(qkv, d_key, d_val, grad_attended, doc_ids, cosine, sine)
    low_other, d_high = lax.optimization_barrier((low_other, d_high))
    high_other = swap(d_high, other_core)
    q1 = 1 + 2 * c
    order = [0, 4 - q1, q1, 2]

    def row(xm, ym):
        yy = y ^ ym
        return ((x ^ xm) * 2 + (yy & 1)) * HALF + (yy >> 1) * QUART

    def along_x(first, second):
        return jnp.stack([row(order[i], order[j]) for i in (first, second) for j in range(4)]).astype(jnp.int32)

    def along_y(first, second):
        return jnp.stack([row(order[i], order[j]) for j in (first, second) for i in range(4)]).astype(jnp.int32)

    lows, highs = (feats, feats_other, d_low, low_other), (feats, feats_other, d_high, high_other)
    sent_x = terms(along_x(2, 3), *lows)
    came_x = swap(sent_x, x_1)
    sent_y = terms(along_y(2, 3), *highs)
    came_y = swap(sent_y, y_1)
    sent_y, *rest = lax.optimization_barrier((sent_y, *highs, *lows))
    sum_x, sum_y = terms(along_x(0, 1), *rest[4:]), terms(along_y(0, 1), *rest[:4])
    groups = (early + middle, late)
    held, sums = zip(*[normed_grad(spots(g), d_low, d_high, tokens, pieces(g)) for g in groups])
    came_x, came_y, sum_x, sum_y, held, sums = lax.optimization_barrier(
        (came_x, came_y, sum_x, sum_y, held, sums)
    )
    d_tokens = tokens_grad(
        spots(early + middle + late),
        [[piece.shape[0] for piece, _ in g] for g in groups],
        tokens,
        scale_r,
        held,
        sums,
    )
    sum_x, sum_y = add(sum_x, came_x), add(sum_y, came_y)
    came_x, came_y = swap(sum_x[4:], x_2), swap(sum_y[4:], y_2)
    came_x, came_y, d_tokens = lax.optimization_barrier((came_x, came_y, d_tokens))
    sum_x, sum_y = add(sum_x[:4], came_x), add(sum_y[:4], came_y)
    for count, step_x, step_y in ((2, y_1, x_1), (1, y_2, x_2)):
        came_x, came_y = swap(sum_x[count:], step_x), swap(sum_y[count:], step_y)
        sum_x, sum_y = add(sum_x[:count], came_x), add(sum_y[:count], came_y)

    total = jnp.concatenate([sum_x[0], sum_y[0]], axis=1).reshape(8, PIECE, QKV)
    got, square = finish(lax.all_to_all(total, "z", 0, 0))

    def x_far(x, y, z, c):
        return x ^ 2, y, z, c

    beside = ((x_1, x_2, x_far), (y_1, y_2, y_far), (z_bit(0),), (z_bit(1),), (z_bit(2),))
    for partner, steps in zip((y_far, z_bit(2), z_bit(1), z_bit(0), other_core), beside):
        came = swap(got, partner)
        square = square + sum([swap(square, s) for s in steps])
        came, square = lax.optimization_barrier((came, square))
        if partner is other_core:
            got_other = came
        else:
            got = jnp.concatenate([got, came], axis=0)
    square = square + swap(square, other_core)
    factor = target_rms * lax.rsqrt(square[0, 0] / (D * QKV) + 1e-06)

    def homes(core):
        own = gray((z + core) % 8)
        out = []
        for i in range(16):
            mask = ((i >> 3) & 1) | (((i >> 2) & 1) << 1) | (((i >> 1) & 1) << 2)
            at_z = (ungray(own ^ mask) + 8 - core) % 8
            out.append(core * HALF + ((y >> 1) ^ (i & 1)) * QUART + at_z * PIECE)
        return jnp.stack(out)

    spots_out = jnp.stack([homes(c), homes(1 - c)]).astype(jnp.int32)
    return d_tokens, rescale(factor, spots_out, got, got_other)


def solution(mesh):
    mesh = Mesh(mesh.devices.reshape(SIZES), AXES)
    spread, rows = P(AXES, None), P(AXES[:2], None)
    return jax.shard_map(
        on_device,
        mesh=mesh,
        in_specs=(spread, spread, spread, rows),
        out_specs=(spread, rows),
        check_vma=False,
    )
```

```python
import jax
import jax.numpy as jnp
from jax import lax
from jax.experimental import pallas as pl
from jax.experimental.pallas import tpu as pltpu
from jax.sharding import Mesh
from jax.sharding import PartitionSpec as P

D = 4096
HD = 128
QH = 8
QKV = 1280
TOK = 256
BLK = D // 8
HALF = BLK // 2
QUART = HALF // 2
PIECE = QUART // 8
COLS = QKV // 2
OUTW = QH * HD
LOW = COLS // HD

AXES = ("x", "y_lo", "y_hi", "z", "core")
SIZES = (4, 2, 2, 8, 2)
target_rms = 0.5
rope_base = 500000.0
F32 = jnp.float32
BF16 = jnp.bfloat16


def place():
    x, y_lo, y_hi, z, c = (lax.axis_index(axis) for axis in AXES)
    return x, y_hi * 2 + y_lo, z, c


def flat(x, y, z, c):
    return (x * 2 + y % 2) * 32 + (y // 2) * 16 + z * 2 + c


def swap(value, partner):
    pairs = []
    for x in range(4):
        for y in range(4):
            for z in range(8):
                for c in range(2):
                    pairs.append((flat(x, y, z, c), flat(*partner(x, y, z, c))))
    return lax.ppermute(value, AXES, pairs)


def near(c):
    return 1 if c == 0 else 3


def other_core(x, y, z, c):
    return x, y, z, 1 - c


def gather_x1(x, y, z, c):
    return x ^ near(c ^ (z & 1)), y, z, c


def gather_x2(x, y, z, c):
    return x ^ (4 - near(c ^ (z & 1))), y, z, c


def flip_y(x, y, z, c):
    return x, y ^ near(c), z, c


def pair_z(x, y, z, c):
    return x, y, (z ^ 1) if c == 0 else ((z + 1) % 8 if z % 2 else (z - 1) % 8), c


def x_1(x, y, z, c):
    return x ^ near(c), y, z, c


def x_2(x, y, z, c):
    return x ^ (4 - near(c)), y, z, c


def y_1(x, y, z, c):
    return x, y ^ near(c), z, c


def y_2(x, y, z, c):
    return x, y ^ (4 - near(c)), z, c


VM = pl.BlockSpec(memory_space=pltpu.VMEM)
SM = pl.BlockSpec(memory_space=pltpu.SMEM)
ANY = pl.BlockSpec(memory_space=pl.ANY)


def dot(a, b, dims):
    return lax.dot_general(a, b, (dims, ((), ())), preferred_element_type=F32)


def norm_body(c, tokens, normed, scale_r, mine, theirs):
    full = tokens[...].astype(F32)
    r = lax.rsqrt(jnp.sum(full * full, axis=1, keepdims=True) * (1.0 / D) + 1e-05)
    scale_r[...] = r
    normed[...] = (full * r).astype(BF16)
    for b in range(8):
        for half, out in ((c[0], mine), (1 - c[0], theirs)):
            cols = pl.ds(pl.multiple_of(b * BLK + half * HALF, HALF), HALF)
            out[b * HALF : (b + 1) * HALF, :] = normed[:, cols].T


def norm(c, tokens):
    turned = jax.ShapeDtypeStruct((D // 2, TOK), BF16)
    return pl.pallas_call(
        norm_body,
        out_shape=(
            jax.ShapeDtypeStruct((TOK, D), BF16),
            jax.ShapeDtypeStruct((TOK, 1), F32),
            turned,
            turned,
        ),
        in_specs=[SM, VM],
        out_specs=(VM, VM, VM, VM),
        compiler_params=pltpu.CompilerParams(vmem_limit_bytes=12 << 20),
        cost_estimate=pl.CostEstimate(flops=10 * TOK * D, bytes_accessed=6 << 20, transcendentals=0),
        name="norm",
    )(c.reshape(1).astype(jnp.int32), tokens)


def halves(pieces):
    return [piece.at[pl.ds(k, HALF), :] for piece in pieces for k in range(0, piece.shape[0], HALF)]


def fetch(pieces, held, sems):
    copies = []
    for i, piece in enumerate(halves(pieces)):
        copies.append(pltpu.make_async_copy(piece, held.at[pl.ds(i * HALF, HALF), :], sems.at[i]))
        copies[-1].start()
    return copies


def project(total, at, normed, held, copies, chunk):
    for first in range(0, len(copies), chunk):
        lhs = []
        for i in range(first, min(first + chunk, len(copies))):
            copies[i].wait()
            lhs.append(normed[:, pl.ds(pl.multiple_of(at[i], HALF), HALF)])
        rows = slice(first * HALF, (first + len(lhs)) * HALF)
        part = dot(jnp.concatenate(lhs, axis=1), held[rows, :], ((1,), (0,)))
        total = part if total is None else total + part
    return total


def part_body(count, at, normed, *refs):
    pieces, out, held, sems = refs[:count], refs[count], refs[count + 1], refs[count + 2]
    out[...] = project(None, at, normed, held, fetch(pieces, held, sems), 4)


def part_qkv(at, normed, pieces):
    count, rows = len(pieces), at.shape[0] * HALF
    return pl.pallas_call(
        lambda *refs: part_body(count, *refs),
        out_shape=jax.ShapeDtypeStruct((TOK, QKV), F32),
        in_specs=[SM, VM] + [ANY] * count,
        out_specs=VM,
        scratch_shapes=[pltpu.VMEM((rows, QKV), BF16), pltpu.SemaphoreType.DMA((rows // HALF,))],
        compiler_params=pltpu.CompilerParams(vmem_limit_bytes=20 << 20),
        cost_estimate=pl.CostEstimate(
            flops=2 * TOK * rows * QKV, bytes_accessed=rows * QKV * 2, transcendentals=0
        ),
        name="qkv_part",
    )(at, normed, *pieces)


def visible(doc_row, doc_col):
    rows = lax.broadcasted_iota(jnp.int32, (TOK, TOK), 0)
    cols = lax.broadcasted_iota(jnp.int32, (TOK, TOK), 1)
    return (cols <= rows) & (doc_col[...] == doc_row[...])


def turn(value, cos, sin):
    return value * cos + pltpu.roll(value, HD // 2, 1) * sin


def head_grads(q_rot, g, k_rot, val, seen, cos, sin):
    scale = HD**-0.5
    scores = jnp.where(seen, dot(q_rot, k_rot, ((1,), (1,))), -1e30)
    expo = jnp.exp((scores - jnp.max(scores, axis=1, keepdims=True)) * scale)
    probs = expo * (1.0 / jnp.sum(expo, axis=1, keepdims=True))
    d_probs = dot(g, val, ((1,), (1,)))
    delta = jnp.sum(d_probs * probs, axis=1, keepdims=True)
    d_scores = (probs * (d_probs - delta)).astype(BF16)
    d_val = dot(probs.astype(BF16), g, ((0,), (0,)))
    d_key = dot(d_scores, q_rot, ((0,), (0,)))
    d_query = dot(d_scores, k_rot, ((1,), (0,))) * scale
    return turn(d_query, cos, -sin).astype(BF16), d_key, d_val


def attend_low_body(count, at, normed, old, grad, doc_row, doc_col, cosine, sine, *refs):
    pieces = refs[:count]
    out, rest, d_key, d_val, held, sems, qkv = refs[count:]
    qkv[...] = project(old[...], at, normed, held, fetch(pieces, held, sems), 2)
    cos, sin = cosine[...], sine[...]
    seen = visible(doc_row, doc_col)
    k_rot = turn(qkv[:, OUTW : OUTW + HD], cos, sin).astype(BF16)
    val = qkv[:, OUTW + HD :].astype(BF16)
    total_key, total_val = jnp.zeros((TOK, HD), F32), jnp.zeros((TOK, HD), F32)
    for h in range(QH):
        head = slice(h * HD, (h + 1) * HD)
        q_rot = turn(qkv[:, head], cos, sin).astype(BF16)
        if h < LOW:
            out[:, head], key, value = head_grads(q_rot, grad[:, head], k_rot, val, seen, cos, sin)
            total_key, total_val = total_key + key, total_val + value
        else:
            rest[:, (h - LOW) * HD : (h - LOW + 1) * HD] = q_rot
    rest[:, COLS - 2 * HD : COLS - HD] = k_rot
    rest[:, COLS - HD :] = val
    d_key[...] = total_key
    d_val[...] = total_val


def attend_high_body(rest, key_low, val_low, grad, doc_row, doc_col, cosine, sine, out):
    cos, sin = cosine[...], sine[...]
    seen = visible(doc_row, doc_col)
    k_rot, val = rest[:, COLS - 2 * HD : COLS - HD], rest[:, COLS - HD :]
    total_key, total_val = key_low[...], val_low[...]
    for h in range(LOW, QH):
        here = slice((h - LOW) * HD, (h - LOW + 1) * HD)
        g = grad[:, h * HD : (h + 1) * HD]
        out[:, here], key, value = head_grads(rest[:, here], g, k_rot, val, seen, cos, sin)
        total_key, total_val = total_key + key, total_val + value
    out[:, COLS - 2 * HD : COLS - HD] = turn(total_key * HD**-0.5, cos, -sin).astype(BF16)
    out[:, COLS - HD :] = total_val.astype(BF16)


def attend_cost(heads):
    return pl.CostEstimate(
        flops=10 * TOK * TOK * HD * heads, bytes_accessed=4 << 20, transcendentals=TOK * TOK * heads
    )


def attend_low(at, normed, pieces, old, grad, doc, cosine, sine):
    count = len(pieces)
    wide, half = jax.ShapeDtypeStruct((TOK, COLS), BF16), jax.ShapeDtypeStruct((TOK, HD), F32)
    return pl.pallas_call(
        lambda *refs: attend_low_body(count, *refs),
        out_shape=(wide, wide, half, half),
        in_specs=[SM] + [VM] * 7 + [ANY] * count,
        out_specs=(VM,) * 4,
        scratch_shapes=[
            pltpu.VMEM((count * HALF, QKV), BF16),
            pltpu.SemaphoreType.DMA((count,)),
            pltpu.VMEM((TOK, QKV), F32),
        ],
        compiler_params=pltpu.CompilerParams(vmem_limit_bytes=16 << 20),
        cost_estimate=attend_cost(LOW),
        name="attend_low",
    )(at, normed, old, grad, doc, doc.reshape(TOK, 1), cosine, sine, *pieces)


def attend_high(rest, d_key, d_val, grad, doc, cosine, sine):
    return pl.pallas_call(
        attend_high_body,
        out_shape=jax.ShapeDtypeStruct((TOK, COLS), BF16),
        in_specs=[VM] * 8,
        out_specs=VM,
        compiler_params=pltpu.CompilerParams(vmem_limit_bytes=12 << 20),
        cost_estimate=attend_cost(QH - LOW),
        name="attend_high",
    )(rest, d_key, d_val, grad, doc, doc.reshape(TOK, 1), cosine, sine)


SLOTS = 4


def tokens_body(count, at, d_low, d_high, tokens, scale_r, *refs):
    pieces = halves(refs[:count])
    out, slots, sems, held, d_qkv = refs[count:]
    count = len(pieces)

    def copy(i):
        return pltpu.make_async_copy(pieces[i], slots.at[i % SLOTS], sems.at[i % SLOTS])

    for i in range(SLOTS):
        copy(i).start()
    d_qkv[:, :COLS] = d_low[...]
    d_qkv[:, COLS:] = d_high[...]
    total = jnp.zeros((TOK, 128), F32)
    for i in range(count):
        cols = pl.ds(pl.multiple_of(at[i], HALF), HALF)
        copy(i).wait()
        part = dot(d_qkv[...], slots[i % SLOTS], ((1,), (1,)))
        if i + SLOTS < count:
            copy(i + SLOTS).start()
        held[:, cols] = part
        part = part * tokens[:, cols].astype(F32)
        for k in range(0, HALF, 128):
            total = total + part[:, k : k + 128]
    r = scale_r[...]
    back = r * r * r * (jnp.sum(total, axis=1, keepdims=True) * (1.0 / D))
    for k in range(0, D, 512):
        cols = slice(k, k + 512)
        out[:, cols] = (r * held[:, cols] - tokens[:, cols].astype(F32) * back).astype(BF16)


def tokens_grad(at, d_low, d_high, tokens, scale_r, pieces):
    count = len(pieces)
    return pl.pallas_call(
        lambda *refs: tokens_body(count, *refs),
        out_shape=jax.ShapeDtypeStruct((TOK, D), BF16),
        in_specs=[SM] + [VM] * 4 + [ANY] * count,
        out_specs=VM,
        scratch_shapes=[
            pltpu.VMEM((SLOTS, HALF, QKV), BF16),
            pltpu.SemaphoreType.DMA((SLOTS,)),
            pltpu.VMEM((TOK, D), F32),
            pltpu.VMEM((TOK, QKV), BF16),
        ],
        compiler_params=pltpu.CompilerParams(vmem_limit_bytes=20 << 20),
        cost_estimate=pl.CostEstimate(flops=2 * TOK * D * QKV, bytes_accessed=16 << 20, transcendentals=0),
        name="tokens_grad",
    )(at, d_low, d_high, tokens, scale_r, *pieces)


def term_product(count, at, feats, feats_other, d_own, d_other, left, sems):
    copies = []
    for i in range(count):
        rows = pl.ds(pl.multiple_of(at[i], QUART), QUART)
        into = pl.ds(i * QUART, QUART)
        for k, ref in enumerate((feats, feats_other)):
            cols = pl.ds(k * TOK, TOK)
            copies.append(pltpu.make_async_copy(ref.at[rows, :], left.at[into, cols], sems.at[2 * i + k]))
            copies[-1].start()
    right = jnp.concatenate([d_own[...], d_other[...]], axis=0)
    for copy in copies:
        copy.wait()
    return dot(left[...], right, ((1,), (0,)))


def term_body(count, at, feats, feats_other, d_own, d_other, out, left, sems):
    part = term_product(count, at, feats, feats_other, d_own, d_other, left, sems)
    out[...] = part.astype(BF16).reshape(count, QUART, COLS)


def term_add_body(count, at, feats, feats_other, d_own, d_other, came, kept, sent, left, sems):
    part = term_product(count, at, feats, feats_other, d_own, d_other, left, sems)
    part = (part.reshape(count, QUART, COLS) + came[...].astype(F32)).astype(BF16)
    kept[...] = part[: count // 2]
    sent[...] = part[count // 2 :]


def terms(at, made, *came):
    count = at.shape[0]
    if came:
        half = jax.ShapeDtypeStruct((count // 2, QUART, COLS), BF16)
        body, out_shape, out_specs = term_add_body, (half, half), (VM, VM)
    else:
        out_shape, out_specs = jax.ShapeDtypeStruct((count, QUART, COLS), BF16), VM
        body = term_body
    return pl.pallas_call(
        lambda *refs: body(count, *refs),
        out_shape=out_shape,
        in_specs=[SM, ANY, ANY, VM, VM] + [VM] * len(came),
        out_specs=out_specs,
        scratch_shapes=[pltpu.VMEM((count * QUART, 2 * TOK), BF16), pltpu.SemaphoreType.DMA((2 * count,))],
        compiler_params=pltpu.CompilerParams(vmem_limit_bytes=12 << 20),
        cost_estimate=pl.CostEstimate(
            flops=2 * count * QUART * COLS * 2 * TOK, bytes_accessed=4 << 20, transcendentals=0
        ),
        name="terms",
    )(at, *made, *came)


def split_body(count, old, came, kept, sent):
    part = (old[...].astype(F32) + came[...].astype(F32)).astype(BF16)
    kept[...] = part[: count // 2]
    sent[...] = part[count // 2 :]


def split(old, came):
    count = old.shape[0]
    half = jax.ShapeDtypeStruct((count // 2, QUART, COLS), BF16)
    return pl.pallas_call(
        lambda *refs: split_body(count, *refs),
        out_shape=(half, half),
        in_specs=[VM, VM],
        out_specs=(VM, VM),
        compiler_params=pltpu.CompilerParams(vmem_limit_bytes=6 << 20),
        name="split",
    )(old, came)


def join_body(old_x, came_x, old_y, came_y, out):
    out[:, :, :COLS] = (old_x[...].astype(F32) + came_x[...].astype(F32)).astype(BF16).reshape(8, PIECE, COLS)
    out[:, :, COLS:] = (old_y[...].astype(F32) + came_y[...].astype(F32)).astype(BF16).reshape(8, PIECE, COLS)


def join(*parts):
    return pl.pallas_call(
        join_body,
        out_shape=jax.ShapeDtypeStruct((8, PIECE, QKV), BF16),
        in_specs=[VM] * 4,
        out_specs=VM,
        compiler_params=pltpu.CompilerParams(vmem_limit_bytes=4 << 20),
        name="join",
    )(*parts)


def finish_body(parts, out):
    total = sum(parts[i].astype(F32) for i in range(8)).astype(BF16)
    for i in range(16):
        out[i] = total


def finish(parts):
    return pl.pallas_call(
        finish_body,
        out_shape=jax.ShapeDtypeStruct((16, PIECE, QKV), BF16),
        in_specs=[VM],
        out_specs=VM,
        compiler_params=pltpu.CompilerParams(vmem_limit_bytes=4 << 20),
        name="finish",
    )(parts)


def squares_body(got, out):
    total = jnp.zeros((PIECE, QKV), F32)
    for i in range(16):
        value = got[i].astype(F32)
        total = total + value * value
    total = jnp.sum(jnp.sum(total, axis=1, keepdims=True), axis=0, keepdims=True)
    out[...] = jnp.broadcast_to(total.reshape(1, 1, 1), (16, 8, 128))


def squares(got):
    return pl.pallas_call(
        squares_body,
        out_shape=jax.ShapeDtypeStruct((16, 8, 128), F32),
        in_specs=[VM],
        out_specs=VM,
        compiler_params=pltpu.CompilerParams(vmem_limit_bytes=4 << 20),
        name="squares",
    )(got)


def rescale_body(at, parts, mine, theirs, out):
    total = sum(parts[i] for i in range(16))
    factor = (target_rms * lax.rsqrt(total * (1.0 / (D * QKV)) + 1e-06))[:1, :1]
    for i, half in enumerate((mine, theirs)):
        rows = pl.ds(pl.multiple_of(at[i], HALF), HALF)
        out[rows, :] = (half[...].reshape(HALF, QKV).astype(F32) * factor).astype(BF16)


def rescale(at, parts, mine, theirs):
    return pl.pallas_call(
        rescale_body,
        out_shape=jax.ShapeDtypeStruct((BLK, QKV), BF16),
        in_specs=[SM, VM, VM, VM],
        out_specs=VM,
        compiler_params=pltpu.CompilerParams(vmem_limit_bytes=8 << 20),
        name="rescale",
    )(at, parts, mine, theirs)


def tables():
    position = jnp.arange(TOK, dtype=F32)
    freq = jnp.exp(-jnp.log(rope_base) * 2.0 * jnp.arange(HD // 2, dtype=F32) / HD)
    angle = position[:, None] * freq[None, :]
    cos, sin = jnp.cos(angle), jnp.sin(angle)
    return jnp.concatenate([cos, cos], axis=1), jnp.concatenate([-sin, sin], axis=1)


def on_device(tokens, grad_attended, doc_ids, w_own):
    x, y, z, c = place()

    w00 = lax.dynamic_slice_in_dim(w_own, c * HALF, HALF, 0)
    wa0 = swap(w00, gather_x1)
    w01 = swap(w00, flip_y)
    normed, scale_r, feats, theirs = norm(c, tokens)
    cosine, sine = tables()
    wa0, normed, theirs, cosine, sine = lax.optimization_barrier((wa0, normed, theirs, cosine, sine))
    wo0 = swap(wa0, gather_x2)
    wa1 = swap(wa0, flip_y)
    wb0 = swap(wa0, pair_z)
    vb0 = swap(wa0, other_core)
    v01 = swap(w01, other_core)

    turn = c ^ (z & 1)
    p1 = 1 + 2 * turn
    p2 = 4 - p1
    step = {"0": 0, "a": p1, "b": p2, "o": 2}

    def column(name, flip, half):
        return ((x ^ step[name]) * 2 + ((y & 1) ^ flip)) * BLK + half * HALF

    def spots(group):
        return jnp.stack([spot for _, *spots in group for spot in spots]).astype(jnp.int32)

    def pieces(group):
        return [piece for piece, *_ in group]

    early = [
        (w_own, column("0", 0, 0), column("0", 0, 1)),
        (w01, column("0", 1, c)),
        (wa0, column("a", 0, c)),
        (vb0, column("b", 0, 1 - c)),
        (v01, column("0", 1, 1 - c)),
    ]
    wo1 = swap(wo0, flip_y)
    wb1 = swap(wa1, pair_z)
    vo0 = swap(wo0, other_core)
    va0 = swap(wb0, other_core)
    vb1 = swap(wa1, other_core)
    feats_other = swap(theirs, other_core)
    middle = [
        (wo0, column("o", 0, c)),
        (wa1, column("a", 1, c)),
        (wb0, column("b", 0, c)),
        (vo0, column("o", 0, 1 - c)),
        (vb1, column("b", 1, 1 - c)),
        (va0, column("a", 0, 1 - c)),
    ]
    part = part_qkv(spots(early + middle), normed, pieces(early + middle))
    wo1, wb1, part = lax.optimization_barrier((wo1, wb1, part))
    vo1 = swap(wo1, other_core)
    va1 = swap(wb1, other_core)
    late = [
        (wo1, column("o", 1, c)),
        (wb1, column("b", 1, c)),
        (vo1, column("o", 1, 1 - c)),
        (va1, column("a", 1, 1 - c)),
    ]
    d_low, rest, d_key, d_val = attend_low(
        spots(late), normed, pieces(late), part, grad_attended, doc_ids, cosine, sine
    )

    low_other = swap(d_low, other_core)
    d_high = attend_high(rest, d_key, d_val, grad_attended, doc_ids, cosine, sine)
    low_other, d_high = lax.optimization_barrier((low_other, d_high))
    high_other = swap(d_high, other_core)
    q1 = 1 + 2 * c
    order = [0, 4 - q1, q1, 2]

    def row(xm, ym):
        yy = y ^ ym
        return ((x ^ xm) * 2 + (yy & 1)) * HALF + (yy >> 1) * QUART

    def along_x(first, second):
        return jnp.stack([row(order[i], order[j]) for i in (first, second) for j in range(4)]).astype(jnp.int32)

    def along_y(first, second):
        return jnp.stack([row(order[i], order[j]) for j in (first, second) for i in range(4)]).astype(jnp.int32)

    lows, highs = (feats, feats_other, d_low, low_other), (feats, feats_other, d_high, high_other)
    came_x = swap(terms(along_x(2, 3), lows), x_1)
    came_y = swap(terms(along_y(2, 3), highs), y_1)
    every = early + middle + late
    d_tokens = tokens_grad(spots(every), d_low, d_high, tokens, scale_r, pieces(every))
    came_x, came_y, d_tokens = lax.optimization_barrier((came_x, came_y, d_tokens))
    sum_x, sent_x = terms(along_x(0, 1), lows, came_x)
    came_x = swap(sent_x, x_2)
    sum_y, sent_y = terms(along_y(0, 1), highs, came_y)
    came_y = swap(sent_y, y_2)
    for step_x, step_y in ((y_1, x_1), (y_2, x_2)):
        sum_x, sent_x = split(sum_x, came_x)
        came_x = swap(sent_x, step_x)
        sum_y, sent_y = split(sum_y, came_y)
        came_y = swap(sent_y, step_y)

    total = join(sum_x, came_x, sum_y, came_y)
    got = finish(lax.all_to_all(total, "z", 0, 0))
    got = lax.all_to_all(got, ("y_hi", "z"), 0, 0)

    theirs = swap(got, other_core)
    parts = lax.all_to_all(squares(got), ("x", "y_lo", "core"), 0, 0)
    at = jnp.stack([c * HALF, (1 - c) * HALF]).astype(jnp.int32)
    return d_tokens, rescale(at, parts, got, theirs)


def solution(mesh):
    mesh = Mesh(mesh.devices.reshape(SIZES), AXES)
    spread, rows = P(AXES, None), P(AXES[:2], None)
    return jax.shard_map(
        on_device,
        mesh=mesh,
        in_specs=(spread, spread, spread, rows),
        out_specs=(spread, rows),
        check_vma=False,
    )
```

```python
import jax
import jax.numpy as jnp
import numpy as np
from jax import lax
from jax.experimental import pallas as pl
from jax.experimental.pallas import tpu as pltpu
from jax.sharding import Mesh
from jax.sharding import PartitionSpec as P

D = 4096
HD = 128
QH = 8
QKV = 1280
TOK = 256
BLK = D // 8
HALF = BLK // 2
QUART = HALF // 2
PIECE = QUART // 8
COLS = QKV // 2
OUTW = QH * HD
LOW = COLS // HD

AXES = ("x", "y_lo", "y_hi", "z", "core")
SIZES = (4, 2, 2, 8, 2)
target_rms = 0.5
rope_base = 500000.0
F32 = jnp.float32
BF16 = jnp.bfloat16


def flat(x, y, z, c):
    return (x * 2 + y % 2) * 32 + (y // 2) * 16 + z * 2 + c


def swap(value, partner):
    pairs = []
    for x in range(4):
        for y in range(4):
            for z in range(8):
                for c in range(2):
                    pairs.append((flat(x, y, z, c), flat(*partner(x, y, z, c))))
    return lax.ppermute(value, AXES, pairs)


def near(c):
    return 1 if c == 0 else 3


def other_core(x, y, z, c):
    return x, y, z, 1 - c


def gather_x1(x, y, z, c):
    return x ^ near(c ^ (z & 1)), y, z, c


def gather_x2(x, y, z, c):
    return x ^ (4 - near(c ^ (z & 1))), y, z, c


def flip_y(x, y, z, c):
    return x, y ^ near(c), z, c


def pair_z(x, y, z, c):
    return x, y, (z ^ 1) if c == 0 else ((z + 1) % 8 if z % 2 else (z - 1) % 8), c


def x_1(x, y, z, c):
    return x ^ near(c), y, z, c


def x_2(x, y, z, c):
    return x ^ (4 - near(c)), y, z, c


def y_1(x, y, z, c):
    return x, y ^ near(c), z, c


def y_2(x, y, z, c):
    return x, y ^ (4 - near(c)), z, c


VM = pl.BlockSpec(memory_space=pltpu.VMEM)
SM = pl.BlockSpec(memory_space=pltpu.SMEM)
ANY = pl.BlockSpec(memory_space=pl.ANY)


def dot(a, b, dims):
    return lax.dot_general(a, b, (dims, ((), ())), preferred_element_type=F32)


def norm_body(at, tokens, normed, scale_r, mine, theirs):
    full = tokens[...].astype(F32)
    r = lax.rsqrt(jnp.sum(full * full, axis=1, keepdims=True) * (1.0 / D) + 1e-05)
    scale_r[...] = r
    normed[...] = (full * r).astype(BF16)
    for b in range(8):
        for k, out in enumerate((mine, theirs)):
            cols = pl.ds(pl.multiple_of(b * BLK + at[SIDE + k], HALF), HALF)
            out[b * HALF : (b + 1) * HALF, :] = normed[:, cols].T


def norm(at, tokens):
    turned = jax.ShapeDtypeStruct((D // 2, TOK), BF16)
    return pl.pallas_call(
        norm_body,
        out_shape=(
            jax.ShapeDtypeStruct((TOK, D), BF16),
            jax.ShapeDtypeStruct((TOK, 1), F32),
            turned,
            turned,
        ),
        in_specs=[SM, VM],
        out_specs=(VM, VM, VM, VM),
        compiler_params=pltpu.CompilerParams(vmem_limit_bytes=12 << 20),
        cost_estimate=pl.CostEstimate(flops=10 * TOK * D, bytes_accessed=6 << 20, transcendentals=0),
        name="norm",
    )(at, tokens)


def halves(pieces):
    return [piece[k : k + HALF, :] for piece in pieces for k in range(0, piece.shape[0], HALF)]


def project(at, first, normed, pieces):
    rows = halves(pieces)
    lhs = [normed[:, pl.ds(pl.multiple_of(at[first + i], HALF), HALF)] for i in range(len(rows))]
    return dot(jnp.concatenate(lhs, axis=1), jnp.concatenate(rows, axis=0), ((1,), (0,)))


def part_body(count, first, at, normed, *refs):
    part = project(at, first, normed, refs[:count])
    out = refs[-1]
    out[...] = part if len(refs) == count + 1 else part + refs[count][...]


def part_qkv(at, first, normed, pieces, *old):
    count, rows = len(pieces), sum(piece.shape[0] for piece in pieces)
    return pl.pallas_call(
        lambda *refs: part_body(count, first, *refs),
        out_shape=jax.ShapeDtypeStruct((TOK, QKV), F32),
        in_specs=[SM, VM] + [VM] * (count + len(old)),
        out_specs=VM,
        compiler_params=pltpu.CompilerParams(vmem_limit_bytes=16 << 20),
        cost_estimate=pl.CostEstimate(
            flops=2 * TOK * rows * QKV, bytes_accessed=rows * QKV * 2, transcendentals=0
        ),
        name="qkv_part",
    )(at, normed, *pieces, *old)


def visible(doc):
    rows = lax.broadcasted_iota(jnp.int32, (TOK, TOK), 0)
    cols = lax.broadcasted_iota(jnp.int32, (TOK, TOK), 1)
    along = jnp.broadcast_to(doc[...], (TOK, TOK))
    return (cols <= rows) & (along == along.T)


def turn(value, cos, sin):
    return value * cos + pltpu.roll(value, HD // 2, 1) * sin


def head_grads(q_rot, g, k_rot, val, seen, cos, sin):
    scale = HD**-0.5
    scores = jnp.where(seen, dot(q_rot, k_rot, ((1,), (1,))), -1e30)
    expo = jnp.exp((scores - jnp.max(scores, axis=1, keepdims=True)) * scale)
    probs = expo * (1.0 / jnp.sum(expo, axis=1, keepdims=True))
    d_probs = dot(g, val, ((1,), (1,)))
    delta = jnp.sum(d_probs * probs, axis=1, keepdims=True)
    d_scores = (probs * (d_probs - delta)).astype(BF16)
    d_val = dot(probs.astype(BF16), g, ((0,), (0,)))
    d_key = dot(d_scores, q_rot, ((0,), (0,)))
    d_query = dot(d_scores, k_rot, ((1,), (0,))) * scale
    return turn(d_query, cos, -sin).astype(BF16), d_key, d_val


def attend_low_body(count, first, at, normed, old, grad, doc, cosine, sine, *refs):
    pieces = refs[:count]
    out, rest, d_key, d_val, qkv = refs[count:]
    qkv[...] = old[...] + project(at, first, normed, pieces)
    cos, sin = cosine[...], sine[...]
    seen = visible(doc)
    k_rot = turn(qkv[:, OUTW : OUTW + HD], cos, sin).astype(BF16)
    val = qkv[:, OUTW + HD :].astype(BF16)
    total_key, total_val = jnp.zeros((TOK, HD), F32), jnp.zeros((TOK, HD), F32)
    for h in range(QH):
        head = slice(h * HD, (h + 1) * HD)
        q_rot = turn(qkv[:, head], cos, sin).astype(BF16)
        if h < LOW:
            out[:, head], key, value = head_grads(q_rot, grad[:, head], k_rot, val, seen, cos, sin)
            total_key, total_val = total_key + key, total_val + value
        else:
            rest[:, (h - LOW) * HD : (h - LOW + 1) * HD] = q_rot
    rest[:, COLS - 2 * HD : COLS - HD] = k_rot
    rest[:, COLS - HD :] = val
    d_key[...] = total_key
    d_val[...] = total_val


def attend_high_body(rest, key_low, val_low, grad, doc, cosine, sine, out):
    cos, sin = cosine[...], sine[...]
    seen = visible(doc)
    k_rot, val = rest[:, COLS - 2 * HD : COLS - HD], rest[:, COLS - HD :]
    total_key, total_val = key_low[...], val_low[...]
    for h in range(LOW, QH):
        here = slice((h - LOW) * HD, (h - LOW + 1) * HD)
        g = grad[:, h * HD : (h + 1) * HD]
        out[:, here], key, value = head_grads(rest[:, here], g, k_rot, val, seen, cos, sin)
        total_key, total_val = total_key + key, total_val + value
    out[:, COLS - 2 * HD : COLS - HD] = turn(total_key * HD**-0.5, cos, -sin).astype(BF16)
    out[:, COLS - HD :] = total_val.astype(BF16)


def attend_cost(heads):
    return pl.CostEstimate(
        flops=10 * TOK * TOK * HD * heads, bytes_accessed=4 << 20, transcendentals=TOK * TOK * heads
    )


def attend_low(at, first, normed, pieces, old, grad, doc):
    count = len(pieces)
    wide, half = jax.ShapeDtypeStruct((TOK, COLS), BF16), jax.ShapeDtypeStruct((TOK, HD), F32)
    return pl.pallas_call(
        lambda *refs: attend_low_body(count, first, *refs),
        out_shape=(wide, wide, half, half),
        in_specs=[SM] + [VM] * (6 + count),
        out_specs=(VM,) * 4,
        scratch_shapes=[pltpu.VMEM((TOK, QKV), F32)],
        compiler_params=pltpu.CompilerParams(vmem_limit_bytes=12 << 20),
        cost_estimate=attend_cost(LOW),
        name="attend_low",
    )(at, normed, old, grad, doc, *TABLES, *pieces)


def attend_high(rest, d_key, d_val, grad, doc):
    return pl.pallas_call(
        attend_high_body,
        out_shape=jax.ShapeDtypeStruct((TOK, COLS), BF16),
        in_specs=[VM] * 7,
        out_specs=VM,
        compiler_params=pltpu.CompilerParams(vmem_limit_bytes=12 << 20),
        cost_estimate=attend_cost(QH - LOW),
        name="attend_high",
    )(rest, d_key, d_val, grad, doc, *TABLES)


def tokens_body(count, first, at, d_low, d_high, tokens, scale_r, *refs):
    out, held = refs[count:]
    d_qkv = jnp.concatenate([d_low[...], d_high[...]], axis=1)
    total = jnp.zeros((TOK, 128), F32)
    for i, piece in enumerate(halves(refs[:count])):
        cols = pl.ds(pl.multiple_of(at[first + i], HALF), HALF)
        part = dot(d_qkv, piece, ((1,), (1,)))
        held[:, cols] = part
        part = part * tokens[:, cols].astype(F32)
        for k in range(0, HALF, 128):
            total = total + part[:, k : k + 128]
    r = scale_r[...]
    back = r * r * r * (jnp.sum(total, axis=1, keepdims=True) * (1.0 / D))
    for k in range(0, D, 512):
        cols = slice(k, k + 512)
        out[:, cols] = (r * held[:, cols] - tokens[:, cols].astype(F32) * back).astype(BF16)


def tokens_grad(at, first, d_low, d_high, tokens, scale_r, pieces):
    count = len(pieces)
    return pl.pallas_call(
        lambda *refs: tokens_body(count, first, *refs),
        out_shape=jax.ShapeDtypeStruct((TOK, D), BF16),
        in_specs=[SM] + [VM] * (4 + count),
        out_specs=VM,
        scratch_shapes=[pltpu.VMEM((TOK, D), F32)],
        compiler_params=pltpu.CompilerParams(vmem_limit_bytes=28 << 20),
        cost_estimate=pl.CostEstimate(flops=2 * TOK * D * QKV, bytes_accessed=16 << 20, transcendentals=0),
        name="tokens_grad",
    )(at, d_low, d_high, tokens, scale_r, *pieces)


def term_product(first, at, feats, feats_other, d_own, d_other):
    left = []
    for ref in (feats, feats_other):
        rows = [ref[pl.ds(pl.multiple_of(at[first + i], QUART), QUART), :] for i in range(8)]
        left.append(jnp.concatenate(rows, axis=0))
    right = jnp.concatenate([d_own[...], d_other[...]], axis=0)
    part = dot(jnp.concatenate(left, axis=1), right, ((1,), (0,)))
    return part.reshape(8, QUART, COLS)


def term_body(first, at, feats, feats_other, d_own, d_other, out):
    out[...] = term_product(first, at, feats, feats_other, d_own, d_other).astype(BF16)


def term_add_body(first, at, feats, feats_other, d_own, d_other, came, kept, sent):
    part = term_product(first, at, feats, feats_other, d_own, d_other)
    part = (part + came[...].astype(F32)).astype(BF16)
    kept[...] = part[:4]
    sent[...] = part[4:]


def terms(at, first, made, *came):
    if came:
        half = jax.ShapeDtypeStruct((4, QUART, COLS), BF16)
        body, out_shape, out_specs = term_add_body, (half, half), (VM, VM)
    else:
        out_shape, out_specs = jax.ShapeDtypeStruct((8, QUART, COLS), BF16), VM
        body = term_body
    return pl.pallas_call(
        lambda *refs: body(first, *refs),
        out_shape=out_shape,
        in_specs=[SM] + [VM] * (4 + len(came)),
        out_specs=out_specs,
        compiler_params=pltpu.CompilerParams(vmem_limit_bytes=12 << 20),
        cost_estimate=pl.CostEstimate(
            flops=2 * 8 * QUART * COLS * 2 * TOK, bytes_accessed=4 << 20, transcendentals=0
        ),
        name="terms",
    )(at, *made, *came)


def split_body(count, old, came, kept, sent):
    part = (old[...].astype(F32) + came[...].astype(F32)).astype(BF16)
    kept[...] = part[: count // 2]
    sent[...] = part[count // 2 :]


def split(old, came):
    count = old.shape[0]
    half = jax.ShapeDtypeStruct((count // 2, QUART, COLS), BF16)
    return pl.pallas_call(
        lambda *refs: split_body(count, *refs),
        out_shape=(half, half),
        in_specs=[VM, VM],
        out_specs=(VM, VM),
        compiler_params=pltpu.CompilerParams(vmem_limit_bytes=6 << 20),
        name="split",
    )(old, came)


def join_body(old_x, came_x, old_y, came_y, out):
    out[:, :, :COLS] = (old_x[...].astype(F32) + came_x[...].astype(F32)).astype(BF16).reshape(8, PIECE, COLS)
    out[:, :, COLS:] = (old_y[...].astype(F32) + came_y[...].astype(F32)).astype(BF16).reshape(8, PIECE, COLS)


def join(*parts):
    return pl.pallas_call(
        join_body,
        out_shape=jax.ShapeDtypeStruct((8, PIECE, QKV), BF16),
        in_specs=[VM] * 4,
        out_specs=VM,
        compiler_params=pltpu.CompilerParams(vmem_limit_bytes=4 << 20),
        name="join",
    )(*parts)


def finish_body(parts, out):
    total = sum(parts[i].astype(F32) for i in range(8)).astype(BF16)
    for i in range(16):
        out[i] = total


def finish(parts):
    return pl.pallas_call(
        finish_body,
        out_shape=jax.ShapeDtypeStruct((16, PIECE, QKV), BF16),
        in_specs=[VM],
        out_specs=VM,
        compiler_params=pltpu.CompilerParams(vmem_limit_bytes=4 << 20),
        name="finish",
    )(parts)


def squares_body(got, out):
    total = jnp.zeros((PIECE, QKV), F32)
    for i in range(16):
        value = got[i].astype(F32)
        total = total + value * value
    total = jnp.sum(jnp.sum(total, axis=1, keepdims=True), axis=0, keepdims=True)
    out[...] = jnp.broadcast_to(total.reshape(1, 1, 1), (16, 8, 128))


def squares(got):
    return pl.pallas_call(
        squares_body,
        out_shape=jax.ShapeDtypeStruct((16, 8, 128), F32),
        in_specs=[VM],
        out_specs=VM,
        compiler_params=pltpu.CompilerParams(vmem_limit_bytes=4 << 20),
        name="squares",
    )(got)


def rescale_body(at, parts, mine, theirs, out):
    total = sum(parts[i] for i in range(16))
    factor = (target_rms * lax.rsqrt(total * (1.0 / (D * QKV)) + 1e-06))[:1, :1]
    for i, half in enumerate((mine, theirs)):
        rows = pl.ds(pl.multiple_of(at[SIDE + i], HALF), HALF)
        out[rows, :] = (half[...].reshape(HALF, QKV).astype(F32) * factor).astype(BF16)


def rescale(at, parts, mine, theirs):
    return pl.pallas_call(
        rescale_body,
        out_shape=jax.ShapeDtypeStruct((BLK, QKV), BF16),
        in_specs=[SM, VM, VM, VM],
        out_specs=VM,
        compiler_params=pltpu.CompilerParams(vmem_limit_bytes=8 << 20),
        name="rescale",
    )(at, parts, mine, theirs)


def tables():
    freq = np.exp(-np.log(rope_base) * 2.0 * np.arange(HD // 2) / HD)
    angle = np.arange(TOK)[:, None] * freq[None, :]
    cos, sin = np.cos(angle), np.sin(angle)
    return np.concatenate([cos, cos], 1).astype(np.float32), np.concatenate([-sin, sin], 1).astype(np.float32)


TABLES = tables()

LATE, SIDE, SEND_X, SEND_Y, KEEP_X, KEEP_Y = 12, 16, 18, 26, 34, 42


def indices(x, y, z, c):
    turned = c ^ (z & 1)
    step = {"0": 0, "a": 1 + 2 * turned, "b": 3 - 2 * turned, "o": 2}

    def column(name, flip, half):
        return ((x ^ step[name]) * 2 + ((y & 1) ^ flip)) * BLK + half * HALF

    own, other = c, 1 - c
    first = [("0", 0, 0), ("0", 0, 1), ("0", 1, own), ("a", 0, own), ("b", 0, other), ("0", 1, other)]
    middle = [("o", 0, own), ("a", 1, own), ("b", 0, own), ("o", 0, other), ("b", 1, other), ("a", 0, other)]
    late = [("o", 1, own), ("b", 1, own), ("o", 1, other), ("a", 1, other)]
    out = [column(*spot) for spot in first + middle + late] + [own * HALF, other * HALF]
    order = [0, 3 - 2 * c, 1 + 2 * c, 2]

    def row(i, j):
        yy = y ^ order[j]
        return ((x ^ order[i]) * 2 + (yy & 1)) * HALF + (yy >> 1) * QUART

    for pair in ((2, 3), (0, 1)):
        out += [row(i, j) for i in pair for j in range(4)]
        out += [row(i, j) for j in pair for i in range(4)]
    return out


def index_table():
    rows = [None] * 256
    for x in range(4):
        for y in range(4):
            for z in range(8):
                for c in range(2):
                    rows[flat(x, y, z, c)] = indices(x, y, z, c)
    return np.array(rows, np.int32)


def on_device(tokens, grad_attended, doc_ids, w_own):
    c = lax.axis_index("core")
    at = lax.dynamic_index_in_dim(jnp.asarray(index_table()), lax.axis_index(AXES), 0, False)

    w00 = lax.dynamic_slice_in_dim(w_own, c * HALF, HALF, 0)
    at, w00 = lax.optimization_barrier((at, w00))
    wa0 = swap(w00, gather_x1)
    w01 = swap(w00, flip_y)
    normed, scale_r, feats, theirs = norm(at, tokens)
    wa0, normed, theirs = lax.optimization_barrier((wa0, normed, theirs))
    wo0 = swap(wa0, gather_x2)
    wa1 = swap(wa0, flip_y)
    wb0 = swap(wa0, pair_z)
    vb0 = swap(wa0, other_core)
    v01 = swap(w01, other_core)
    early = [w_own, w01, wa0, vb0, v01]
    part = part_qkv(at, 0, normed, early)
    wo0, wa1, part = lax.optimization_barrier((wo0, wa1, part))
    wo1 = swap(wo0, flip_y)
    wb1 = swap(wa1, pair_z)
    vo0 = swap(wo0, other_core)
    va0 = swap(wb0, other_core)
    vb1 = swap(wa1, other_core)
    feats_other = swap(theirs, other_core)
    middle = [wo0, wa1, wb0, vo0, vb1, va0]
    part = part_qkv(at, 6, normed, middle, part)
    wo1, wb1, part = lax.optimization_barrier((wo1, wb1, part))
    vo1 = swap(wo1, other_core)
    va1 = swap(wb1, other_core)
    late = [wo1, wb1, vo1, va1]
    d_low, rest, d_key, d_val = attend_low(at, LATE, normed, late, part, grad_attended, doc_ids)

    low_other = swap(d_low, other_core)
    d_high = attend_high(rest, d_key, d_val, grad_attended, doc_ids)
    low_other, d_high = lax.optimization_barrier((low_other, d_high))
    high_other = swap(d_high, other_core)
    lows, highs = (feats, feats_other, d_low, low_other), (feats, feats_other, d_high, high_other)
    came_x = swap(terms(at, SEND_X, lows), x_1)
    came_y = swap(terms(at, SEND_Y, highs), y_1)
    d_tokens = tokens_grad(at, 0, d_low, d_high, tokens, scale_r, early + middle + late)
    came_x, came_y, d_tokens = lax.optimization_barrier((came_x, came_y, d_tokens))
    sum_x, sent_x = terms(at, KEEP_X, lows, came_x)
    came_x = swap(sent_x, x_2)
    sum_y, sent_y = terms(at, KEEP_Y, highs, came_y)
    came_y = swap(sent_y, y_2)
    for step_x, step_y in ((y_1, x_1), (y_2, x_2)):
        sum_x, sent_x = split(sum_x, came_x)
        came_x = swap(sent_x, step_x)
        sum_y, sent_y = split(sum_y, came_y)
        came_y = swap(sent_y, step_y)

    total = join(sum_x, came_x, sum_y, came_y)
    got = finish(lax.all_to_all(total, "z", 0, 0))
    got = lax.all_to_all(got, ("y_hi", "z"), 0, 0)

    theirs = swap(got, other_core)
    parts = lax.all_to_all(squares(got), ("x", "y_lo", "core"), 0, 0)
    return d_tokens, rescale(at, parts, got, theirs)


def solution(mesh):
    mesh = Mesh(mesh.devices.reshape(SIZES), AXES)
    spread, rows = P(AXES, None), P(AXES[:2], None)
    return jax.shard_map(
        on_device,
        mesh=mesh,
        in_specs=(spread, spread, spread, rows),
        out_specs=(spread, rows),
        check_vma=False,
    )
```

```python
import jax
import jax.numpy as jnp
import numpy as np
from jax import lax
from jax.experimental import pallas as pl
from jax.experimental.pallas import tpu as pltpu
from jax.sharding import Mesh
from jax.sharding import PartitionSpec as P

D = 4096
HD = 128
QH = 8
QKV = 1280
TOK = 256
BLK = D // 8
HALF = BLK // 2
QUART = HALF // 2
PIECE = QUART // 8
COLS = QKV // 2
OUTW = QH * HD
LOW = COLS // HD

AXES = ("x", "y_lo", "y_hi", "z", "core")
SIZES = (4, 2, 2, 8, 2)
target_rms = 0.5
rope_base = 500000.0
F32 = jnp.float32
BF16 = jnp.bfloat16


def flat(x, y, z, c):
    return (x * 2 + y % 2) * 32 + (y // 2) * 16 + z * 2 + c


def swap(value, partner):
    pairs = []
    for x in range(4):
        for y in range(4):
            for z in range(8):
                for c in range(2):
                    pairs.append((flat(x, y, z, c), flat(*partner(x, y, z, c))))
    return lax.ppermute(value, AXES, pairs)


def near(c):
    return 1 if c == 0 else 3


def other_core(x, y, z, c):
    return x, y, z, 1 - c


def gather_x1(x, y, z, c):
    return x ^ near(c ^ (z & 1)), y, z, c


def gather_x2(x, y, z, c):
    return x ^ (4 - near(c ^ (z & 1))), y, z, c


def flip_y(x, y, z, c):
    return x, y ^ near(c), z, c


def pair_z(x, y, z, c):
    return x, y, (z ^ 1) if c == 0 else ((z + 1) % 8 if z % 2 else (z - 1) % 8), c


def x_1(x, y, z, c):
    return x ^ near(c), y, z, c


def x_2(x, y, z, c):
    return x ^ (4 - near(c)), y, z, c


def y_1(x, y, z, c):
    return x, y ^ near(c), z, c


def y_2(x, y, z, c):
    return x, y ^ (4 - near(c)), z, c


VM = pl.BlockSpec(memory_space=pltpu.VMEM)
SM = pl.BlockSpec(memory_space=pltpu.SMEM)


def dot(a, b, dims):
    return lax.dot_general(a, b, (dims, ((), ())), preferred_element_type=F32)


def where():
    x, y_lo, y_hi, z, c = (lax.axis_index(axis) for axis in AXES)
    return x, y_hi * 2 + y_lo, z, c


def aligned(start, size):
    return pl.ds(pl.multiple_of(start, size), size)


def norm_body(tokens, scale_r, own, send_low, send_high):
    full = tokens[...].astype(F32)
    r = lax.rsqrt(jnp.sum(full * full, axis=1, keepdims=True) * (1.0 / D) + 1e-05)
    scale_r[...] = r
    c = lax.axis_index("core")
    for b in range(8):
        here = slice(b * HALF, (b + 1) * HALF)
        for side in (c, 1 - c):
            part = (tokens[:, aligned(b * BLK + side * HALF, HALF)].astype(F32) * r).astype(BF16)
            if side is c:
                own[:, here] = part
            else:
                send_low[:, here] = part[: TOK // 2]
                send_high[:, here] = part[TOK // 2 :]


def norm(tokens):
    half = jax.ShapeDtypeStruct((TOK, D // 2), BF16)
    quarter = jax.ShapeDtypeStruct((TOK // 2, D // 2), BF16)
    return pl.pallas_call(
        norm_body,
        out_shape=(jax.ShapeDtypeStruct((TOK, 1), F32), half, quarter, quarter),
        in_specs=[VM],
        out_specs=(VM,) * 4,
        compiler_params=pltpu.CompilerParams(vmem_limit_bytes=12 << 20),
        cost_estimate=pl.CostEstimate(flops=10 * TOK * D, bytes_accessed=4 << 20, transcendentals=0),
        name="norm",
    )(tokens)


def transpose_body(own, low, high, out):
    for b in range(8):
        cols = slice(b * HALF, (b + 1) * HALF)
        out[cols, :TOK] = own[:, cols].T
        out[cols, TOK:] = jnp.concatenate([low[:, cols], high[:, cols]], axis=0).T


def transpose(own, low, high):
    return pl.pallas_call(
        transpose_body,
        out_shape=jax.ShapeDtypeStruct((D // 2, 2 * TOK), BF16),
        in_specs=[VM] * 3,
        out_specs=VM,
        compiler_params=pltpu.CompilerParams(vmem_limit_bytes=6 << 20),
        cost_estimate=pl.CostEstimate(flops=4 * TOK * D, bytes_accessed=4 << 20, transcendentals=0),
        name="transpose",
    )(own, low, high)


def block(name, flip):
    x, y, z, c = where()
    turned = c ^ (z & 1)
    step = {"0": 0, "a": 1 + 2 * turned, "b": 3 - 2 * turned, "o": 2}[name]
    return (x ^ step) * 2 + ((y & 1) ^ flip)


def product(spots, feats, pieces):
    cols = [aligned(block(*spot) * HALF, HALF) for spot in spots]
    lhs = jnp.concatenate([jnp.concatenate([ref[:, k] for k in cols], axis=1) for ref in feats], axis=0)
    return dot(lhs, jnp.concatenate([p[...] for p in pieces], axis=0), ((1,), (0,)))


def part_body(spots, own, low, high, *refs):
    count = len(spots)
    pieces, old, outs = refs[:count], refs[count:-2], refs[-2:]
    part = product(spots, (own, low, high), pieces)
    for k, half in enumerate((part[:TOK], part[TOK:])):
        outs[k][...] = half + old[k][...] if old else half


def project(spots, feats, pieces, *old):
    count, out = len(pieces), jax.ShapeDtypeStruct((TOK, QKV), F32)
    return pl.pallas_call(
        lambda *refs: part_body(spots, *refs),
        out_shape=(out, out),
        in_specs=[VM] * (3 + count + len(old)),
        out_specs=(VM, VM),
        compiler_params=pltpu.CompilerParams(vmem_limit_bytes=12 << 20),
        cost_estimate=pl.CostEstimate(
            flops=4 * TOK * HALF * count * QKV, bytes_accessed=6 << 20, transcendentals=0
        ),
        name="project",
    )(*feats, *pieces, *old)


def late_body(spots, count, *refs):
    feats, pieces, old, out = refs[:count], refs[count:-2], refs[-2], refs[-1]
    out[...] = (old[...] + product(spots, feats, pieces)).astype(out.dtype)


def project_late(spots, feats, pieces, old, dtype):
    count = len(feats)
    return pl.pallas_call(
        lambda *refs: late_body(spots, count, *refs),
        out_shape=jax.ShapeDtypeStruct((TOK, QKV), dtype),
        in_specs=[VM] * (1 + count + len(pieces)),
        out_specs=VM,
        compiler_params=pltpu.CompilerParams(vmem_limit_bytes=8 << 20),
        cost_estimate=pl.CostEstimate(
            flops=2 * TOK * HALF * len(pieces) * QKV, bytes_accessed=4 << 20, transcendentals=0
        ),
        name="project_late",
    )(*feats, *pieces, old)


def visible(doc):
    rows = lax.broadcasted_iota(jnp.int32, (TOK, TOK), 0)
    cols = lax.broadcasted_iota(jnp.int32, (TOK, TOK), 1)
    along = jnp.broadcast_to(doc[...], (TOK, TOK))
    return (cols <= rows) & (along == along.T)


def turn(value, cos, sin):
    return value * cos + pltpu.roll(value, HD // 2, 1) * sin


def head_grads(q_rot, g, k_rot, val, seen, cos, sin):
    scale = HD**-0.5
    scores = jnp.where(seen, dot(q_rot, k_rot, ((1,), (1,))), -1e30)
    expo = jnp.exp((scores - jnp.max(scores, axis=1, keepdims=True)) * scale)
    probs = expo * (1.0 / jnp.sum(expo, axis=1, keepdims=True))
    d_probs = dot(g, val, ((1,), (1,)))
    delta = jnp.sum(d_probs * probs, axis=1, keepdims=True)
    d_scores = (probs * (d_probs - delta)).astype(BF16)
    d_val = dot(probs.astype(BF16), g, ((0,), (0,)))
    d_key = dot(d_scores, q_rot, ((0,), (0,)))
    d_query = dot(d_scores, k_rot, ((1,), (0,))) * scale
    return turn(d_query, cos, -sin).astype(BF16), d_key, d_val


def attend_low_body(own, came, grad, doc, cosine, sine, out, rest, d_key, d_val, qkv):
    qkv[...] = own[...] + came[...].astype(F32)
    cos, sin = cosine[...], sine[...]
    seen = visible(doc)
    k_rot = turn(qkv[:, OUTW : OUTW + HD], cos, sin).astype(BF16)
    val = qkv[:, OUTW + HD :].astype(BF16)
    total_key, total_val = jnp.zeros((TOK, HD), F32), jnp.zeros((TOK, HD), F32)
    for h in range(QH):
        head = slice(h * HD, (h + 1) * HD)
        q_rot = turn(qkv[:, head], cos, sin).astype(BF16)
        if h < LOW:
            out[:, head], key, value = head_grads(q_rot, grad[:, head], k_rot, val, seen, cos, sin)
            total_key, total_val = total_key + key, total_val + value
        else:
            rest[:, (h - LOW) * HD : (h - LOW + 1) * HD] = q_rot
    rest[:, COLS - 2 * HD : COLS - HD] = k_rot
    rest[:, COLS - HD :] = val
    d_key[...] = total_key
    d_val[...] = total_val


def attend_high_body(rest, key_low, val_low, grad, doc, cosine, sine, out):
    cos, sin = cosine[...], sine[...]
    seen = visible(doc)
    k_rot, val = rest[:, COLS - 2 * HD : COLS - HD], rest[:, COLS - HD :]
    total_key, total_val = key_low[...], val_low[...]
    for h in range(LOW, QH):
        here = slice((h - LOW) * HD, (h - LOW + 1) * HD)
        g = grad[:, h * HD : (h + 1) * HD]
        out[:, here], key, value = head_grads(rest[:, here], g, k_rot, val, seen, cos, sin)
        total_key, total_val = total_key + key, total_val + value
    out[:, COLS - 2 * HD : COLS - HD] = turn(total_key * HD**-0.5, cos, -sin).astype(BF16)
    out[:, COLS - HD :] = total_val.astype(BF16)


def attend_cost(heads):
    return pl.CostEstimate(
        flops=10 * TOK * TOK * HD * heads, bytes_accessed=4 << 20, transcendentals=TOK * TOK * heads
    )


def attend_low(own, came, grad, doc):
    wide, half = jax.ShapeDtypeStruct((TOK, COLS), BF16), jax.ShapeDtypeStruct((TOK, HD), F32)
    return pl.pallas_call(
        attend_low_body,
        out_shape=(wide, wide, half, half),
        in_specs=[VM] * 6,
        out_specs=(VM,) * 4,
        scratch_shapes=[pltpu.VMEM((TOK, QKV), F32)],
        compiler_params=pltpu.CompilerParams(vmem_limit_bytes=12 << 20),
        cost_estimate=attend_cost(LOW),
        name="attend_low",
    )(own, came, grad, doc, *TABLES)


def attend_high(rest, d_key, d_val, grad, doc):
    return pl.pallas_call(
        attend_high_body,
        out_shape=jax.ShapeDtypeStruct((TOK, COLS), BF16),
        in_specs=[VM] * 7,
        out_specs=VM,
        compiler_params=pltpu.CompilerParams(vmem_limit_bytes=12 << 20),
        cost_estimate=attend_cost(QH - LOW),
        name="attend_high",
    )(rest, d_key, d_val, grad, doc, *TABLES)


def normed_body(spots, low, low_other, high, high_other, *refs):
    pieces, own, send = refs[: len(spots)], refs[-2], refs[-1]
    for lower, higher, out in ((low_other, high_other, send), (low, high, own)):
        d_qkv = jnp.concatenate([lower[...], higher[...]], axis=1)
        for spot, piece in zip(spots, pieces):
            part = dot(d_qkv, piece[...], ((1,), (1,)))
            out[:, aligned(block(*spot) * HALF, HALF)] = part.astype(out.dtype)


def normed_grad(spots, grads, pieces):
    count = len(pieces)
    return pl.pallas_call(
        lambda *refs: normed_body(spots, *refs),
        out_shape=(
            jax.ShapeDtypeStruct((TOK, D // 2), F32),
            jax.ShapeDtypeStruct((TOK, D // 2), BF16),
        ),
        in_specs=[VM] * (4 + count),
        out_specs=(VM, VM),
        compiler_params=pltpu.CompilerParams(vmem_limit_bytes=12 << 20),
        cost_estimate=pl.CostEstimate(flops=2 * TOK * D * QKV, bytes_accessed=8 << 20, transcendentals=0),
        name="normed_grad",
    )(*grads, *pieces)


def tokens_body(own, came, tokens, scale_r, out):
    c = lax.axis_index("core")
    places = [
        (aligned(b * BLK + side * HALF, HALF), ref, slice(b * HALF, (b + 1) * HALF))
        for b in range(8)
        for side, ref in ((c, own), (1 - c, came))
    ]
    total = jnp.zeros((TOK, HALF), F32)
    for cols, ref, here in places:
        total = total + ref[:, here].astype(F32) * tokens[:, cols].astype(F32)
    r = scale_r[...]
    back = r * r * r * (jnp.sum(total, axis=1, keepdims=True) * (1.0 / D))
    for cols, ref, here in places:
        out[:, cols] = (r * ref[:, here].astype(F32) - tokens[:, cols].astype(F32) * back).astype(BF16)


def tokens_grad(own, came, tokens, scale_r):
    return pl.pallas_call(
        tokens_body,
        out_shape=jax.ShapeDtypeStruct((TOK, D), BF16),
        in_specs=[VM] * 4,
        out_specs=VM,
        compiler_params=pltpu.CompilerParams(vmem_limit_bytes=8 << 20),
        cost_estimate=pl.CostEstimate(flops=10 * TOK * D, bytes_accessed=8 << 20, transcendentals=0),
        name="tokens_grad",
    )(own, came, tokens, scale_r)


def term_product(along_x, level, feats, d_own, d_other):
    x, y, z, c = where()
    order = (0, 3 - 2 * c, 1 + 2 * c, 2)
    rows = []
    for first in (2 * level, 2 * level + 1):
        for second in range(4):
            i, j = (first, second) if along_x else (second, first)
            yy = y ^ order[j]
            start = ((x ^ order[i]) * 2 + (yy & 1)) * HALF + (yy >> 1) * QUART
            rows.append(feats[aligned(start, QUART), :])
    right = jnp.concatenate([d_own[...], d_other[...]], axis=0)
    return dot(jnp.concatenate(rows, axis=0), right, ((1,), (0,))).reshape(8, QUART, COLS)


def term_body(along_x, feats, d_own, d_other, out):
    out[...] = term_product(along_x, 1, feats, d_own, d_other).astype(BF16)


def term_add_body(along_x, feats, d_own, d_other, came, kept, sent):
    part = term_product(along_x, 0, feats, d_own, d_other)
    part = (part + came[...].astype(F32)).astype(BF16)
    kept[...] = part[:4]
    sent[...] = part[4:]


def terms(along_x, made, *came):
    if came:
        half = jax.ShapeDtypeStruct((4, QUART, COLS), BF16)
        body, out_shape, out_specs = term_add_body, (half, half), (VM, VM)
    else:
        out_shape, out_specs = jax.ShapeDtypeStruct((8, QUART, COLS), BF16), VM
        body = term_body
    return pl.pallas_call(
        lambda *refs: body(along_x, *refs),
        out_shape=out_shape,
        in_specs=[VM] * (3 + len(came)),
        out_specs=out_specs,
        compiler_params=pltpu.CompilerParams(vmem_limit_bytes=12 << 20),
        cost_estimate=pl.CostEstimate(
            flops=2 * 8 * QUART * COLS * 2 * TOK, bytes_accessed=4 << 20, transcendentals=0
        ),
        name="terms",
    )(*made, *came)


def split_body(count, old, came, kept, sent):
    part = (old[...].astype(F32) + came[...].astype(F32)).astype(BF16)
    kept[...] = part[: count // 2]
    sent[...] = part[count // 2 :]


def split(old, came):
    count = old.shape[0]
    half = jax.ShapeDtypeStruct((count // 2, QUART, COLS), BF16)
    return pl.pallas_call(
        lambda *refs: split_body(count, *refs),
        out_shape=(half, half),
        in_specs=[VM, VM],
        out_specs=(VM, VM),
        compiler_params=pltpu.CompilerParams(vmem_limit_bytes=6 << 20),
        name="split",
    )(old, came)


def join_body(old_x, came_x, old_y, came_y, out):
    out[:, :, :COLS] = (old_x[...].astype(F32) + came_x[...].astype(F32)).astype(BF16).reshape(8, PIECE, COLS)
    out[:, :, COLS:] = (old_y[...].astype(F32) + came_y[...].astype(F32)).astype(BF16).reshape(8, PIECE, COLS)


def join(*parts):
    return pl.pallas_call(
        join_body,
        out_shape=jax.ShapeDtypeStruct((8, PIECE, QKV), BF16),
        in_specs=[VM] * 4,
        out_specs=VM,
        compiler_params=pltpu.CompilerParams(vmem_limit_bytes=4 << 20),
        name="join",
    )(*parts)


def finish_body(parts, out):
    total = sum(parts[i].astype(F32) for i in range(8)).astype(BF16)
    for i in range(16):
        out[i] = total


def finish(parts):
    return pl.pallas_call(
        finish_body,
        out_shape=jax.ShapeDtypeStruct((16, PIECE, QKV), BF16),
        in_specs=[VM],
        out_specs=VM,
        compiler_params=pltpu.CompilerParams(vmem_limit_bytes=4 << 20),
        name="finish",
    )(parts)


def squares_body(got, out):
    total = jnp.zeros((PIECE, QKV), F32)
    for i in range(16):
        value = got[i].astype(F32)
        total = total + value * value
    total = jnp.sum(jnp.sum(total, axis=1, keepdims=True), axis=0, keepdims=True)
    out[...] = jnp.broadcast_to(total.reshape(1, 1, 1), (16, 8, 128))


def squares(got):
    return pl.pallas_call(
        squares_body,
        out_shape=jax.ShapeDtypeStruct((16, 8, 128), F32),
        in_specs=[VM],
        out_specs=VM,
        compiler_params=pltpu.CompilerParams(vmem_limit_bytes=4 << 20),
        name="squares",
    )(got)


def rescale_body(parts, mine, theirs, out):
    total = sum(parts[i] for i in range(16))
    factor = (target_rms * lax.rsqrt(total * (1.0 / (D * QKV)) + 1e-06))[:1, :1]
    c = lax.axis_index("core")
    for side, half in ((c, mine), (1 - c, theirs)):
        out[aligned(side * HALF, HALF), :] = (half[...].reshape(HALF, QKV).astype(F32) * factor).astype(BF16)


def rescale(parts, mine, theirs):
    return pl.pallas_call(
        rescale_body,
        out_shape=jax.ShapeDtypeStruct((BLK, QKV), BF16),
        in_specs=[VM] * 3,
        out_specs=VM,
        compiler_params=pltpu.CompilerParams(vmem_limit_bytes=8 << 20),
        name="rescale",
    )(parts, mine, theirs)


def tables():
    freq = np.exp(-np.log(rope_base) * 2.0 * np.arange(HD // 2) / HD)
    angle = np.arange(TOK)[:, None] * freq[None, :]
    cos, sin = np.cos(angle), np.sin(angle)
    return np.concatenate([cos, cos], 1).astype(np.float32), np.concatenate([-sin, sin], 1).astype(np.float32)


TABLES = tables()

def on_device(tokens, grad_attended, doc_ids, w_own):
    w00 = lax.dynamic_slice_in_dim(w_own, lax.axis_index("core") * HALF, HALF, 0)
    w00, tokens = lax.optimization_barrier((w00, tokens))
    wa0 = swap(w00, gather_x1)
    w01 = swap(w00, flip_y)
    scale_r, own, send_low, send_high = norm(tokens)
    other = [swap(send, other_core) for send in (send_low, send_high)]
    wa0, w01, own, other = lax.optimization_barrier((wa0, w01, own, other))
    both = (own, *other)
    wo0 = swap(wa0, gather_x2)
    wa1 = swap(wa0, flip_y)
    wb0 = swap(wa0, pair_z)
    early, early_spots = [w00, w01, wa0], [("0", 0), ("0", 1), ("a", 0)]
    part_own, part_other = project(early_spots, both, early)
    feats = transpose(*both)
    wo0, wa1, part_own, part_other, feats = lax.optimization_barrier((wo0, wa1, part_own, part_other, feats))
    wo1 = swap(wo0, flip_y)
    wb1 = swap(wa1, pair_z)
    middle, middle_spots = [wo0, wa1, wb0], [("o", 0), ("a", 1), ("b", 0)]
    part_own, part_other = project(middle_spots, both, middle, part_own, part_other)
    wo1, wb1, part_own, part_other = lax.optimization_barrier((wo1, wb1, part_own, part_other))
    late, late_spots = [wo1, wb1], [("o", 1), ("b", 1)]
    late_other = project_late(late_spots, other, late, part_other, BF16)
    came = swap(late_other, other_core)
    late_other, part_own = lax.optimization_barrier((late_other, part_own))
    qkv = project_late(late_spots, [own], late, part_own, F32)
    d_low, rest, d_key, d_val = attend_low(qkv, came, grad_attended, doc_ids)

    low_other = swap(d_low, other_core)
    d_high = attend_high(rest, d_key, d_val, grad_attended, doc_ids)
    low_other, d_high = lax.optimization_barrier((low_other, d_high))
    high_other = swap(d_high, other_core)
    lows, highs = (feats, d_low, low_other), (feats, d_high, high_other)
    came_x = swap(terms(True, lows), x_1)
    sent_y = terms(False, highs)
    came_y = swap(sent_y, y_1)
    spots, pieces = early_spots + middle_spots + late_spots, early + middle + late
    sent_y, d_low, low_other, d_high, high_other = lax.optimization_barrier(
        (sent_y, d_low, low_other, d_high, high_other)
    )
    normed_own, normed_send = normed_grad(spots, (d_low, low_other, d_high, high_other), pieces)
    normed_came = swap(normed_send, other_core)
    came_x, normed_own = lax.optimization_barrier((came_x, normed_own))
    sum_x, sent_x = terms(True, lows, came_x)
    came_x = swap(sent_x, x_2)
    sum_y, sent_y = terms(False, highs, came_y)
    came_y = swap(sent_y, y_2)
    sent_y, normed_came = lax.optimization_barrier((sent_y, normed_came))
    d_tokens = tokens_grad(normed_own, normed_came, tokens, scale_r)
    came_x, d_tokens = lax.optimization_barrier((came_x, d_tokens))
    for step_x, step_y in ((y_1, x_1), (y_2, x_2)):
        sum_x, sent_x = split(sum_x, came_x)
        came_x = swap(sent_x, step_x)
        sum_y, sent_y = split(sum_y, came_y)
        came_y = swap(sent_y, step_y)

    total = join(sum_x, came_x, sum_y, came_y)
    got = finish(lax.all_to_all(total, "z", 0, 0))
    got = lax.all_to_all(got, ("y_hi", "z"), 0, 0)

    theirs = swap(got, other_core)
    parts = lax.all_to_all(squares(got), ("x", "y_lo", "core"), 0, 0)
    return d_tokens, rescale(parts, got, theirs)


def solution(mesh):
    mesh = Mesh(mesh.devices.reshape(SIZES), AXES)
    spread, rows = P(AXES, None), P(AXES[:2], None)
    return jax.shard_map(
        on_device,
        mesh=mesh,
        in_specs=(spread, spread, spread, rows),
        out_specs=(spread, rows),
        check_vma=False,
    )
```

```python
import jax
import jax.numpy as jnp
import numpy as np
from jax import lax
from jax.experimental import pallas as pl
from jax.experimental.pallas import tpu as pltpu
from jax.sharding import Mesh
from jax.sharding import PartitionSpec as P

D = 4096
HD = 128
QH = 8
QKV = 1280
TOK = 256
BLK = D // 8
HALF = BLK // 2
QUART = HALF // 2
PIECE = QUART // 8
COLS = QKV // 2
OUTW = QH * HD
LOW = COLS // HD

AXES = ("x", "y_lo", "y_hi", "z", "core")
SIZES = (4, 2, 2, 8, 2)
target_rms = 0.5
rope_base = 500000.0
F32 = jnp.float32
BF16 = jnp.bfloat16


def flat(x, y, z, c):
    return (x * 2 + y % 2) * 32 + (y // 2) * 16 + z * 2 + c


def swap(value, partner):
    pairs = []
    for x in range(4):
        for y in range(4):
            for z in range(8):
                for c in range(2):
                    pairs.append((flat(x, y, z, c), flat(*partner(x, y, z, c))))
    return lax.ppermute(value, AXES, pairs)


def near(c):
    return 1 if c == 0 else 3


def other_core(x, y, z, c):
    return x, y, z, 1 - c


def gather_x1(x, y, z, c):
    return x ^ near(c ^ (z & 1)), y, z, c


def gather_x2(x, y, z, c):
    return x ^ (4 - near(c ^ (z & 1))), y, z, c


def flip_y(x, y, z, c):
    return x, y ^ near(c), z, c


def pair_z(x, y, z, c):
    return x, y, (z ^ 1) if c == 0 else ((z + 1) % 8 if z % 2 else (z - 1) % 8), c


def x_1(x, y, z, c):
    return x ^ near(c), y, z, c


def x_2(x, y, z, c):
    return x ^ (4 - near(c)), y, z, c


def y_1(x, y, z, c):
    return x, y ^ near(c), z, c


def y_2(x, y, z, c):
    return x, y ^ (4 - near(c)), z, c


VM = pl.BlockSpec(memory_space=pltpu.VMEM)
SM = pl.BlockSpec(memory_space=pltpu.SMEM)


def dot(a, b, dims):
    return lax.dot_general(a, b, (dims, ((), ())), preferred_element_type=F32)


def where():
    x, y_lo, y_hi, z, c = (lax.axis_index(axis) for axis in AXES)
    return x, y_hi * 2 + y_lo, z, c


def aligned(start, size):
    return pl.ds(pl.multiple_of(start, size), size)


def norm_body(tokens, scale_r, own, send_low, send_high):
    full = tokens[...].astype(F32)
    r = lax.rsqrt(jnp.sum(full * full, axis=1, keepdims=True) * (1.0 / D) + 1e-05)
    scale_r[...] = r
    c = lax.axis_index("core")
    for b in range(8):
        here = slice(b * HALF, (b + 1) * HALF)
        for side in (c, 1 - c):
            part = (tokens[:, aligned(b * BLK + side * HALF, HALF)].astype(F32) * r).astype(BF16)
            if side is c:
                own[:, here] = part
            else:
                send_low[:, here] = part[: TOK // 2]
                send_high[:, here] = part[TOK // 2 :]


def norm(tokens):
    half = jax.ShapeDtypeStruct((TOK, D // 2), BF16)
    quarter = jax.ShapeDtypeStruct((TOK // 2, D // 2), BF16)
    return pl.pallas_call(
        norm_body,
        out_shape=(jax.ShapeDtypeStruct((TOK, 1), F32), half, quarter, quarter),
        in_specs=[VM],
        out_specs=(VM,) * 4,
        compiler_params=pltpu.CompilerParams(vmem_limit_bytes=12 << 20),
        cost_estimate=pl.CostEstimate(flops=10 * TOK * D, bytes_accessed=4 << 20, transcendentals=0),
        name="norm",
    )(tokens)


def transpose_body(own, low, high, out):
    for b in range(8):
        cols = slice(b * HALF, (b + 1) * HALF)
        out[cols, :TOK] = own[:, cols].T
        out[cols, TOK:] = jnp.concatenate([low[:, cols], high[:, cols]], axis=0).T


def transpose(own, low, high):
    return pl.pallas_call(
        transpose_body,
        out_shape=jax.ShapeDtypeStruct((D // 2, 2 * TOK), BF16),
        in_specs=[VM] * 3,
        out_specs=VM,
        compiler_params=pltpu.CompilerParams(vmem_limit_bytes=6 << 20),
        cost_estimate=pl.CostEstimate(flops=4 * TOK * D, bytes_accessed=4 << 20, transcendentals=0),
        name="transpose",
    )(own, low, high)


def block(name, flip):
    x, y, z, c = where()
    turned = c ^ (z & 1)
    step = {"0": 0, "a": 1 + 2 * turned, "b": 3 - 2 * turned, "o": 2}[name]
    return (x ^ step) * 2 + ((y & 1) ^ flip)


def product(spots, feats, pieces):
    cols = [aligned(block(*spot) * HALF, HALF) for spot in spots]
    lhs = jnp.concatenate([jnp.concatenate([ref[:, k] for k in cols], axis=1) for ref in feats], axis=0)
    return dot(lhs, jnp.concatenate([p[...] for p in pieces], axis=0), ((1,), (0,)))


def part_body(spots, own, low, high, *refs):
    count = len(spots)
    pieces, old, outs = refs[:count], refs[count:-2], refs[-2:]
    part = product(spots, (own, low, high), pieces)
    for k, half in enumerate((part[:TOK], part[TOK:])):
        outs[k][...] = half + old[k][...] if old else half


def project(spots, feats, pieces, *old):
    count, out = len(pieces), jax.ShapeDtypeStruct((TOK, QKV), F32)
    return pl.pallas_call(
        lambda *refs: part_body(spots, *refs),
        out_shape=(out, out),
        in_specs=[VM] * (3 + count + len(old)),
        out_specs=(VM, VM),
        compiler_params=pltpu.CompilerParams(vmem_limit_bytes=12 << 20),
        cost_estimate=pl.CostEstimate(
            flops=4 * TOK * HALF * count * QKV, bytes_accessed=6 << 20, transcendentals=0
        ),
        name="project",
    )(*feats, *pieces, *old)


def late_body(spots, count, *refs):
    feats, pieces, old, out = refs[:count], refs[count:-2], refs[-2], refs[-1]
    out[...] = (old[...] + product(spots, feats, pieces)).astype(out.dtype)


def project_late(spots, feats, pieces, old, dtype):
    count = len(feats)
    return pl.pallas_call(
        lambda *refs: late_body(spots, count, *refs),
        out_shape=jax.ShapeDtypeStruct((TOK, QKV), dtype),
        in_specs=[VM] * (1 + count + len(pieces)),
        out_specs=VM,
        compiler_params=pltpu.CompilerParams(vmem_limit_bytes=8 << 20),
        cost_estimate=pl.CostEstimate(
            flops=2 * TOK * HALF * len(pieces) * QKV, bytes_accessed=4 << 20, transcendentals=0
        ),
        name="project_late",
    )(*feats, *pieces, old)


def visible(doc):
    rows = lax.broadcasted_iota(jnp.int32, (TOK, TOK), 0)
    cols = lax.broadcasted_iota(jnp.int32, (TOK, TOK), 1)
    along = jnp.broadcast_to(doc[...], (TOK, TOK))
    return (cols <= rows) & (along == along.T)


def turn(value, cos, sin):
    return value * cos + pltpu.roll(value, HD // 2, 1) * sin


def head_grads(q_rot, g, k_rot, val, seen, count):
    scale = HD**-0.5
    scores = dot(q_rot, k_rot, ((1,), (1,))).reshape(count, TOK, TOK)
    scores = jnp.where(seen[None], scores, -1e30)
    expo = jnp.exp((scores - jnp.max(scores, axis=2, keepdims=True)) * scale)
    probs = expo * (1.0 / jnp.sum(expo, axis=2, keepdims=True))
    d_probs = dot(g, val, ((1,), (1,))).reshape(count, TOK, TOK)
    delta = jnp.sum(d_probs * probs, axis=2, keepdims=True)
    d_scores = (probs * (d_probs - delta)).astype(BF16).reshape(count * TOK, TOK)
    probs = probs.astype(BF16).reshape(count * TOK, TOK)
    d_val = dot(probs, g, ((0,), (0,)))
    d_key = dot(d_scores, q_rot, ((0,), (0,)))
    return dot(d_scores, k_rot, ((1,), (0,))) * scale, d_key, d_val


def attend_low_body(own, came, grad, doc, cosine, sine, out, rest, d_key, d_val, qkv):
    qkv[...] = own[...] + came[...].astype(F32)
    cos, sin = cosine[...], sine[...]
    seen = visible(doc)
    k_rot = turn(qkv[:, OUTW : OUTW + HD], cos, sin).astype(BF16)
    val = qkv[:, OUTW + HD :].astype(BF16)
    q_rot = [turn(qkv[:, h * HD : (h + 1) * HD], cos, sin).astype(BF16) for h in range(QH)]
    g = jnp.concatenate([grad[:, h * HD : (h + 1) * HD] for h in range(LOW)], axis=0)
    stacked = jnp.concatenate(q_rot[:LOW], axis=0)
    d_query, d_key[...], d_val[...] = head_grads(stacked, g, k_rot, val, seen, LOW)
    for h in range(LOW):
        out[:, h * HD : (h + 1) * HD] = turn(d_query[h * TOK : (h + 1) * TOK], cos, -sin).astype(BF16)
    for h in range(LOW, QH):
        rest[:, (h - LOW) * HD : (h - LOW + 1) * HD] = q_rot[h]
    rest[:, COLS - 2 * HD : COLS - HD] = k_rot
    rest[:, COLS - HD :] = val


def attend_high_body(rest, key_low, val_low, grad, doc, cosine, sine, out):
    cos, sin = cosine[...], sine[...]
    k_rot, val = rest[:, COLS - 2 * HD : COLS - HD], rest[:, COLS - HD :]
    count = QH - LOW
    g = jnp.concatenate([grad[:, h * HD : (h + 1) * HD] for h in range(LOW, QH)], axis=0)
    stacked = jnp.concatenate([rest[:, k * HD : (k + 1) * HD] for k in range(count)], axis=0)
    d_query, key, value = head_grads(stacked, g, k_rot, val, visible(doc), count)
    for k in range(count):
        out[:, k * HD : (k + 1) * HD] = turn(d_query[k * TOK : (k + 1) * TOK], cos, -sin).astype(BF16)
    total_key = (key_low[...] + key) * HD**-0.5
    out[:, COLS - 2 * HD : COLS - HD] = turn(total_key, cos, -sin).astype(BF16)
    out[:, COLS - HD :] = (val_low[...] + value).astype(BF16)


def attend_cost(heads):
    return pl.CostEstimate(
        flops=10 * TOK * TOK * HD * heads, bytes_accessed=4 << 20, transcendentals=TOK * TOK * heads
    )


def attend_low(own, came, grad, doc):
    wide, half = jax.ShapeDtypeStruct((TOK, COLS), BF16), jax.ShapeDtypeStruct((TOK, HD), F32)
    return pl.pallas_call(
        attend_low_body,
        out_shape=(wide, wide, half, half),
        in_specs=[VM] * 6,
        out_specs=(VM,) * 4,
        scratch_shapes=[pltpu.VMEM((TOK, QKV), F32)],
        compiler_params=pltpu.CompilerParams(vmem_limit_bytes=12 << 20),
        cost_estimate=attend_cost(LOW),
        name="attend_low",
    )(own, came, grad, doc, *TABLES)


def attend_high(rest, d_key, d_val, grad, doc):
    return pl.pallas_call(
        attend_high_body,
        out_shape=jax.ShapeDtypeStruct((TOK, COLS), BF16),
        in_specs=[VM] * 7,
        out_specs=VM,
        compiler_params=pltpu.CompilerParams(vmem_limit_bytes=12 << 20),
        cost_estimate=attend_cost(QH - LOW),
        name="attend_high",
    )(rest, d_key, d_val, grad, doc, *TABLES)


def normed_body(spots, low, low_other, high, high_other, *refs):
    pieces, own, send = refs[: len(spots)], refs[-2], refs[-1]
    for lower, higher, out in ((low_other, high_other, send), (low, high, own)):
        d_qkv = jnp.concatenate([lower[...], higher[...]], axis=1)
        for spot, piece in zip(spots, pieces):
            part = dot(d_qkv, piece[...], ((1,), (1,)))
            out[:, aligned(block(*spot) * HALF, HALF)] = part.astype(out.dtype)


def normed_grad(spots, grads, pieces):
    count = len(pieces)
    return pl.pallas_call(
        lambda *refs: normed_body(spots, *refs),
        out_shape=(
            jax.ShapeDtypeStruct((TOK, D // 2), F32),
            jax.ShapeDtypeStruct((TOK, D // 2), BF16),
        ),
        in_specs=[VM] * (4 + count),
        out_specs=(VM, VM),
        compiler_params=pltpu.CompilerParams(vmem_limit_bytes=12 << 20),
        cost_estimate=pl.CostEstimate(flops=2 * TOK * D * QKV, bytes_accessed=8 << 20, transcendentals=0),
        name="normed_grad",
    )(*grads, *pieces)


def tokens_body(own, came, tokens, scale_r, out):
    c = lax.axis_index("core")
    places = [
        (aligned(b * BLK + side * HALF, HALF), ref, slice(b * HALF, (b + 1) * HALF))
        for b in range(8)
        for side, ref in ((c, own), (1 - c, came))
    ]
    total = jnp.zeros((TOK, HALF), F32)
    for cols, ref, here in places:
        total = total + ref[:, here].astype(F32) * tokens[:, cols].astype(F32)
    r = scale_r[...]
    back = r * r * r * (jnp.sum(total, axis=1, keepdims=True) * (1.0 / D))
    for cols, ref, here in places:
        out[:, cols] = (r * ref[:, here].astype(F32) - tokens[:, cols].astype(F32) * back).astype(BF16)


def tokens_grad(own, came, tokens, scale_r):
    return pl.pallas_call(
        tokens_body,
        out_shape=jax.ShapeDtypeStruct((TOK, D), BF16),
        in_specs=[VM] * 4,
        out_specs=VM,
        compiler_params=pltpu.CompilerParams(vmem_limit_bytes=8 << 20),
        cost_estimate=pl.CostEstimate(flops=10 * TOK * D, bytes_accessed=8 << 20, transcendentals=0),
        name="tokens_grad",
    )(own, came, tokens, scale_r)


def term_product(along_x, level, feats, d_own, d_other):
    x, y, z, c = where()
    order = (0, 3 - 2 * c, 1 + 2 * c, 2)
    rows = []
    for first in (2 * level, 2 * level + 1):
        for second in range(4):
            i, j = (first, second) if along_x else (second, first)
            yy = y ^ order[j]
            start = ((x ^ order[i]) * 2 + (yy & 1)) * HALF + (yy >> 1) * QUART
            rows.append(feats[aligned(start, QUART), :])
    right = jnp.concatenate([d_own[...], d_other[...]], axis=0)
    return dot(jnp.concatenate(rows, axis=0), right, ((1,), (0,))).reshape(8, QUART, COLS)


def term_body(along_x, level, feats, d_own, d_other, out):
    out[...] = term_product(along_x, level, feats, d_own, d_other).astype(BF16)


def terms(along_x, level, made):
    return pl.pallas_call(
        lambda *refs: term_body(along_x, level, *refs),
        out_shape=jax.ShapeDtypeStruct((8, QUART, COLS), BF16),
        in_specs=[VM] * 3,
        out_specs=VM,
        compiler_params=pltpu.CompilerParams(vmem_limit_bytes=12 << 20),
        cost_estimate=pl.CostEstimate(
            flops=2 * 8 * QUART * COLS * 2 * TOK, bytes_accessed=4 << 20, transcendentals=0
        ),
        name="terms",
    )(*made)


def split_body(count, old, came, kept, sent):
    part = (old[...].astype(F32) + came[...].astype(F32)).astype(BF16)
    kept[...] = part[: count // 2]
    sent[...] = part[count // 2 :]


def split(old, came):
    count = old.shape[0]
    half = jax.ShapeDtypeStruct((count // 2, QUART, COLS), BF16)
    return pl.pallas_call(
        lambda *refs: split_body(count, *refs),
        out_shape=(half, half),
        in_specs=[VM, VM],
        out_specs=(VM, VM),
        compiler_params=pltpu.CompilerParams(vmem_limit_bytes=6 << 20),
        name="split",
    )(old, came)


def join_body(old_x, came_x, old_y, came_y, out):
    out[:, :, :COLS] = (old_x[...].astype(F32) + came_x[...].astype(F32)).astype(BF16).reshape(8, PIECE, COLS)
    out[:, :, COLS:] = (old_y[...].astype(F32) + came_y[...].astype(F32)).astype(BF16).reshape(8, PIECE, COLS)


def join(*parts):
    return pl.pallas_call(
        join_body,
        out_shape=jax.ShapeDtypeStruct((8, PIECE, QKV), BF16),
        in_specs=[VM] * 4,
        out_specs=VM,
        compiler_params=pltpu.CompilerParams(vmem_limit_bytes=4 << 20),
        name="join",
    )(*parts)


def finish_body(parts, out):
    total = sum(parts[i].astype(F32) for i in range(8)).astype(BF16)
    for i in range(16):
        out[i] = total


def finish(parts):
    return pl.pallas_call(
        finish_body,
        out_shape=jax.ShapeDtypeStruct((16, PIECE, QKV), BF16),
        in_specs=[VM],
        out_specs=VM,
        compiler_params=pltpu.CompilerParams(vmem_limit_bytes=4 << 20),
        name="finish",
    )(parts)


def squares_body(got, out):
    total = jnp.zeros((PIECE, QKV), F32)
    for i in range(16):
        value = got[i].astype(F32)
        total = total + value * value
    total = jnp.sum(jnp.sum(total, axis=1, keepdims=True), axis=0, keepdims=True)
    out[...] = jnp.broadcast_to(total.reshape(1, 1, 1), (16, 8, 128))


def squares(got):
    return pl.pallas_call(
        squares_body,
        out_shape=jax.ShapeDtypeStruct((16, 8, 128), F32),
        in_specs=[VM],
        out_specs=VM,
        compiler_params=pltpu.CompilerParams(vmem_limit_bytes=4 << 20),
        name="squares",
    )(got)


def rescale_body(parts, mine, theirs, out):
    total = sum(parts[i] for i in range(16))
    factor = (target_rms * lax.rsqrt(total * (1.0 / (D * QKV)) + 1e-06))[:1, :1]
    c = lax.axis_index("core")
    for side, half in ((c, mine), (1 - c, theirs)):
        out[aligned(side * HALF, HALF), :] = (half[...].reshape(HALF, QKV).astype(F32) * factor).astype(BF16)


def rescale(parts, mine, theirs):
    return pl.pallas_call(
        rescale_body,
        out_shape=jax.ShapeDtypeStruct((BLK, QKV), BF16),
        in_specs=[VM] * 3,
        out_specs=VM,
        compiler_params=pltpu.CompilerParams(vmem_limit_bytes=8 << 20),
        name="rescale",
    )(parts, mine, theirs)


def tables():
    freq = np.exp(-np.log(rope_base) * 2.0 * np.arange(HD // 2) / HD)
    angle = np.arange(TOK)[:, None] * freq[None, :]
    cos, sin = np.cos(angle), np.sin(angle)
    return np.concatenate([cos, cos], 1).astype(np.float32), np.concatenate([-sin, sin], 1).astype(np.float32)


TABLES = tables()

def on_device(tokens, grad_attended, doc_ids, w_own):
    w00 = lax.dynamic_slice_in_dim(w_own, lax.axis_index("core") * HALF, HALF, 0)
    w00, tokens = lax.optimization_barrier((w00, tokens))
    wa0 = swap(w00, gather_x1)
    w01 = swap(w00, flip_y)
    scale_r, own, send_low, send_high = norm(tokens)
    other = [swap(send, other_core) for send in (send_low, send_high)]
    wa0, w01, own, other = lax.optimization_barrier((wa0, w01, own, other))
    both = (own, *other)
    wo0 = swap(wa0, gather_x2)
    wa1 = swap(wa0, flip_y)
    wb0 = swap(wa0, pair_z)
    early, early_spots = [w00, w01, wa0], [("0", 0), ("0", 1), ("a", 0)]
    part_own, part_other = project(early_spots, both, early)
    feats = transpose(*both)
    wo0, wa1, part_own, part_other, feats = lax.optimization_barrier((wo0, wa1, part_own, part_other, feats))
    wo1 = swap(wo0, flip_y)
    wb1 = swap(wa1, pair_z)
    middle, middle_spots = [wo0, wa1, wb0], [("o", 0), ("a", 1), ("b", 0)]
    part_own, part_other = project(middle_spots, both, middle, part_own, part_other)
    wo1, wb1, part_own, part_other = lax.optimization_barrier((wo1, wb1, part_own, part_other))
    late, late_spots = [wo1, wb1], [("o", 1), ("b", 1)]
    late_other = project_late(late_spots, other, late, part_other, BF16)
    came = swap(late_other, other_core)
    late_other, part_own = lax.optimization_barrier((late_other, part_own))
    qkv = project_late(late_spots, [own], late, part_own, F32)
    d_low, rest, d_key, d_val = attend_low(qkv, came, grad_attended, doc_ids)

    low_other = swap(d_low, other_core)
    d_high = attend_high(rest, d_key, d_val, grad_attended, doc_ids)
    low_other, d_high = lax.optimization_barrier((low_other, d_high))
    high_other = swap(d_high, other_core)
    lows, highs = (feats, d_low, low_other), (feats, d_high, high_other)
    came_x = swap(terms(True, 1, lows), x_1)
    sent_y = terms(False, 1, highs)
    came_y = swap(sent_y, y_1)
    spots, pieces = early_spots + middle_spots + late_spots, early + middle + late
    sent_y, lows, highs = lax.optimization_barrier((sent_y, lows, highs))
    sum_x, sum_y = terms(True, 0, lows), terms(False, 0, highs)
    normed_own, normed_send = normed_grad(spots, (*lows[1:], *highs[1:]), pieces)
    normed_came = swap(normed_send, other_core)
    came_x, sum_x, sum_y, normed_own = lax.optimization_barrier((came_x, sum_x, sum_y, normed_own))
    sum_x, sent_x = split(sum_x, came_x)
    came_x = swap(sent_x, x_2)
    sum_y, sent_y = split(sum_y, came_y)
    came_y = swap(sent_y, y_2)
    sent_y, normed_came = lax.optimization_barrier((sent_y, normed_came))
    d_tokens = tokens_grad(normed_own, normed_came, tokens, scale_r)
    came_x, d_tokens = lax.optimization_barrier((came_x, d_tokens))
    for step_x, step_y in ((y_1, x_1), (y_2, x_2)):
        sum_x, sent_x = split(sum_x, came_x)
        came_x = swap(sent_x, step_x)
        sum_y, sent_y = split(sum_y, came_y)
        came_y = swap(sent_y, step_y)

    total = join(sum_x, came_x, sum_y, came_y)
    got = finish(lax.all_to_all(total, "z", 0, 0))
    got = lax.all_to_all(got, ("y_hi", "z"), 0, 0)

    theirs = swap(got, other_core)
    parts = lax.all_to_all(squares(got), ("x", "y_lo", "core"), 0, 0)
    return d_tokens, rescale(parts, got, theirs)


def solution(mesh):
    mesh = Mesh(mesh.devices.reshape(SIZES), AXES)
    spread, rows = P(AXES, None), P(AXES[:2], None)
    return jax.shard_map(
        on_device,
        mesh=mesh,
        in_specs=(spread, spread, spread, rows),
        out_specs=(spread, rows),
        check_vma=False,
    )
```

```python
import jax
import jax.numpy as jnp
import numpy as np
from jax import lax
from jax.experimental import pallas as pl
from jax.experimental.pallas import tpu as pltpu
from jax.sharding import Mesh
from jax.sharding import PartitionSpec as P

D = 4096
HD = 128
QH = 8
QKV = 1280
TOK = 256
BLK = D // 8
HALF = BLK // 2
QUART = HALF // 2
PIECE = QUART // 8
COLS = QKV // 2
OUTW = QH * HD
LOW = COLS // HD

AXES = ("x", "y_lo", "y_hi", "z", "core")
SIZES = (4, 2, 2, 8, 2)
target_rms = 0.5
rope_base = 500000.0
F32 = jnp.float32
BF16 = jnp.bfloat16


def flat(x, y, z, c):
    return (x * 2 + y % 2) * 32 + (y // 2) * 16 + z * 2 + c


def swap(value, partner):
    pairs = []
    for x in range(4):
        for y in range(4):
            for z in range(8):
                for c in range(2):
                    pairs.append((flat(x, y, z, c), flat(*partner(x, y, z, c))))
    return lax.ppermute(value, AXES, pairs)


def near(c):
    return 1 if c == 0 else 3


def other_core(x, y, z, c):
    return x, y, z, 1 - c


def gather_x1(x, y, z, c):
    return x ^ near(c ^ (z & 1)), y, z, c


def gather_x2(x, y, z, c):
    return x ^ (4 - near(c ^ (z & 1))), y, z, c


def flip_y(x, y, z, c):
    return x, y ^ near(c), z, c


def pair_z(x, y, z, c):
    return x, y, (z ^ 1) if c == 0 else ((z + 1) % 8 if z % 2 else (z - 1) % 8), c


def x_1(x, y, z, c):
    return x ^ near(c), y, z, c


def x_2(x, y, z, c):
    return x ^ (4 - near(c)), y, z, c


def y_1(x, y, z, c):
    return x, y ^ near(c), z, c


def y_2(x, y, z, c):
    return x, y ^ (4 - near(c)), z, c


VM = pl.BlockSpec(memory_space=pltpu.VMEM)
SM = pl.BlockSpec(memory_space=pltpu.SMEM)


def dot(a, b, dims):
    return lax.dot_general(a, b, (dims, ((), ())), preferred_element_type=F32)


def where():
    x, y_lo, y_hi, z, c = (lax.axis_index(axis) for axis in AXES)
    return x, y_hi * 2 + y_lo, z, c


def aligned(start, size):
    return pl.ds(pl.multiple_of(start, size), size)


def norm_body(tokens, scale_r, own, send_low, send_high):
    full = tokens[...].astype(F32)
    r = lax.rsqrt(jnp.sum(full * full, axis=1, keepdims=True) * (1.0 / D) + 1e-05)
    scale_r[...] = r
    c = lax.axis_index("core")
    for b in range(8):
        here = slice(b * HALF, (b + 1) * HALF)
        for side in (c, 1 - c):
            part = (tokens[:, aligned(b * BLK + side * HALF, HALF)].astype(F32) * r).astype(BF16)
            if side is c:
                own[:, here] = part
            else:
                send_low[:, here] = part[: TOK // 2]
                send_high[:, here] = part[TOK // 2 :]


def norm(tokens):
    half = jax.ShapeDtypeStruct((TOK, D // 2), BF16)
    quarter = jax.ShapeDtypeStruct((TOK // 2, D // 2), BF16)
    return pl.pallas_call(
        norm_body,
        out_shape=(jax.ShapeDtypeStruct((TOK, 1), F32), half, quarter, quarter),
        in_specs=[VM],
        out_specs=(VM,) * 4,
        compiler_params=pltpu.CompilerParams(vmem_limit_bytes=12 << 20),
        cost_estimate=pl.CostEstimate(flops=10 * TOK * D, bytes_accessed=4 << 20, transcendentals=0),
        name="norm",
    )(tokens)


def transpose_body(own, low, high, out):
    for b in range(8):
        cols = slice(b * HALF, (b + 1) * HALF)
        out[cols, :TOK] = own[:, cols].T
        out[cols, TOK:] = jnp.concatenate([low[:, cols], high[:, cols]], axis=0).T


def transpose(own, low, high):
    return pl.pallas_call(
        transpose_body,
        out_shape=jax.ShapeDtypeStruct((D // 2, 2 * TOK), BF16),
        in_specs=[VM] * 3,
        out_specs=VM,
        compiler_params=pltpu.CompilerParams(vmem_limit_bytes=6 << 20),
        cost_estimate=pl.CostEstimate(flops=4 * TOK * D, bytes_accessed=4 << 20, transcendentals=0),
        name="transpose",
    )(own, low, high)


def block(name, flip):
    x, y, z, c = where()
    turned = c ^ (z & 1)
    step = {"0": 0, "a": 1 + 2 * turned, "b": 3 - 2 * turned, "o": 2}[name]
    return (x ^ step) * 2 + ((y & 1) ^ flip)


def product(spots, feats, pieces):
    cols = [aligned(block(*spot) * HALF, HALF) for spot in spots]
    lhs = jnp.concatenate([jnp.concatenate([ref[:, k] for k in cols], axis=1) for ref in feats], axis=0)
    return dot(lhs, jnp.concatenate([p[...] for p in pieces], axis=0), ((1,), (0,)))


def part_body(spots, own, low, high, *refs):
    count = len(spots)
    pieces, old, outs = refs[:count], refs[count:-2], refs[-2:]
    part = product(spots, (own, low, high), pieces)
    for k, half in enumerate((part[:TOK], part[TOK:])):
        outs[k][...] = half + old[k][...] if old else half


def project(spots, feats, pieces, *old):
    count, out = len(pieces), jax.ShapeDtypeStruct((TOK, QKV), F32)
    return pl.pallas_call(
        lambda *refs: part_body(spots, *refs),
        out_shape=(out, out),
        in_specs=[VM] * (3 + count + len(old)),
        out_specs=(VM, VM),
        compiler_params=pltpu.CompilerParams(vmem_limit_bytes=12 << 20),
        cost_estimate=pl.CostEstimate(
            flops=4 * TOK * HALF * count * QKV, bytes_accessed=6 << 20, transcendentals=0
        ),
        name="project",
    )(*feats, *pieces, *old)


def late_body(spots, count, *refs):
    feats, pieces, old, out = refs[:count], refs[count:-2], refs[-2], refs[-1]
    out[...] = (old[...] + product(spots, feats, pieces)).astype(out.dtype)


def project_late(spots, feats, pieces, old, dtype):
    count = len(feats)
    return pl.pallas_call(
        lambda *refs: late_body(spots, count, *refs),
        out_shape=jax.ShapeDtypeStruct((TOK, QKV), dtype),
        in_specs=[VM] * (1 + count + len(pieces)),
        out_specs=VM,
        compiler_params=pltpu.CompilerParams(vmem_limit_bytes=8 << 20),
        cost_estimate=pl.CostEstimate(
            flops=2 * TOK * HALF * len(pieces) * QKV, bytes_accessed=4 << 20, transcendentals=0
        ),
        name="project_late",
    )(*feats, *pieces, old)


def visible(doc):
    rows = lax.broadcasted_iota(jnp.int32, (TOK, TOK), 0)
    cols = lax.broadcasted_iota(jnp.int32, (TOK, TOK), 1)
    along = jnp.broadcast_to(doc[...], (TOK, TOK))
    return (cols <= rows) & (along == along.T)


def turn(value, cos, sin):
    return value * cos + pltpu.roll(value, HD // 2, 1) * sin


def head_grads(q_rot, g, k_rot, val, seen, count):
    scale = HD**-0.5
    scores = dot(q_rot, k_rot, ((1,), (1,))).reshape(count, TOK, TOK)
    scores = jnp.where(seen[None], scores, -1e30)
    expo = jnp.exp((scores - jnp.max(scores, axis=2, keepdims=True)) * scale)
    probs = expo * (1.0 / jnp.sum(expo, axis=2, keepdims=True))
    d_probs = dot(g, val, ((1,), (1,))).reshape(count, TOK, TOK)
    delta = jnp.sum(d_probs * probs, axis=2, keepdims=True)
    d_scores = (probs * (d_probs - delta)).astype(BF16).reshape(count * TOK, TOK)
    probs = probs.astype(BF16).reshape(count * TOK, TOK)
    d_val = dot(probs, g, ((0,), (0,)))
    d_key = dot(d_scores, q_rot, ((0,), (0,)))
    return dot(d_scores, k_rot, ((1,), (0,))) * scale, d_key, d_val


def attend_low_body(own, came, grad, doc, cosine, sine, out, rest, d_key, d_val, qkv):
    qkv[...] = own[...] + came[...].astype(F32)
    cos, sin = cosine[...], sine[...]
    seen = visible(doc)
    k_rot = turn(qkv[:, OUTW : OUTW + HD], cos, sin).astype(BF16)
    val = qkv[:, OUTW + HD :].astype(BF16)
    q_rot = [turn(qkv[:, h * HD : (h + 1) * HD], cos, sin).astype(BF16) for h in range(QH)]
    g = jnp.concatenate([grad[:, h * HD : (h + 1) * HD] for h in range(LOW)], axis=0)
    stacked = jnp.concatenate(q_rot[:LOW], axis=0)
    d_query, d_key[...], d_val[...] = head_grads(stacked, g, k_rot, val, seen, LOW)
    for h in range(LOW):
        out[:, h * HD : (h + 1) * HD] = turn(d_query[h * TOK : (h + 1) * TOK], cos, -sin).astype(BF16)
    for h in range(LOW, QH):
        rest[:, (h - LOW) * HD : (h - LOW + 1) * HD] = q_rot[h]
    rest[:, COLS - 2 * HD : COLS - HD] = k_rot
    rest[:, COLS - HD :] = val


def attend_high_body(rest, key_low, val_low, grad, doc, cosine, sine, out):
    cos, sin = cosine[...], sine[...]
    k_rot, val = rest[:, COLS - 2 * HD : COLS - HD], rest[:, COLS - HD :]
    count = QH - LOW
    g = jnp.concatenate([grad[:, h * HD : (h + 1) * HD] for h in range(LOW, QH)], axis=0)
    stacked = jnp.concatenate([rest[:, k * HD : (k + 1) * HD] for k in range(count)], axis=0)
    d_query, key, value = head_grads(stacked, g, k_rot, val, visible(doc), count)
    for k in range(count):
        out[:, k * HD : (k + 1) * HD] = turn(d_query[k * TOK : (k + 1) * TOK], cos, -sin).astype(BF16)
    total_key = (key_low[...] + key) * HD**-0.5
    out[:, COLS - 2 * HD : COLS - HD] = turn(total_key, cos, -sin).astype(BF16)
    out[:, COLS - HD :] = (val_low[...] + value).astype(BF16)


def attend_cost(heads):
    return pl.CostEstimate(
        flops=10 * TOK * TOK * HD * heads, bytes_accessed=4 << 20, transcendentals=TOK * TOK * heads
    )


def attend_low(own, came, grad, doc):
    wide, half = jax.ShapeDtypeStruct((TOK, COLS), BF16), jax.ShapeDtypeStruct((TOK, HD), F32)
    return pl.pallas_call(
        attend_low_body,
        out_shape=(wide, wide, half, half),
        in_specs=[VM] * 6,
        out_specs=(VM,) * 4,
        scratch_shapes=[pltpu.VMEM((TOK, QKV), F32)],
        compiler_params=pltpu.CompilerParams(vmem_limit_bytes=12 << 20),
        cost_estimate=attend_cost(LOW),
        name="attend_low",
    )(own, came, grad, doc, *TABLES)


def attend_high(rest, d_key, d_val, grad, doc):
    return pl.pallas_call(
        attend_high_body,
        out_shape=jax.ShapeDtypeStruct((TOK, COLS), BF16),
        in_specs=[VM] * 7,
        out_specs=VM,
        compiler_params=pltpu.CompilerParams(vmem_limit_bytes=12 << 20),
        cost_estimate=attend_cost(QH - LOW),
        name="attend_high",
    )(rest, d_key, d_val, grad, doc, *TABLES)


def normed_body(spots, low, low_other, high, high_other, *refs):
    pieces, own, send = refs[: len(spots)], refs[-2], refs[-1]
    for lower, higher, out in ((low_other, high_other, send), (low, high, own)):
        d_qkv = jnp.concatenate([lower[...], higher[...]], axis=1)
        for spot, piece in zip(spots, pieces):
            part = dot(d_qkv, piece[...], ((1,), (1,)))
            out[:, aligned(block(*spot) * HALF, HALF)] = part.astype(out.dtype)


def normed_grad(spots, grads, pieces):
    count = len(pieces)
    return pl.pallas_call(
        lambda *refs: normed_body(spots, *refs),
        out_shape=(
            jax.ShapeDtypeStruct((TOK, D // 2), F32),
            jax.ShapeDtypeStruct((TOK, D // 2), BF16),
        ),
        in_specs=[VM] * (4 + count),
        out_specs=(VM, VM),
        compiler_params=pltpu.CompilerParams(vmem_limit_bytes=12 << 20),
        cost_estimate=pl.CostEstimate(flops=2 * TOK * D * QKV, bytes_accessed=8 << 20, transcendentals=0),
        name="normed_grad",
    )(*grads, *pieces)


def tokens_body(own, came, tokens, scale_r, out):
    c = lax.axis_index("core")
    places = [
        (aligned(b * BLK + side * HALF, HALF), ref, slice(b * HALF, (b + 1) * HALF))
        for b in range(8)
        for side, ref in ((c, own), (1 - c, came))
    ]
    total = jnp.zeros((TOK, HALF), F32)
    for cols, ref, here in places:
        total = total + ref[:, here].astype(F32) * tokens[:, cols].astype(F32)
    r = scale_r[...]
    back = r * r * r * (jnp.sum(total, axis=1, keepdims=True) * (1.0 / D))
    for cols, ref, here in places:
        out[:, cols] = (r * ref[:, here].astype(F32) - tokens[:, cols].astype(F32) * back).astype(BF16)


def tokens_grad(own, came, tokens, scale_r):
    return pl.pallas_call(
        tokens_body,
        out_shape=jax.ShapeDtypeStruct((TOK, D), BF16),
        in_specs=[VM] * 4,
        out_specs=VM,
        compiler_params=pltpu.CompilerParams(vmem_limit_bytes=8 << 20),
        cost_estimate=pl.CostEstimate(flops=10 * TOK * D, bytes_accessed=8 << 20, transcendentals=0),
        name="tokens_grad",
    )(own, came, tokens, scale_r)


def term_product(along_x, level, feats, d_own, d_other):
    x, y, z, c = where()
    order = (0, 3 - 2 * c, 1 + 2 * c, 2)
    rows = []
    for first in (2 * level, 2 * level + 1):
        for second in range(4):
            i, j = (first, second) if along_x else (second, first)
            yy = y ^ order[j]
            start = ((x ^ order[i]) * 2 + (yy & 1)) * HALF + (yy >> 1) * QUART
            rows.append(feats[aligned(start, QUART), :])
    right = jnp.concatenate([d_own[...], d_other[...]], axis=0)
    return dot(jnp.concatenate(rows, axis=0), right, ((1,), (0,))).reshape(8, QUART, COLS)


def term_body(along_x, level, feats, d_own, d_other, out):
    out[...] = term_product(along_x, level, feats, d_own, d_other).astype(BF16)


def terms(along_x, level, made):
    return pl.pallas_call(
        lambda *refs: term_body(along_x, level, *refs),
        out_shape=jax.ShapeDtypeStruct((8, QUART, COLS), BF16),
        in_specs=[VM] * 3,
        out_specs=VM,
        compiler_params=pltpu.CompilerParams(vmem_limit_bytes=12 << 20),
        cost_estimate=pl.CostEstimate(
            flops=2 * 8 * QUART * COLS * 2 * TOK, bytes_accessed=4 << 20, transcendentals=0
        ),
        name="terms",
    )(*made)


def add_body(parts, cuts, *refs):
    total = sum(ref[first : first + count].astype(F32) for ref, (first, count) in zip(refs, parts)).astype(BF16)
    for out, (first, count) in zip(refs[len(parts) :], cuts):
        out[...] = total[first : first + count]


def add(parts, cuts):
    arrays, spans = [part[0] for part in parts], [part[1:] for part in parts]
    return pl.pallas_call(
        lambda *refs: add_body(spans, cuts, *refs),
        out_shape=tuple(jax.ShapeDtypeStruct((count, QUART, COLS), BF16) for _, count in cuts),
        in_specs=[VM] * len(parts),
        out_specs=(VM,) * len(cuts),
        compiler_params=pltpu.CompilerParams(vmem_limit_bytes=6 << 20),
        cost_estimate=pl.CostEstimate(flops=1 << 20, bytes_accessed=1 << 20, transcendentals=0),
        name="add",
    )(*arrays)


def join_body(old_x, came_x, old_y, came_y, out):
    out[:, :, :COLS] = (old_x[...].astype(F32) + came_x[...].astype(F32)).astype(BF16).reshape(8, PIECE, COLS)
    out[:, :, COLS:] = (old_y[...].astype(F32) + came_y[...].astype(F32)).astype(BF16).reshape(8, PIECE, COLS)


def join(*parts):
    return pl.pallas_call(
        join_body,
        out_shape=jax.ShapeDtypeStruct((8, PIECE, QKV), BF16),
        in_specs=[VM] * 4,
        out_specs=VM,
        compiler_params=pltpu.CompilerParams(vmem_limit_bytes=4 << 20),
        name="join",
    )(*parts)


def finish_body(parts, out):
    total = sum(parts[i].astype(F32) for i in range(8)).astype(BF16)
    for i in range(16):
        out[i] = total


def finish(parts):
    return pl.pallas_call(
        finish_body,
        out_shape=jax.ShapeDtypeStruct((16, PIECE, QKV), BF16),
        in_specs=[VM],
        out_specs=VM,
        compiler_params=pltpu.CompilerParams(vmem_limit_bytes=4 << 20),
        name="finish",
    )(parts)


def squares_body(got, out):
    total = jnp.zeros((PIECE, QKV), F32)
    for i in range(16):
        value = got[i].astype(F32)
        total = total + value * value
    total = jnp.sum(jnp.sum(total, axis=1, keepdims=True), axis=0, keepdims=True)
    out[...] = jnp.broadcast_to(total.reshape(1, 1, 1), (16, 8, 128))


def squares(got):
    return pl.pallas_call(
        squares_body,
        out_shape=jax.ShapeDtypeStruct((16, 8, 128), F32),
        in_specs=[VM],
        out_specs=VM,
        compiler_params=pltpu.CompilerParams(vmem_limit_bytes=4 << 20),
        name="squares",
    )(got)


def rescale_body(parts, mine, theirs, out):
    total = sum(parts[i] for i in range(16))
    factor = (target_rms * lax.rsqrt(total * (1.0 / (D * QKV)) + 1e-06))[:1, :1]
    c = lax.axis_index("core")
    for side, half in ((c, mine), (1 - c, theirs)):
        out[aligned(side * HALF, HALF), :] = (half[...].reshape(HALF, QKV).astype(F32) * factor).astype(BF16)


def rescale(parts, mine, theirs):
    return pl.pallas_call(
        rescale_body,
        out_shape=jax.ShapeDtypeStruct((BLK, QKV), BF16),
        in_specs=[VM] * 3,
        out_specs=VM,
        compiler_params=pltpu.CompilerParams(vmem_limit_bytes=8 << 20),
        name="rescale",
    )(parts, mine, theirs)


def tables():
    freq = np.exp(-np.log(rope_base) * 2.0 * np.arange(HD // 2) / HD)
    angle = np.arange(TOK)[:, None] * freq[None, :]
    cos, sin = np.cos(angle), np.sin(angle)
    return np.concatenate([cos, cos], 1).astype(np.float32), np.concatenate([-sin, sin], 1).astype(np.float32)


TABLES = tables()

def on_device(tokens, grad_attended, doc_ids, w_own):
    w00 = lax.dynamic_slice_in_dim(w_own, lax.axis_index("core") * HALF, HALF, 0)
    w00, tokens = lax.optimization_barrier((w00, tokens))
    wa0 = swap(w00, gather_x1)
    w01 = swap(w00, flip_y)
    scale_r, own, send_low, send_high = norm(tokens)
    other = [swap(send, other_core) for send in (send_low, send_high)]
    wa0, w01, own, other = lax.optimization_barrier((wa0, w01, own, other))
    both = (own, *other)
    wo0 = swap(wa0, gather_x2)
    wa1 = swap(wa0, flip_y)
    wb0 = swap(wa0, pair_z)
    early, early_spots = [w00, w01, wa0], [("0", 0), ("0", 1), ("a", 0)]
    part_own, part_other = project(early_spots, both, early)
    feats = transpose(*both)
    wo0, wa1, part_own, part_other, feats = lax.optimization_barrier((wo0, wa1, part_own, part_other, feats))
    wo1 = swap(wo0, flip_y)
    wb1 = swap(wa1, pair_z)
    middle, middle_spots = [wo0, wa1, wb0], [("o", 0), ("a", 1), ("b", 0)]
    part_own, part_other = project(middle_spots, both, middle, part_own, part_other)
    wo1, wb1, part_own, part_other = lax.optimization_barrier((wo1, wb1, part_own, part_other))
    late, late_spots = [wo1, wb1], [("o", 1), ("b", 1)]
    late_other = project_late(late_spots, other, late, part_other, BF16)
    came = swap(late_other, other_core)
    late_other, part_own = lax.optimization_barrier((late_other, part_own))
    qkv = project_late(late_spots, [own], late, part_own, F32)
    d_low, rest, d_key, d_val = attend_low(qkv, came, grad_attended, doc_ids)

    low_other = swap(d_low, other_core)
    d_high = attend_high(rest, d_key, d_val, grad_attended, doc_ids)
    low_other, d_high = lax.optimization_barrier((low_other, d_high))
    high_other = swap(d_high, other_core)
    lows, highs = (feats, d_low, low_other), (feats, d_high, high_other)
    came_x = swap(terms(True, 1, lows), x_1)
    sent_y = terms(False, 1, highs)
    came_y = swap(sent_y, y_1)
    spots, pieces = early_spots + middle_spots + late_spots, early + middle + late
    sent_y, lows, highs = lax.optimization_barrier((sent_y, lows, highs))
    sum_x, sum_y = terms(True, 0, lows), terms(False, 0, highs)
    normed_own, normed_send = normed_grad(spots, (*lows[1:], *highs[1:]), pieces)
    normed_came = swap(normed_send, other_core)
    came_x, sum_x, sum_y, normed_own = lax.optimization_barrier((came_x, sum_x, sum_y, normed_own))
    first, second = add([(sum_x, 4, 4), (came_x, 4, 4)], [(2, 2), (0, 2)])
    pass_x, keep_x = swap(first, x_2), swap(second, x_2)
    first, second = add([(sum_y, 4, 4), (came_y, 4, 4)], [(2, 2), (0, 2)])
    pass_y, keep_y = swap(first, y_2), swap(second, y_2)
    first, normed_came = lax.optimization_barrier((first, normed_came))
    d_tokens = tokens_grad(normed_own, normed_came, tokens, scale_r)
    pass_x, d_tokens = lax.optimization_barrier((pass_x, d_tokens))
    (sent,) = add([(sum_x, 2, 2), (came_x, 2, 2), (pass_x, 0, 2)], [(0, 2)])
    pass_x = swap(sent, y_1)
    (sent,) = add([(sum_y, 2, 2), (came_y, 2, 2), (pass_y, 0, 2)], [(0, 2)])
    pass_y = swap(sent, x_1)
    sum_x, sent = add([(sum_x, 0, 2), (came_x, 0, 2), (keep_x, 0, 2), (pass_x, 0, 2)], [(0, 1), (1, 1)])
    came_x = swap(sent, y_2)
    sum_y, sent = add([(sum_y, 0, 2), (came_y, 0, 2), (keep_y, 0, 2), (pass_y, 0, 2)], [(0, 1), (1, 1)])
    came_y = swap(sent, x_2)

    total = join(sum_x, came_x, sum_y, came_y)
    got = finish(lax.all_to_all(total, "z", 0, 0))
    got = lax.all_to_all(got, ("y_hi", "z"), 0, 0)

    theirs = swap(got, other_core)
    parts = lax.all_to_all(squares(got), ("x", "y_lo", "core"), 0, 0)
    return d_tokens, rescale(parts, got, theirs)


def solution(mesh):
    mesh = Mesh(mesh.devices.reshape(SIZES), AXES)
    spread, rows = P(AXES, None), P(AXES[:2], None)
    return jax.shard_map(
        on_device,
        mesh=mesh,
        in_specs=(spread, spread, spread, rows),
        out_specs=(spread, rows),
        check_vma=False,
    )
```

```python
import jax
import jax.numpy as jnp
import numpy as np
from jax import lax
from jax.experimental import pallas as pl
from jax.experimental.pallas import tpu as pltpu
from jax.sharding import Mesh
from jax.sharding import PartitionSpec as P

D = 4096
HD = 128
QH = 8
QKV = 1280
TOK = 256
BLK = D // 8
HALF = BLK // 2
QUART = HALF // 2
PIECE = QUART // 8
COLS = QKV // 2
OUTW = QH * HD
LOW = COLS // HD

AXES = ("x", "y_lo", "y_hi", "z", "core")
SIZES = (4, 2, 2, 8, 2)
target_rms = 0.5
rope_base = 500000.0
F32 = jnp.float32
BF16 = jnp.bfloat16


def flat(x, y, z, c):
    return (x * 2 + y % 2) * 32 + (y // 2) * 16 + z * 2 + c


def swap(value, partner):
    pairs = []
    for x in range(4):
        for y in range(4):
            for z in range(8):
                for c in range(2):
                    pairs.append((flat(x, y, z, c), flat(*partner(x, y, z, c))))
    return lax.ppermute(value, AXES, pairs)


def near(c):
    return 1 if c == 0 else 3


def other_core(x, y, z, c):
    return x, y, z, 1 - c


def gather_x1(x, y, z, c):
    return x ^ near(c ^ (z & 1)), y, z, c


def gather_x2(x, y, z, c):
    return x ^ (4 - near(c ^ (z & 1))), y, z, c


def flip_y(x, y, z, c):
    return x, y ^ near(c), z, c


def pair_z(x, y, z, c):
    return x, y, (z ^ 1) if c == 0 else ((z + 1) % 8 if z % 2 else (z - 1) % 8), c


def x_1(x, y, z, c):
    return x ^ near(c), y, z, c


def x_2(x, y, z, c):
    return x ^ (4 - near(c)), y, z, c


def y_1(x, y, z, c):
    return x, y ^ near(c), z, c


def y_2(x, y, z, c):
    return x, y ^ (4 - near(c)), z, c


VM = pl.BlockSpec(memory_space=pltpu.VMEM)
SM = pl.BlockSpec(memory_space=pltpu.SMEM)


def dot(a, b, dims):
    return lax.dot_general(a, b, (dims, ((), ())), preferred_element_type=F32)


def where():
    x, y_lo, y_hi, z, c = (lax.axis_index(axis) for axis in AXES)
    return x, y_hi * 2 + y_lo, z, c


def aligned(start, size):
    return pl.ds(pl.multiple_of(start, size), size)


def norm_body(tokens, scale_r, own, send_low, send_high):
    full = tokens[...].astype(F32)
    r = lax.rsqrt(jnp.sum(full * full, axis=1, keepdims=True) * (1.0 / D) + 1e-05)
    scale_r[...] = r
    c = lax.axis_index("core")
    for b in range(8):
        here = slice(b * HALF, (b + 1) * HALF)
        for side in (c, 1 - c):
            part = (tokens[:, aligned(b * BLK + side * HALF, HALF)].astype(F32) * r).astype(BF16)
            if side is c:
                own[:, here] = part
            else:
                send_low[:, here] = part[: TOK // 2]
                send_high[:, here] = part[TOK // 2 :]


def norm(tokens):
    half = jax.ShapeDtypeStruct((TOK, D // 2), BF16)
    quarter = jax.ShapeDtypeStruct((TOK // 2, D // 2), BF16)
    return pl.pallas_call(
        norm_body,
        out_shape=(jax.ShapeDtypeStruct((TOK, 1), F32), half, quarter, quarter),
        in_specs=[VM],
        out_specs=(VM,) * 4,
        compiler_params=pltpu.CompilerParams(vmem_limit_bytes=12 << 20),
        cost_estimate=pl.CostEstimate(flops=10 * TOK * D, bytes_accessed=4 << 20, transcendentals=0),
        name="norm",
    )(tokens)


def transpose_body(own, low, high, out):
    for b in range(8):
        cols = slice(b * HALF, (b + 1) * HALF)
        out[cols, :TOK] = own[:, cols].T
        out[cols, TOK:] = jnp.concatenate([low[:, cols], high[:, cols]], axis=0).T


def transpose(own, low, high):
    return pl.pallas_call(
        transpose_body,
        out_shape=jax.ShapeDtypeStruct((D // 2, 2 * TOK), BF16),
        in_specs=[VM] * 3,
        out_specs=VM,
        compiler_params=pltpu.CompilerParams(vmem_limit_bytes=6 << 20),
        cost_estimate=pl.CostEstimate(flops=4 * TOK * D, bytes_accessed=4 << 20, transcendentals=0),
        name="transpose",
    )(own, low, high)


def block(name, flip):
    x, y, z, c = where()
    turned = c ^ (z & 1)
    step = {"0": 0, "a": 1 + 2 * turned, "b": 3 - 2 * turned, "o": 2}[name]
    return (x ^ step) * 2 + ((y & 1) ^ flip)


def product(spots, feats, pieces):
    cols = [aligned(block(*spot) * HALF, HALF) for spot in spots]
    lhs = jnp.concatenate([jnp.concatenate([ref[:, k] for k in cols], axis=1) for ref in feats], axis=0)
    return dot(lhs, jnp.concatenate([p[...] for p in pieces], axis=0), ((1,), (0,)))


def part_body(spots, own, low, high, *refs):
    count = len(spots)
    pieces, old, outs = refs[:count], refs[count:-2], refs[-2:]
    part = product(spots, (own, low, high), pieces)
    for k, half in enumerate((part[:TOK], part[TOK:])):
        outs[k][...] = half + old[k][...] if old else half


def project(spots, feats, pieces, *old):
    count, out = len(pieces), jax.ShapeDtypeStruct((TOK, QKV), F32)
    return pl.pallas_call(
        lambda *refs: part_body(spots, *refs),
        out_shape=(out, out),
        in_specs=[VM] * (3 + count + len(old)),
        out_specs=(VM, VM),
        compiler_params=pltpu.CompilerParams(vmem_limit_bytes=12 << 20),
        cost_estimate=pl.CostEstimate(
            flops=4 * TOK * HALF * count * QKV, bytes_accessed=6 << 20, transcendentals=0
        ),
        name="project",
    )(*feats, *pieces, *old)


def late_body(spots, count, *refs):
    feats, pieces, old, out = refs[:count], refs[count:-2], refs[-2], refs[-1]
    out[...] = (old[...] + product(spots, feats, pieces)).astype(out.dtype)


def project_late(spots, feats, pieces, old, dtype):
    count = len(feats)
    return pl.pallas_call(
        lambda *refs: late_body(spots, count, *refs),
        out_shape=jax.ShapeDtypeStruct((TOK, QKV), dtype),
        in_specs=[VM] * (1 + count + len(pieces)),
        out_specs=VM,
        compiler_params=pltpu.CompilerParams(vmem_limit_bytes=8 << 20),
        cost_estimate=pl.CostEstimate(
            flops=2 * TOK * HALF * len(pieces) * QKV, bytes_accessed=4 << 20, transcendentals=0
        ),
        name="project_late",
    )(*feats, *pieces, old)


def visible(doc):
    rows = lax.broadcasted_iota(jnp.int32, (TOK, TOK), 0)
    cols = lax.broadcasted_iota(jnp.int32, (TOK, TOK), 1)
    along = jnp.broadcast_to(doc[...], (TOK, TOK))
    return (cols <= rows) & (along == along.T)


def turn(value, cos, sin):
    return value * cos + pltpu.roll(value, HD // 2, 1) * sin


def head_grads(q_rot, g, k_rot, val, seen, count):
    scale = HD**-0.5
    scores = dot(q_rot, k_rot, ((1,), (1,))).reshape(count, TOK, TOK)
    scores = jnp.where(seen[None], scores, -1e30)
    expo = jnp.exp((scores - jnp.max(scores, axis=2, keepdims=True)) * scale)
    probs = expo * (1.0 / jnp.sum(expo, axis=2, keepdims=True))
    d_probs = dot(g, val, ((1,), (1,))).reshape(count, TOK, TOK)
    delta = jnp.sum(d_probs * probs, axis=2, keepdims=True)
    d_scores = (probs * (d_probs - delta)).astype(BF16).reshape(count * TOK, TOK)
    probs = probs.astype(BF16).reshape(count * TOK, TOK)
    d_val = dot(probs, g, ((0,), (0,)))
    d_key = dot(d_scores, q_rot, ((0,), (0,)))
    return dot(d_scores, k_rot, ((1,), (0,))) * scale, d_key, d_val


def attend_low_body(own, came, grad, doc, cosine, sine, out, rest, d_key, d_val, qkv):
    qkv[...] = own[...] + came[...].astype(F32)
    cos, sin = cosine[...], sine[...]
    seen = visible(doc)
    k_rot = turn(qkv[:, OUTW : OUTW + HD], cos, sin).astype(BF16)
    val = qkv[:, OUTW + HD :].astype(BF16)
    q_rot = [turn(qkv[:, h * HD : (h + 1) * HD], cos, sin).astype(BF16) for h in range(QH)]
    g = jnp.concatenate([grad[:, h * HD : (h + 1) * HD] for h in range(LOW)], axis=0)
    stacked = jnp.concatenate(q_rot[:LOW], axis=0)
    d_query, d_key[...], d_val[...] = head_grads(stacked, g, k_rot, val, seen, LOW)
    for h in range(LOW):
        out[:, h * HD : (h + 1) * HD] = turn(d_query[h * TOK : (h + 1) * TOK], cos, -sin).astype(BF16)
    for h in range(LOW, QH):
        rest[:, (h - LOW) * HD : (h - LOW + 1) * HD] = q_rot[h]
    rest[:, COLS - 2 * HD : COLS - HD] = k_rot
    rest[:, COLS - HD :] = val


def attend_high_body(rest, key_low, val_low, grad, doc, cosine, sine, out):
    cos, sin = cosine[...], sine[...]
    k_rot, val = rest[:, COLS - 2 * HD : COLS - HD], rest[:, COLS - HD :]
    count = QH - LOW
    g = jnp.concatenate([grad[:, h * HD : (h + 1) * HD] for h in range(LOW, QH)], axis=0)
    stacked = jnp.concatenate([rest[:, k * HD : (k + 1) * HD] for k in range(count)], axis=0)
    d_query, key, value = head_grads(stacked, g, k_rot, val, visible(doc), count)
    for k in range(count):
        out[:, k * HD : (k + 1) * HD] = turn(d_query[k * TOK : (k + 1) * TOK], cos, -sin).astype(BF16)
    total_key = (key_low[...] + key) * HD**-0.5
    out[:, COLS - 2 * HD : COLS - HD] = turn(total_key, cos, -sin).astype(BF16)
    out[:, COLS - HD :] = (val_low[...] + value).astype(BF16)


def attend_cost(heads):
    return pl.CostEstimate(
        flops=10 * TOK * TOK * HD * heads, bytes_accessed=4 << 20, transcendentals=TOK * TOK * heads
    )


def attend_low(own, came, grad, doc):
    wide, half = jax.ShapeDtypeStruct((TOK, COLS), BF16), jax.ShapeDtypeStruct((TOK, HD), F32)
    return pl.pallas_call(
        attend_low_body,
        out_shape=(wide, wide, half, half),
        in_specs=[VM] * 6,
        out_specs=(VM,) * 4,
        scratch_shapes=[pltpu.VMEM((TOK, QKV), F32)],
        compiler_params=pltpu.CompilerParams(vmem_limit_bytes=12 << 20),
        cost_estimate=attend_cost(LOW),
        name="attend_low",
    )(own, came, grad, doc, *TABLES)


def attend_high(rest, d_key, d_val, grad, doc):
    return pl.pallas_call(
        attend_high_body,
        out_shape=jax.ShapeDtypeStruct((TOK, COLS), BF16),
        in_specs=[VM] * 7,
        out_specs=VM,
        compiler_params=pltpu.CompilerParams(vmem_limit_bytes=12 << 20),
        cost_estimate=attend_cost(QH - LOW),
        name="attend_high",
    )(rest, d_key, d_val, grad, doc, *TABLES)


def normed_body(spots, low, low_other, high, high_other, *refs):
    pieces, own, send = refs[: len(spots)], refs[-2], refs[-1]
    for lower, higher, out in ((low_other, high_other, send), (low, high, own)):
        d_qkv = jnp.concatenate([lower[...], higher[...]], axis=1)
        for spot, piece in zip(spots, pieces):
            part = dot(d_qkv, piece[...], ((1,), (1,)))
            out[:, aligned(block(*spot) * HALF, HALF)] = part.astype(out.dtype)


def normed_grad(spots, grads, pieces):
    count = len(pieces)
    return pl.pallas_call(
        lambda *refs: normed_body(spots, *refs),
        out_shape=(
            jax.ShapeDtypeStruct((TOK, D // 2), F32),
            jax.ShapeDtypeStruct((TOK, D // 2), BF16),
        ),
        in_specs=[VM] * (4 + count),
        out_specs=(VM, VM),
        compiler_params=pltpu.CompilerParams(vmem_limit_bytes=12 << 20),
        cost_estimate=pl.CostEstimate(flops=2 * TOK * D * QKV, bytes_accessed=8 << 20, transcendentals=0),
        name="normed_grad",
    )(*grads, *pieces)


def tokens_body(own, came, tokens, scale_r, out):
    c = lax.axis_index("core")
    places = [
        (aligned(b * BLK + side * HALF, HALF), ref, slice(b * HALF, (b + 1) * HALF))
        for b in range(8)
        for side, ref in ((c, own), (1 - c, came))
    ]
    total = jnp.zeros((TOK, HALF), F32)
    for cols, ref, here in places:
        total = total + ref[:, here].astype(F32) * tokens[:, cols].astype(F32)
    r = scale_r[...]
    back = r * r * r * (jnp.sum(total, axis=1, keepdims=True) * (1.0 / D))
    for cols, ref, here in places:
        out[:, cols] = (r * ref[:, here].astype(F32) - tokens[:, cols].astype(F32) * back).astype(BF16)


def tokens_grad(own, came, tokens, scale_r):
    return pl.pallas_call(
        tokens_body,
        out_shape=jax.ShapeDtypeStruct((TOK, D), BF16),
        in_specs=[VM] * 4,
        out_specs=VM,
        compiler_params=pltpu.CompilerParams(vmem_limit_bytes=8 << 20),
        cost_estimate=pl.CostEstimate(flops=10 * TOK * D, bytes_accessed=8 << 20, transcendentals=0),
        name="tokens_grad",
    )(own, came, tokens, scale_r)


def term_product(along_x, level, feats, d_own, d_other):
    x, y, z, c = where()
    order = (0, 3 - 2 * c, 1 + 2 * c, 2)
    rows = []
    for first in (2 * level, 2 * level + 1):
        for second in range(4):
            i, j = (first, second) if along_x else (second, first)
            yy = y ^ order[j]
            start = ((x ^ order[i]) * 2 + (yy & 1)) * HALF + (yy >> 1) * QUART
            rows.append(feats[aligned(start, QUART), :])
    right = jnp.concatenate([d_own[...], d_other[...]], axis=0)
    return dot(jnp.concatenate(rows, axis=0), right, ((1,), (0,))).reshape(8, QUART, COLS)


def term_body(along_x, level, feats, d_own, d_other, out):
    out[...] = term_product(along_x, level, feats, d_own, d_other).astype(BF16)


def terms(along_x, level, made):
    return pl.pallas_call(
        lambda *refs: term_body(along_x, level, *refs),
        out_shape=jax.ShapeDtypeStruct((8, QUART, COLS), BF16),
        in_specs=[VM] * 3,
        out_specs=VM,
        compiler_params=pltpu.CompilerParams(vmem_limit_bytes=12 << 20),
        cost_estimate=pl.CostEstimate(
            flops=2 * 8 * QUART * COLS * 2 * TOK, bytes_accessed=4 << 20, transcendentals=0
        ),
        name="terms",
    )(*made)


def add_body(parts, cuts, *refs):
    total = sum(ref[first : first + count].astype(F32) for ref, (first, count) in zip(refs, parts)).astype(BF16)
    for out, (first, count) in zip(refs[len(parts) :], cuts):
        out[...] = total[first : first + count]


def add(parts, cuts):
    arrays, spans = [part[0] for part in parts], [part[1:] for part in parts]
    return pl.pallas_call(
        lambda *refs: add_body(spans, cuts, *refs),
        out_shape=tuple(jax.ShapeDtypeStruct((count, QUART, COLS), BF16) for _, count in cuts),
        in_specs=[VM] * len(parts),
        out_specs=(VM,) * len(cuts),
        compiler_params=pltpu.CompilerParams(vmem_limit_bytes=6 << 20),
        cost_estimate=pl.CostEstimate(flops=1 << 20, bytes_accessed=1 << 20, transcendentals=0),
        name="add",
    )(*arrays)


def join_body(old_x, came_x, old_y, came_y, out):
    out[:, :, :COLS] = (old_x[...].astype(F32) + came_x[...].astype(F32)).astype(BF16).reshape(8, PIECE, COLS)
    out[:, :, COLS:] = (old_y[...].astype(F32) + came_y[...].astype(F32)).astype(BF16).reshape(8, PIECE, COLS)


def join(*parts):
    return pl.pallas_call(
        join_body,
        out_shape=jax.ShapeDtypeStruct((8, PIECE, QKV), BF16),
        in_specs=[VM] * 4,
        out_specs=VM,
        compiler_params=pltpu.CompilerParams(vmem_limit_bytes=4 << 20),
        name="join",
    )(*parts)


def finish_body(parts, out):
    total = sum(parts[i].astype(F32) for i in range(8)).astype(BF16)
    for i in range(16):
        out[i] = total


def finish(parts):
    return pl.pallas_call(
        finish_body,
        out_shape=jax.ShapeDtypeStruct((16, PIECE, QKV), BF16),
        in_specs=[VM],
        out_specs=VM,
        compiler_params=pltpu.CompilerParams(vmem_limit_bytes=4 << 20),
        name="finish",
    )(parts)


def squares_body(got, out):
    total = jnp.zeros((PIECE, 128), F32)
    for i in range(16):
        value = got[i].astype(F32)
        value = value * value
        for k in range(0, QKV, 128):
            total = total + value[:, k : k + 128]
    out[...] = jnp.broadcast_to((total[:8] + total[8:])[None], (16, 8, 128))


def squares(got):
    return pl.pallas_call(
        squares_body,
        out_shape=jax.ShapeDtypeStruct((16, 8, 128), F32),
        in_specs=[VM],
        out_specs=VM,
        compiler_params=pltpu.CompilerParams(vmem_limit_bytes=4 << 20),
        name="squares",
    )(got)


def rescale_body(parts, mine, theirs, out, held, sems):
    total = sum(parts[i] for i in range(16))
    total = jnp.sum(jnp.sum(total, axis=1, keepdims=True), axis=0, keepdims=True)
    factor = target_rms * lax.rsqrt(total * (1.0 / (D * QKV)) + 1e-06)
    c = lax.axis_index("core")
    copies = []
    for side, half in ((c, mine), (1 - c, theirs)):
        for k in range(2):
            i = len(copies)
            part = half[8 * k : 8 * (k + 1)].reshape(QUART, QKV)
            held[i] = (part.astype(F32) * factor).astype(BF16)
            rows = aligned(side * HALF + k * QUART, QUART)
            copies.append(pltpu.make_async_copy(held.at[i], out.at[rows, :], sems.at[i]))
            copies[-1].start()
    for copy in copies:
        copy.wait()


def rescale(parts, mine, theirs):
    return pl.pallas_call(
        rescale_body,
        out_shape=jax.ShapeDtypeStruct((BLK, QKV), BF16),
        in_specs=[VM] * 3,
        out_specs=pl.BlockSpec(memory_space=pl.ANY),
        scratch_shapes=[pltpu.VMEM((4, QUART, QKV), BF16), pltpu.SemaphoreType.DMA((4,))],
        compiler_params=pltpu.CompilerParams(vmem_limit_bytes=8 << 20),
        name="rescale",
    )(parts, mine, theirs)


def tables():
    freq = np.exp(-np.log(rope_base) * 2.0 * np.arange(HD // 2) / HD)
    angle = np.arange(TOK)[:, None] * freq[None, :]
    cos, sin = np.cos(angle), np.sin(angle)
    return np.concatenate([cos, cos], 1).astype(np.float32), np.concatenate([-sin, sin], 1).astype(np.float32)


TABLES = tables()

def on_device(tokens, grad_attended, doc_ids, w_own):
    w00 = lax.dynamic_slice_in_dim(w_own, lax.axis_index("core") * HALF, HALF, 0)
    w00, tokens = lax.optimization_barrier((w00, tokens))
    wa0 = swap(w00, gather_x1)
    w01 = swap(w00, flip_y)
    scale_r, own, send_low, send_high = norm(tokens)
    other = [swap(send, other_core) for send in (send_low, send_high)]
    wa0, w01, own, other = lax.optimization_barrier((wa0, w01, own, other))
    both = (own, *other)
    wo0 = swap(wa0, gather_x2)
    wa1 = swap(wa0, flip_y)
    wb0 = swap(wa0, pair_z)
    early, early_spots = [w00, w01, wa0], [("0", 0), ("0", 1), ("a", 0)]
    part_own, part_other = project(early_spots, both, early)
    feats = transpose(*both)
    wo0, wa1, part_own, part_other, feats = lax.optimization_barrier((wo0, wa1, part_own, part_other, feats))
    wo1 = swap(wo0, flip_y)
    wb1 = swap(wa1, pair_z)
    middle, middle_spots = [wo0, wa1, wb0], [("o", 0), ("a", 1), ("b", 0)]
    part_own, part_other = project(middle_spots, both, middle, part_own, part_other)
    wo1, wb1, part_own, part_other = lax.optimization_barrier((wo1, wb1, part_own, part_other))
    late, late_spots = [wo1, wb1], [("o", 1), ("b", 1)]
    late_other = project_late(late_spots, other, late, part_other, BF16)
    came = swap(late_other, other_core)
    late_other, part_own = lax.optimization_barrier((late_other, part_own))
    qkv = project_late(late_spots, [own], late, part_own, F32)
    d_low, rest, d_key, d_val = attend_low(qkv, came, grad_attended, doc_ids)

    low_other = swap(d_low, other_core)
    d_high = attend_high(rest, d_key, d_val, grad_attended, doc_ids)
    low_other, d_high = lax.optimization_barrier((low_other, d_high))
    high_other = swap(d_high, other_core)
    lows, highs = (feats, d_low, low_other), (feats, d_high, high_other)
    came_x = swap(terms(True, 1, lows), x_1)
    sent_y = terms(False, 1, highs)
    came_y = swap(sent_y, y_1)
    spots, pieces = early_spots + middle_spots + late_spots, early + middle + late
    sent_y, lows, highs = lax.optimization_barrier((sent_y, lows, highs))
    sum_x, sum_y = terms(True, 0, lows), terms(False, 0, highs)
    normed_own, normed_send = normed_grad(spots, (*lows[1:], *highs[1:]), pieces)
    normed_came = swap(normed_send, other_core)
    came_x, sum_x, sum_y, normed_own = lax.optimization_barrier((came_x, sum_x, sum_y, normed_own))
    first, second = add([(sum_x, 4, 4), (came_x, 4, 4)], [(2, 2), (0, 2)])
    pass_x, keep_x = swap(first, x_2), swap(second, x_2)
    first, second = add([(sum_y, 4, 4), (came_y, 4, 4)], [(2, 2), (0, 2)])
    pass_y, keep_y = swap(first, y_2), swap(second, y_2)
    first, normed_came = lax.optimization_barrier((first, normed_came))
    d_tokens = tokens_grad(normed_own, normed_came, tokens, scale_r)
    pass_x, d_tokens = lax.optimization_barrier((pass_x, d_tokens))
    (sent,) = add([(sum_x, 2, 2), (came_x, 2, 2), (pass_x, 0, 2)], [(0, 2)])
    pass_x = swap(sent, y_1)
    (sent,) = add([(sum_y, 2, 2), (came_y, 2, 2), (pass_y, 0, 2)], [(0, 2)])
    pass_y = swap(sent, x_1)
    sum_x, sent = add([(sum_x, 0, 2), (came_x, 0, 2), (keep_x, 0, 2), (pass_x, 0, 2)], [(0, 1), (1, 1)])
    came_x = swap(sent, y_2)
    sum_y, sent = add([(sum_y, 0, 2), (came_y, 0, 2), (keep_y, 0, 2), (pass_y, 0, 2)], [(0, 1), (1, 1)])
    came_y = swap(sent, x_2)

    total = join(sum_x, came_x, sum_y, came_y)
    got = finish(lax.all_to_all(total, "z", 0, 0))
    got = lax.all_to_all(got, ("y_hi", "z"), 0, 0)

    theirs = swap(got, other_core)
    parts = lax.all_to_all(squares(got), ("x", "y_lo", "core"), 0, 0)
    return d_tokens, rescale(parts, got, theirs)


def solution(mesh):
    mesh = Mesh(mesh.devices.reshape(SIZES), AXES)
    spread, rows = P(AXES, None), P(AXES[:2], None)
    return jax.shard_map(
        on_device,
        mesh=mesh,
        in_specs=(spread, spread, spread, rows),
        out_specs=(spread, rows),
        check_vma=False,
    )
```

```python
import jax
import jax.numpy as jnp
import numpy as np
from jax import lax
from jax.experimental import pallas as pl
from jax.experimental.pallas import tpu as pltpu
from jax.sharding import Mesh
from jax.sharding import PartitionSpec as P

D = 4096
HD = 128
QH = 8
QKV = 1280
TOK = 256
BLK = D // 8
HALF = BLK // 2
QUART = HALF // 2
PIECE = QUART // 8
COLS = QKV // 2
OUTW = QH * HD
LOW = COLS // HD

AXES = ("x", "y_lo", "y_hi", "z", "core")
SIZES = (4, 2, 2, 8, 2)
target_rms = 0.5
rope_base = 500000.0
F32 = jnp.float32
BF16 = jnp.bfloat16


def flat(x, y, z, c):
    return (x * 2 + y % 2) * 32 + (y // 2) * 16 + z * 2 + c


def swap(value, partner):
    pairs = []
    for x in range(4):
        for y in range(4):
            for z in range(8):
                for c in range(2):
                    pairs.append((flat(x, y, z, c), flat(*partner(x, y, z, c))))
    return lax.ppermute(value, AXES, pairs)


def near(c):
    return 1 if c == 0 else 3


def other_core(x, y, z, c):
    return x, y, z, 1 - c


def gather_x1(x, y, z, c):
    return x ^ near(c ^ (z & 1)), y, z, c


def gather_x2(x, y, z, c):
    return x ^ (4 - near(c ^ (z & 1))), y, z, c


def flip_y(x, y, z, c):
    return x, y ^ near(c), z, c


def pair_z(x, y, z, c):
    return x, y, (z ^ 1) if c == 0 else ((z + 1) % 8 if z % 2 else (z - 1) % 8), c


def x_1(x, y, z, c):
    return x ^ near(c), y, z, c


def x_2(x, y, z, c):
    return x ^ (4 - near(c)), y, z, c


def y_1(x, y, z, c):
    return x, y ^ near(c), z, c


def y_2(x, y, z, c):
    return x, y ^ (4 - near(c)), z, c


VM = pl.BlockSpec(memory_space=pltpu.VMEM)
SM = pl.BlockSpec(memory_space=pltpu.SMEM)


def dot(a, b, dims):
    return lax.dot_general(a, b, (dims, ((), ())), preferred_element_type=F32)


def where():
    x, y_lo, y_hi, z, c = (lax.axis_index(axis) for axis in AXES)
    return x, y_hi * 2 + y_lo, z, c


def aligned(start, size):
    return pl.ds(pl.multiple_of(start, size), size)


def norm_body(tokens, scale_r, own, send_low, send_high):
    full = tokens[...].astype(F32)
    r = lax.rsqrt(jnp.sum(full * full, axis=1, keepdims=True) * (1.0 / D) + 1e-05)
    scale_r[...] = r
    c = lax.axis_index("core")
    for b in range(8):
        here = slice(b * HALF, (b + 1) * HALF)
        for side in (c, 1 - c):
            part = (tokens[:, aligned(b * BLK + side * HALF, HALF)].astype(F32) * r).astype(BF16)
            if side is c:
                own[:, here] = part
            else:
                send_low[:, here] = part[: TOK // 2]
                send_high[:, here] = part[TOK // 2 :]


def norm(tokens):
    half = jax.ShapeDtypeStruct((TOK, D // 2), BF16)
    quarter = jax.ShapeDtypeStruct((TOK // 2, D // 2), BF16)
    return pl.pallas_call(
        norm_body,
        out_shape=(jax.ShapeDtypeStruct((TOK, 1), F32), half, quarter, quarter),
        in_specs=[VM],
        out_specs=(VM,) * 4,
        compiler_params=pltpu.CompilerParams(vmem_limit_bytes=12 << 20),
        cost_estimate=pl.CostEstimate(flops=10 * TOK * D, bytes_accessed=4 << 20, transcendentals=0),
        name="norm",
    )(tokens)


def transpose_body(own, low, high, out):
    for b in range(8):
        cols = slice(b * HALF, (b + 1) * HALF)
        out[cols, :TOK] = own[:, cols].T
        out[cols, TOK:] = jnp.concatenate([low[:, cols], high[:, cols]], axis=0).T


def transpose(own, low, high):
    return pl.pallas_call(
        transpose_body,
        out_shape=jax.ShapeDtypeStruct((D // 2, 2 * TOK), BF16),
        in_specs=[VM] * 3,
        out_specs=VM,
        compiler_params=pltpu.CompilerParams(vmem_limit_bytes=6 << 20),
        cost_estimate=pl.CostEstimate(flops=4 * TOK * D, bytes_accessed=4 << 20, transcendentals=0),
        name="transpose",
    )(own, low, high)


def block(name, flip):
    x, y, z, c = where()
    turned = c ^ (z & 1)
    step = {"0": 0, "a": 1 + 2 * turned, "b": 3 - 2 * turned, "o": 2}[name]
    return (x ^ step) * 2 + ((y & 1) ^ flip)


def product(spots, feats, pieces):
    cols = [aligned(block(*spot) * HALF, HALF) for spot in spots]
    lhs = jnp.concatenate([jnp.concatenate([ref[:, k] for k in cols], axis=1) for ref in feats], axis=0)
    return dot(lhs, jnp.concatenate([p[...] for p in pieces], axis=0), ((1,), (0,)))


def part_body(spots, own, low, high, *refs):
    count = len(spots)
    pieces, old, outs = refs[:count], refs[count:-2], refs[-2:]
    part = product(spots, (own, low, high), pieces)
    for k, half in enumerate((part[:TOK], part[TOK:])):
        outs[k][...] = half + old[k][...] if old else half


def project(spots, feats, pieces, *old):
    count, out = len(pieces), jax.ShapeDtypeStruct((TOK, QKV), F32)
    return pl.pallas_call(
        lambda *refs: part_body(spots, *refs),
        out_shape=(out, out),
        in_specs=[VM] * (3 + count + len(old)),
        out_specs=(VM, VM),
        compiler_params=pltpu.CompilerParams(vmem_limit_bytes=12 << 20),
        cost_estimate=pl.CostEstimate(
            flops=4 * TOK * HALF * count * QKV, bytes_accessed=6 << 20, transcendentals=0
        ),
        name="project",
    )(*feats, *pieces, *old)


def late_body(spots, count, *refs):
    feats, pieces, old, out = refs[:count], refs[count:-2], refs[-2], refs[-1]
    out[...] = (old[...] + product(spots, feats, pieces)).astype(out.dtype)


def project_late(spots, feats, pieces, old, dtype):
    count = len(feats)
    return pl.pallas_call(
        lambda *refs: late_body(spots, count, *refs),
        out_shape=jax.ShapeDtypeStruct((TOK, QKV), dtype),
        in_specs=[VM] * (1 + count + len(pieces)),
        out_specs=VM,
        compiler_params=pltpu.CompilerParams(vmem_limit_bytes=8 << 20),
        cost_estimate=pl.CostEstimate(
            flops=2 * TOK * HALF * len(pieces) * QKV, bytes_accessed=4 << 20, transcendentals=0
        ),
        name="project_late",
    )(*feats, *pieces, old)


def visible(doc):
    rows = lax.broadcasted_iota(jnp.int32, (TOK, TOK), 0)
    cols = lax.broadcasted_iota(jnp.int32, (TOK, TOK), 1)
    along = jnp.broadcast_to(doc[...], (TOK, TOK))
    return (cols <= rows) & (along == along.T)


def turn(value, cos, sin):
    return value * cos + pltpu.roll(value, HD // 2, 1) * sin


def head_grads(q_rot, g, k_rot, val, seen, count):
    scale = HD**-0.5
    scores = dot(q_rot, k_rot, ((1,), (1,))).reshape(count, TOK, TOK)
    scores = jnp.where(seen[None], scores, -1e30)
    expo = jnp.exp((scores - jnp.max(scores, axis=2, keepdims=True)) * scale)
    probs = expo * (1.0 / jnp.sum(expo, axis=2, keepdims=True))
    d_probs = dot(g, val, ((1,), (1,))).reshape(count, TOK, TOK)
    delta = jnp.sum(d_probs * probs, axis=2, keepdims=True)
    d_scores = (probs * (d_probs - delta)).astype(BF16).reshape(count * TOK, TOK)
    probs = probs.astype(BF16).reshape(count * TOK, TOK)
    d_val = dot(probs, g, ((0,), (0,)))
    d_key = dot(d_scores, q_rot, ((0,), (0,)))
    return dot(d_scores, k_rot, ((1,), (0,))) * scale, d_key, d_val


def attend_low_body(own, came, grad, doc, cosine, sine, out, rest, d_key, d_val, qkv):
    qkv[...] = own[...] + came[...].astype(F32)
    cos, sin = cosine[...], sine[...]
    seen = visible(doc)
    k_rot = turn(qkv[:, OUTW : OUTW + HD], cos, sin).astype(BF16)
    val = qkv[:, OUTW + HD :].astype(BF16)
    q_rot = [turn(qkv[:, h * HD : (h + 1) * HD], cos, sin).astype(BF16) for h in range(QH)]
    g = jnp.concatenate([grad[:, h * HD : (h + 1) * HD] for h in range(LOW)], axis=0)
    stacked = jnp.concatenate(q_rot[:LOW], axis=0)
    d_query, d_key[...], d_val[...] = head_grads(stacked, g, k_rot, val, seen, LOW)
    for h in range(LOW):
        out[:, h * HD : (h + 1) * HD] = turn(d_query[h * TOK : (h + 1) * TOK], cos, -sin).astype(BF16)
    for h in range(LOW, QH):
        rest[:, (h - LOW) * HD : (h - LOW + 1) * HD] = q_rot[h]
    rest[:, COLS - 2 * HD : COLS - HD] = k_rot
    rest[:, COLS - HD :] = val


def attend_high_body(rest, key_low, val_low, grad, doc, cosine, sine, out):
    cos, sin = cosine[...], sine[...]
    k_rot, val = rest[:, COLS - 2 * HD : COLS - HD], rest[:, COLS - HD :]
    count = QH - LOW
    g = jnp.concatenate([grad[:, h * HD : (h + 1) * HD] for h in range(LOW, QH)], axis=0)
    stacked = jnp.concatenate([rest[:, k * HD : (k + 1) * HD] for k in range(count)], axis=0)
    d_query, key, value = head_grads(stacked, g, k_rot, val, visible(doc), count)
    for k in range(count):
        out[:, k * HD : (k + 1) * HD] = turn(d_query[k * TOK : (k + 1) * TOK], cos, -sin).astype(BF16)
    total_key = (key_low[...] + key) * HD**-0.5
    out[:, COLS - 2 * HD : COLS - HD] = turn(total_key, cos, -sin).astype(BF16)
    out[:, COLS - HD :] = (val_low[...] + value).astype(BF16)


def attend_cost(heads):
    return pl.CostEstimate(
        flops=10 * TOK * TOK * HD * heads, bytes_accessed=4 << 20, transcendentals=TOK * TOK * heads
    )


def attend_low(own, came, grad, doc):
    wide, half = jax.ShapeDtypeStruct((TOK, COLS), BF16), jax.ShapeDtypeStruct((TOK, HD), F32)
    return pl.pallas_call(
        attend_low_body,
        out_shape=(wide, wide, half, half),
        in_specs=[VM] * 6,
        out_specs=(VM,) * 4,
        scratch_shapes=[pltpu.VMEM((TOK, QKV), F32)],
        compiler_params=pltpu.CompilerParams(vmem_limit_bytes=12 << 20),
        cost_estimate=attend_cost(LOW),
        name="attend_low",
    )(own, came, grad, doc, *TABLES)


def attend_high(rest, d_key, d_val, grad, doc):
    return pl.pallas_call(
        attend_high_body,
        out_shape=jax.ShapeDtypeStruct((TOK, COLS), BF16),
        in_specs=[VM] * 7,
        out_specs=VM,
        compiler_params=pltpu.CompilerParams(vmem_limit_bytes=12 << 20),
        cost_estimate=attend_cost(QH - LOW),
        name="attend_high",
    )(rest, d_key, d_val, grad, doc, *TABLES)


def normed_body(spots, low, low_other, high, high_other, *refs):
    pieces, own, send = refs[: len(spots)], refs[-2], refs[-1]
    for lower, higher, out in ((low_other, high_other, send), (low, high, own)):
        d_qkv = jnp.concatenate([lower[...], higher[...]], axis=1)
        for spot, piece in zip(spots, pieces):
            part = dot(d_qkv, piece[...], ((1,), (1,)))
            out[:, aligned(block(*spot) * HALF, HALF)] = part.astype(out.dtype)


def normed_grad(spots, grads, pieces):
    count = len(pieces)
    return pl.pallas_call(
        lambda *refs: normed_body(spots, *refs),
        out_shape=(
            jax.ShapeDtypeStruct((TOK, D // 2), F32),
            jax.ShapeDtypeStruct((TOK, D // 2), BF16),
        ),
        in_specs=[VM] * (4 + count),
        out_specs=(VM, VM),
        compiler_params=pltpu.CompilerParams(vmem_limit_bytes=12 << 20),
        cost_estimate=pl.CostEstimate(flops=2 * TOK * D * QKV, bytes_accessed=8 << 20, transcendentals=0),
        name="normed_grad",
    )(*grads, *pieces)


def tokens_body(own, came, tokens, scale_r, out):
    c = lax.axis_index("core")
    places = [
        (aligned(b * BLK + side * HALF, HALF), ref, slice(b * HALF, (b + 1) * HALF))
        for b in range(8)
        for side, ref in ((c, own), (1 - c, came))
    ]
    total = jnp.zeros((TOK, HALF), F32)
    for cols, ref, here in places:
        total = total + ref[:, here].astype(F32) * tokens[:, cols].astype(F32)
    r = scale_r[...]
    back = r * r * r * (jnp.sum(total, axis=1, keepdims=True) * (1.0 / D))
    for cols, ref, here in places:
        out[:, cols] = (r * ref[:, here].astype(F32) - tokens[:, cols].astype(F32) * back).astype(BF16)


def tokens_grad(own, came, tokens, scale_r):
    return pl.pallas_call(
        tokens_body,
        out_shape=jax.ShapeDtypeStruct((TOK, D), BF16),
        in_specs=[VM] * 4,
        out_specs=VM,
        compiler_params=pltpu.CompilerParams(vmem_limit_bytes=8 << 20),
        cost_estimate=pl.CostEstimate(flops=10 * TOK * D, bytes_accessed=8 << 20, transcendentals=0),
        name="tokens_grad",
    )(own, came, tokens, scale_r)


def term_product(along_x, level, feats, d_own, d_other):
    x, y, z, c = where()
    order = (0, 3 - 2 * c, 1 + 2 * c, 2)
    rows = []
    for first in (2 * level, 2 * level + 1):
        for second in range(4):
            i, j = (first, second) if along_x else (second, first)
            yy = y ^ order[j]
            start = ((x ^ order[i]) * 2 + (yy & 1)) * HALF + (yy >> 1) * QUART
            rows.append(feats[aligned(start, QUART), :])
    right = jnp.concatenate([d_own[...], d_other[...]], axis=0)
    return dot(jnp.concatenate(rows, axis=0), right, ((1,), (0,))).reshape(8, QUART, COLS)


def term_body(along_x, level, feats, d_own, d_other, out):
    out[...] = term_product(along_x, level, feats, d_own, d_other).astype(BF16)


def terms(along_x, level, made):
    return pl.pallas_call(
        lambda *refs: term_body(along_x, level, *refs),
        out_shape=jax.ShapeDtypeStruct((8, QUART, COLS), BF16),
        in_specs=[VM] * 3,
        out_specs=VM,
        compiler_params=pltpu.CompilerParams(vmem_limit_bytes=12 << 20),
        cost_estimate=pl.CostEstimate(
            flops=2 * 8 * QUART * COLS * 2 * TOK, bytes_accessed=4 << 20, transcendentals=0
        ),
        name="terms",
    )(*made)


def add_body(parts, cuts, *refs):
    total = sum(ref[first : first + count].astype(F32) for ref, (first, count) in zip(refs, parts)).astype(BF16)
    for out, (first, count) in zip(refs[len(parts) :], cuts):
        out[...] = total[first : first + count]


def add(parts, cuts):
    arrays, spans = [part[0] for part in parts], [part[1:] for part in parts]
    return pl.pallas_call(
        lambda *refs: add_body(spans, cuts, *refs),
        out_shape=tuple(jax.ShapeDtypeStruct((count, QUART, COLS), BF16) for _, count in cuts),
        in_specs=[VM] * len(parts),
        out_specs=(VM,) * len(cuts),
        compiler_params=pltpu.CompilerParams(vmem_limit_bytes=6 << 20),
        cost_estimate=pl.CostEstimate(flops=1 << 20, bytes_accessed=1 << 20, transcendentals=0),
        name="add",
    )(*arrays)


def join_body(old_x, came_x, old_y, came_y, out):
    out[:, :, :COLS] = (old_x[...].astype(F32) + came_x[...].astype(F32)).astype(BF16).reshape(8, PIECE, COLS)
    out[:, :, COLS:] = (old_y[...].astype(F32) + came_y[...].astype(F32)).astype(BF16).reshape(8, PIECE, COLS)


def join(*parts):
    return pl.pallas_call(
        join_body,
        out_shape=jax.ShapeDtypeStruct((8, PIECE, QKV), BF16),
        in_specs=[VM] * 4,
        out_specs=VM,
        compiler_params=pltpu.CompilerParams(vmem_limit_bytes=4 << 20),
        name="join",
    )(*parts)


def finish_body(parts, out):
    total = sum(parts[i].astype(F32) for i in range(8)).astype(BF16)
    for i in range(16):
        out[i] = total


def finish(parts):
    return pl.pallas_call(
        finish_body,
        out_shape=jax.ShapeDtypeStruct((16, PIECE, QKV), BF16),
        in_specs=[VM],
        out_specs=VM,
        compiler_params=pltpu.CompilerParams(vmem_limit_bytes=4 << 20),
        name="finish",
    )(parts)


def squares_body(got, out):
    total = jnp.zeros((PIECE, 128), F32)
    for i in range(16):
        value = got[i].astype(F32)
        value = value * value
        for k in range(0, QKV, 128):
            total = total + value[:, k : k + 128]
    out[...] = jnp.broadcast_to((total[:8] + total[8:])[None], (16, 8, 128))


def squares(got):
    return pl.pallas_call(
        squares_body,
        out_shape=jax.ShapeDtypeStruct((16, 8, 128), F32),
        in_specs=[VM],
        out_specs=VM,
        compiler_params=pltpu.CompilerParams(vmem_limit_bytes=4 << 20),
        name="squares",
    )(got)


def rescale_body(parts, mine, theirs, out, held, sems):
    total = sum(parts[i] for i in range(16))
    total = jnp.sum(jnp.sum(total, axis=1, keepdims=True), axis=0, keepdims=True)
    factor = target_rms * lax.rsqrt(total * (1.0 / (D * QKV)) + 1e-06)
    c = lax.axis_index("core")
    copies = []
    for side, half in ((c, mine), (1 - c, theirs)):
        for k in range(2):
            i = len(copies)
            part = half[8 * k : 8 * (k + 1)].reshape(QUART, QKV)
            held[i] = (part.astype(F32) * factor).astype(BF16)
            rows = aligned(side * HALF + k * QUART, QUART)
            copies.append(pltpu.make_async_copy(held.at[i], out.at[rows, :], sems.at[i]))
            copies[-1].start()
    for copy in copies:
        copy.wait()


def rescale(parts, mine, theirs):
    return pl.pallas_call(
        rescale_body,
        out_shape=jax.ShapeDtypeStruct((BLK, QKV), BF16),
        in_specs=[VM] * 3,
        out_specs=pl.BlockSpec(memory_space=pl.ANY),
        scratch_shapes=[pltpu.VMEM((4, QUART, QKV), BF16), pltpu.SemaphoreType.DMA((4,))],
        compiler_params=pltpu.CompilerParams(vmem_limit_bytes=8 << 20),
        name="rescale",
    )(parts, mine, theirs)


def tables():
    freq = np.exp(-np.log(rope_base) * 2.0 * np.arange(HD // 2) / HD)
    angle = np.arange(TOK)[:, None] * freq[None, :]
    cos, sin = np.cos(angle), np.sin(angle)
    return np.concatenate([cos, cos], 1).astype(np.float32), np.concatenate([-sin, sin], 1).astype(np.float32)


TABLES = tables()

def on_device(tokens, grad_attended, doc_ids, w_own):
    w00 = lax.dynamic_slice_in_dim(w_own, lax.axis_index("core") * HALF, HALF, 0)
    w00, tokens = lax.optimization_barrier((w00, tokens))
    wa0 = swap(w00, gather_x1)
    w01 = swap(w00, flip_y)
    scale_r, own, send_low, send_high = norm(tokens)
    other = [swap(send, other_core) for send in (send_low, send_high)]
    wa0, w01, own, other = lax.optimization_barrier((wa0, w01, own, other))
    both = (own, *other)
    wo0 = swap(wa0, gather_x2)
    wa1 = swap(wa0, flip_y)
    wb0 = swap(wa0, pair_z)
    early, early_spots = [w00, w01, wa0], [("0", 0), ("0", 1), ("a", 0)]
    part_own, part_other = project(early_spots, both, early)
    feats = transpose(*both)
    wo0, wa1, part_own, part_other, feats = lax.optimization_barrier((wo0, wa1, part_own, part_other, feats))
    wo1 = swap(wo0, flip_y)
    wb1 = swap(wa1, pair_z)
    middle, middle_spots = [wo0, wa1, wb0], [("o", 0), ("a", 1), ("b", 0)]
    part_own, part_other = project(middle_spots, both, middle, part_own, part_other)
    wo1, wb1, part_own, part_other = lax.optimization_barrier((wo1, wb1, part_own, part_other))
    late, late_spots = [wo1, wb1], [("o", 1), ("b", 1)]
    late_other = project_late(late_spots, other, late, part_other, BF16)
    came = swap(late_other, other_core)
    late_other, part_own = lax.optimization_barrier((late_other, part_own))
    qkv = project_late(late_spots, [own], late, part_own, F32)
    d_low, rest, d_key, d_val = attend_low(qkv, came, grad_attended, doc_ids)

    low_other = swap(d_low, other_core)
    d_high = attend_high(rest, d_key, d_val, grad_attended, doc_ids)
    low_other, d_high = lax.optimization_barrier((low_other, d_high))
    high_other = swap(d_high, other_core)
    lows, highs = (feats, d_low, low_other), (feats, d_high, high_other)
    came_x = swap(terms(True, 1, lows), x_1)
    sent_y = terms(False, 1, highs)
    came_y = swap(sent_y, y_1)
    spots, pieces = early_spots + middle_spots + late_spots, early + middle + late
    sent_y, lows, highs = lax.optimization_barrier((sent_y, lows, highs))
    sum_x, sum_y = terms(True, 0, lows), terms(False, 0, highs)
    normed_own, normed_send = normed_grad(spots, (*lows[1:], *highs[1:]), pieces)
    normed_came = swap(normed_send, other_core)
    normed_came, sum_x, sum_y = lax.optimization_barrier((normed_came, sum_x, sum_y))
    d_tokens = tokens_grad(normed_own, normed_came, tokens, scale_r)
    came_x, sum_x, sum_y, d_tokens = lax.optimization_barrier((came_x, sum_x, sum_y, d_tokens))
    first, second = add([(sum_x, 4, 4), (came_x, 4, 4)], [(2, 2), (0, 2)])
    pass_x, keep_x = swap(first, x_2), swap(second, x_2)
    first, second = add([(sum_y, 4, 4), (came_y, 4, 4)], [(2, 2), (0, 2)])
    pass_y, keep_y = swap(first, y_2), swap(second, y_2)
    (sent,) = add([(sum_x, 2, 2), (came_x, 2, 2), (pass_x, 0, 2)], [(0, 2)])
    pass_x = swap(sent, y_1)
    (sent,) = add([(sum_y, 2, 2), (came_y, 2, 2), (pass_y, 0, 2)], [(0, 2)])
    pass_y = swap(sent, x_1)
    sum_x, sent = add([(sum_x, 0, 2), (came_x, 0, 2), (keep_x, 0, 2), (pass_x, 0, 2)], [(0, 1), (1, 1)])
    came_x = swap(sent, y_2)
    sum_y, sent = add([(sum_y, 0, 2), (came_y, 0, 2), (keep_y, 0, 2), (pass_y, 0, 2)], [(0, 1), (1, 1)])
    came_y = swap(sent, x_2)

    total = join(sum_x, came_x, sum_y, came_y)
    got = finish(lax.all_to_all(total, "z", 0, 0))
    got = lax.all_to_all(got, ("y_hi", "z"), 0, 0)

    theirs = swap(got, other_core)
    parts = lax.all_to_all(squares(got), ("x", "y_lo", "core"), 0, 0)
    return d_tokens, rescale(parts, got, theirs)


def solution(mesh):
    mesh = Mesh(mesh.devices.reshape(SIZES), AXES)
    spread, rows = P(AXES, None), P(AXES[:2], None)
    return jax.shard_map(
        on_device,
        mesh=mesh,
        in_specs=(spread, spread, spread, rows),
        out_specs=(spread, rows),
        check_vma=False,
    )
```

```python
import jax
import jax.numpy as jnp
import numpy as np
from jax import lax
from jax.experimental import pallas as pl
from jax.experimental.pallas import tpu as pltpu
from jax.sharding import Mesh
from jax.sharding import PartitionSpec as P

D = 4096
HD = 128
QH = 8
QKV = 1280
TOK = 256
BLK = D // 8
HALF = BLK // 2
QUART = HALF // 2
PIECE = QUART // 8
COLS = QKV // 2
OUTW = QH * HD
LOW = COLS // HD

AXES = ("x", "y_lo", "y_hi", "z", "core")
SIZES = (4, 2, 2, 8, 2)
target_rms = 0.5
rope_base = 500000.0
F32 = jnp.float32
BF16 = jnp.bfloat16


def flat(x, y, z, c):
    return (x * 2 + y % 2) * 32 + (y // 2) * 16 + z * 2 + c


def swap(value, partner):
    pairs = []
    for x in range(4):
        for y in range(4):
            for z in range(8):
                for c in range(2):
                    pairs.append((flat(x, y, z, c), flat(*partner(x, y, z, c))))
    return lax.ppermute(value, AXES, pairs)


def near(c):
    return 1 if c == 0 else 3


def other_core(x, y, z, c):
    return x, y, z, 1 - c


def gather_x1(x, y, z, c):
    return x ^ near(c ^ (z & 1)), y, z, c


def gather_x2(x, y, z, c):
    return x ^ (4 - near(c ^ (z & 1))), y, z, c


def flip_y(x, y, z, c):
    return x, y ^ near(c), z, c


def pair_z(x, y, z, c):
    return x, y, (z ^ 1) if c == 0 else ((z + 1) % 8 if z % 2 else (z - 1) % 8), c


def x_1(x, y, z, c):
    return x ^ near(c), y, z, c


def x_2(x, y, z, c):
    return x ^ (4 - near(c)), y, z, c


def y_1(x, y, z, c):
    return x, y ^ near(c), z, c


def y_2(x, y, z, c):
    return x, y ^ (4 - near(c)), z, c


VM = pl.BlockSpec(memory_space=pltpu.VMEM)
SM = pl.BlockSpec(memory_space=pltpu.SMEM)


def dot(a, b, dims):
    return lax.dot_general(a, b, (dims, ((), ())), preferred_element_type=F32)


def where():
    x, y_lo, y_hi, z, c = (lax.axis_index(axis) for axis in AXES)
    return x, y_hi * 2 + y_lo, z, c


def aligned(start, size):
    return pl.ds(pl.multiple_of(start, size), size)


def norm_body(tokens, scale_r, own, send_low, send_high):
    full = tokens[...].astype(F32)
    r = lax.rsqrt(jnp.sum(full * full, axis=1, keepdims=True) * (1.0 / D) + 1e-05)
    scale_r[...] = r
    c = lax.axis_index("core")
    for b in range(8):
        here = slice(b * HALF, (b + 1) * HALF)
        for side in (c, 1 - c):
            part = (tokens[:, aligned(b * BLK + side * HALF, HALF)].astype(F32) * r).astype(BF16)
            if side is c:
                own[:, here] = part
            else:
                send_low[:, here] = part[: TOK // 2]
                send_high[:, here] = part[TOK // 2 :]


def norm(tokens):
    half = jax.ShapeDtypeStruct((TOK, D // 2), BF16)
    quarter = jax.ShapeDtypeStruct((TOK // 2, D // 2), BF16)
    return pl.pallas_call(
        norm_body,
        out_shape=(jax.ShapeDtypeStruct((TOK, 1), F32), half, quarter, quarter),
        in_specs=[VM],
        out_specs=(VM,) * 4,
        compiler_params=pltpu.CompilerParams(vmem_limit_bytes=12 << 20),
        cost_estimate=pl.CostEstimate(flops=10 * TOK * D, bytes_accessed=4 << 20, transcendentals=0),
        name="norm",
    )(tokens)


def transpose_body(own, low, high, out):
    for b in range(8):
        cols = slice(b * HALF, (b + 1) * HALF)
        out[cols, :TOK] = own[:, cols].T
        out[cols, TOK:] = jnp.concatenate([low[:, cols], high[:, cols]], axis=0).T


def transpose(own, low, high):
    return pl.pallas_call(
        transpose_body,
        out_shape=jax.ShapeDtypeStruct((D // 2, 2 * TOK), BF16),
        in_specs=[VM] * 3,
        out_specs=VM,
        compiler_params=pltpu.CompilerParams(vmem_limit_bytes=6 << 20),
        cost_estimate=pl.CostEstimate(flops=4 * TOK * D, bytes_accessed=4 << 20, transcendentals=0),
        name="transpose",
    )(own, low, high)


def block(name, flip):
    x, y, z, c = where()
    turned = c ^ (z & 1)
    step = {"0": 0, "a": 1 + 2 * turned, "b": 3 - 2 * turned, "o": 2}[name]
    return (x ^ step) * 2 + ((y & 1) ^ flip)


def product(spots, feats, pieces):
    cols = [aligned(block(*spot) * HALF, HALF) for spot in spots]
    lhs = jnp.concatenate([jnp.concatenate([ref[:, k] for k in cols], axis=1) for ref in feats], axis=0)
    return dot(lhs, jnp.concatenate([piece[...] for piece in pieces], axis=0), ((1,), (0,)))


def part_body(spots, own, low, high, *refs):
    count = 2 * len(spots)
    pieces, old, outs = refs[:count], refs[count:-2], refs[-2:]
    part = product(spots, (own, low, high), pieces)
    for k, half in enumerate((part[:TOK], part[TOK:])):
        outs[k][...] = half + old[k][...] if old else half


def project(spots, feats, pieces, *old):
    count, out = len(pieces), jax.ShapeDtypeStruct((TOK, QKV), F32)
    return pl.pallas_call(
        lambda *refs: part_body(spots, *refs),
        out_shape=(out, out),
        in_specs=[VM] * (3 + count + len(old)),
        out_specs=(VM, VM),
        compiler_params=pltpu.CompilerParams(vmem_limit_bytes=12 << 20),
        cost_estimate=pl.CostEstimate(
            flops=4 * TOK * HALF * count * QKV, bytes_accessed=6 << 20, transcendentals=0
        ),
        name="project",
    )(*feats, *pieces, *old)


def late_body(spots, count, *refs):
    feats, pieces, old, out = refs[:count], refs[count:-2], refs[-2], refs[-1]
    out[...] = (old[...] + product(spots, feats, pieces)).astype(out.dtype)


def project_late(spots, feats, pieces, old, dtype):
    count = len(feats)
    return pl.pallas_call(
        lambda *refs: late_body(spots, count, *refs),
        out_shape=jax.ShapeDtypeStruct((TOK, QKV), dtype),
        in_specs=[VM] * (1 + count + len(pieces)),
        out_specs=VM,
        compiler_params=pltpu.CompilerParams(vmem_limit_bytes=8 << 20),
        cost_estimate=pl.CostEstimate(
            flops=2 * TOK * HALF * len(pieces) * QKV, bytes_accessed=4 << 20, transcendentals=0
        ),
        name="project_late",
    )(*feats, *pieces, old)


def visible(doc):
    rows = lax.broadcasted_iota(jnp.int32, (TOK, TOK), 0)
    cols = lax.broadcasted_iota(jnp.int32, (TOK, TOK), 1)
    along = jnp.broadcast_to(doc[...], (TOK, TOK))
    return (cols <= rows) & (along == along.T)


def turn(value, cos, sin):
    return value * cos + pltpu.roll(value, HD // 2, 1) * sin


def head_grads(q_rot, g, k_rot, val, seen, count):
    scale = HD**-0.5
    scores = dot(q_rot, k_rot, ((1,), (1,))).reshape(count, TOK, TOK)
    scores = jnp.where(seen[None], scores, -1e30)
    expo = jnp.exp((scores - jnp.max(scores, axis=2, keepdims=True)) * scale)
    probs = expo * (1.0 / jnp.sum(expo, axis=2, keepdims=True))
    d_probs = dot(g, val, ((1,), (1,))).reshape(count, TOK, TOK)
    delta = jnp.sum(d_probs * probs, axis=2, keepdims=True)
    d_scores = (probs * (d_probs - delta)).astype(BF16).reshape(count * TOK, TOK)
    probs = probs.astype(BF16).reshape(count * TOK, TOK)
    d_val = dot(probs, g, ((0,), (0,)))
    d_key = dot(d_scores, q_rot, ((0,), (0,)))
    return dot(d_scores, k_rot, ((1,), (0,))) * scale, d_key, d_val


def attend_low_body(own, came, grad, doc, cosine, sine, out, rest, d_key, d_val, qkv):
    qkv[...] = own[...] + came[...].astype(F32)
    cos, sin = cosine[...], sine[...]
    seen = visible(doc)
    k_rot = turn(qkv[:, OUTW : OUTW + HD], cos, sin).astype(BF16)
    val = qkv[:, OUTW + HD :].astype(BF16)
    q_rot = [turn(qkv[:, h * HD : (h + 1) * HD], cos, sin).astype(BF16) for h in range(QH)]
    g = jnp.concatenate([grad[:, h * HD : (h + 1) * HD] for h in range(LOW)], axis=0)
    stacked = jnp.concatenate(q_rot[:LOW], axis=0)
    d_query, d_key[...], d_val[...] = head_grads(stacked, g, k_rot, val, seen, LOW)
    for h in range(LOW):
        out[:, h * HD : (h + 1) * HD] = turn(d_query[h * TOK : (h + 1) * TOK], cos, -sin).astype(BF16)
    for h in range(LOW, QH):
        rest[:, (h - LOW) * HD : (h - LOW + 1) * HD] = q_rot[h]
    rest[:, COLS - 2 * HD : COLS - HD] = k_rot
    rest[:, COLS - HD :] = val


def attend_high_body(rest, key_low, val_low, grad, doc, cosine, sine, out):
    cos, sin = cosine[...], sine[...]
    k_rot, val = rest[:, COLS - 2 * HD : COLS - HD], rest[:, COLS - HD :]
    count = QH - LOW
    g = jnp.concatenate([grad[:, h * HD : (h + 1) * HD] for h in range(LOW, QH)], axis=0)
    stacked = jnp.concatenate([rest[:, k * HD : (k + 1) * HD] for k in range(count)], axis=0)
    d_query, key, value = head_grads(stacked, g, k_rot, val, visible(doc), count)
    for k in range(count):
        out[:, k * HD : (k + 1) * HD] = turn(d_query[k * TOK : (k + 1) * TOK], cos, -sin).astype(BF16)
    total_key = (key_low[...] + key) * HD**-0.5
    out[:, COLS - 2 * HD : COLS - HD] = turn(total_key, cos, -sin).astype(BF16)
    out[:, COLS - HD :] = (val_low[...] + value).astype(BF16)


def attend_cost(heads):
    return pl.CostEstimate(
        flops=10 * TOK * TOK * HD * heads, bytes_accessed=4 << 20, transcendentals=TOK * TOK * heads
    )


def attend_low(own, came, grad, doc):
    wide, half = jax.ShapeDtypeStruct((TOK, COLS), BF16), jax.ShapeDtypeStruct((TOK, HD), F32)
    return pl.pallas_call(
        attend_low_body,
        out_shape=(wide, wide, half, half),
        in_specs=[VM] * 6,
        out_specs=(VM,) * 4,
        scratch_shapes=[pltpu.VMEM((TOK, QKV), F32)],
        compiler_params=pltpu.CompilerParams(vmem_limit_bytes=12 << 20),
        cost_estimate=attend_cost(LOW),
        name="attend_low",
    )(own, came, grad, doc, *TABLES)


def attend_high(rest, d_key, d_val, grad, doc):
    return pl.pallas_call(
        attend_high_body,
        out_shape=jax.ShapeDtypeStruct((TOK, COLS), BF16),
        in_specs=[VM] * 7,
        out_specs=VM,
        compiler_params=pltpu.CompilerParams(vmem_limit_bytes=12 << 20),
        cost_estimate=attend_cost(QH - LOW),
        name="attend_high",
    )(rest, d_key, d_val, grad, doc, *TABLES)


def normed_body(spots, low, low_other, high, high_other, *refs):
    count = 2 * len(spots)
    pieces, own, send = refs[:count], refs[-2], refs[-1]
    for lower, higher, out in ((low_other, high_other, send), (low, high, own)):
        d_qkv = jnp.concatenate([lower[...], higher[...]], axis=1)
        for i, spot in enumerate(spots):
            piece = jnp.concatenate([pieces[2 * i][...], pieces[2 * i + 1][...]], axis=0)
            out[:, aligned(block(*spot) * HALF, HALF)] = dot(d_qkv, piece, ((1,), (1,))).astype(out.dtype)


def normed_grad(spots, grads, pieces):
    return pl.pallas_call(
        lambda *refs: normed_body(spots, *refs),
        out_shape=(
            jax.ShapeDtypeStruct((TOK, D // 2), F32),
            jax.ShapeDtypeStruct((TOK, D // 2), BF16),
        ),
        in_specs=[VM] * (4 + len(pieces)),
        out_specs=(VM, VM),
        compiler_params=pltpu.CompilerParams(vmem_limit_bytes=12 << 20),
        cost_estimate=pl.CostEstimate(flops=2 * TOK * D * QKV, bytes_accessed=8 << 20, transcendentals=0),
        name="normed_grad",
    )(*grads, *pieces)


def tokens_body(own, came, tokens, scale_r, out):
    c = lax.axis_index("core")
    places = [
        (aligned(b * BLK + side * HALF, HALF), ref, slice(b * HALF, (b + 1) * HALF))
        for b in range(8)
        for side, ref in ((c, own), (1 - c, came))
    ]
    total = jnp.zeros((TOK, HALF), F32)
    for cols, ref, here in places:
        total = total + ref[:, here].astype(F32) * tokens[:, cols].astype(F32)
    r = scale_r[...]
    back = r * r * r * (jnp.sum(total, axis=1, keepdims=True) * (1.0 / D))
    for cols, ref, here in places:
        out[:, cols] = (r * ref[:, here].astype(F32) - tokens[:, cols].astype(F32) * back).astype(BF16)


def tokens_grad(own, came, tokens, scale_r):
    return pl.pallas_call(
        tokens_body,
        out_shape=jax.ShapeDtypeStruct((TOK, D), BF16),
        in_specs=[VM] * 4,
        out_specs=VM,
        compiler_params=pltpu.CompilerParams(vmem_limit_bytes=8 << 20),
        cost_estimate=pl.CostEstimate(flops=10 * TOK * D, bytes_accessed=8 << 20, transcendentals=0),
        name="tokens_grad",
    )(own, came, tokens, scale_r)


def term_product(along_x, level, feats, d_own, d_other):
    x, y, z, c = where()
    order = (0, 3 - 2 * c, 1 + 2 * c, 2)
    rows = []
    for first in (2 * level, 2 * level + 1):
        for second in range(4):
            i, j = (first, second) if along_x else (second, first)
            yy = y ^ order[j]
            start = ((x ^ order[i]) * 2 + (yy & 1)) * HALF + (yy >> 1) * QUART
            rows.append(feats[aligned(start, QUART), :])
    right = jnp.concatenate([d_own[...], d_other[...]], axis=0)
    return dot(jnp.concatenate(rows, axis=0), right, ((1,), (0,))).reshape(8, QUART, COLS)


def term_body(along_x, level, feats, d_own, d_other, out):
    out[...] = term_product(along_x, level, feats, d_own, d_other).astype(BF16)


def terms(along_x, level, made):
    return pl.pallas_call(
        lambda *refs: term_body(along_x, level, *refs),
        out_shape=jax.ShapeDtypeStruct((8, QUART, COLS), BF16),
        in_specs=[VM] * 3,
        out_specs=VM,
        compiler_params=pltpu.CompilerParams(vmem_limit_bytes=12 << 20),
        cost_estimate=pl.CostEstimate(
            flops=2 * 8 * QUART * COLS * 2 * TOK, bytes_accessed=4 << 20, transcendentals=0
        ),
        name="terms",
    )(*made)


def add_body(parts, cuts, *refs):
    total = sum(ref[first : first + count].astype(F32) for ref, (first, count) in zip(refs, parts)).astype(BF16)
    for out, (first, count) in zip(refs[len(parts) :], cuts):
        out[...] = total[first : first + count]


def add(parts, cuts):
    arrays, spans = [part[0] for part in parts], [part[1:] for part in parts]
    return pl.pallas_call(
        lambda *refs: add_body(spans, cuts, *refs),
        out_shape=tuple(jax.ShapeDtypeStruct((count, QUART, COLS), BF16) for _, count in cuts),
        in_specs=[VM] * len(parts),
        out_specs=(VM,) * len(cuts),
        compiler_params=pltpu.CompilerParams(vmem_limit_bytes=6 << 20),
        cost_estimate=pl.CostEstimate(flops=1 << 20, bytes_accessed=1 << 20, transcendentals=0),
        name="add",
    )(*arrays)


def join_body(old_x, came_x, old_y, came_y, out):
    out[:, :, :COLS] = (old_x[...].astype(F32) + came_x[...].astype(F32)).astype(BF16).reshape(8, PIECE, COLS)
    out[:, :, COLS:] = (old_y[...].astype(F32) + came_y[...].astype(F32)).astype(BF16).reshape(8, PIECE, COLS)


def join(*parts):
    return pl.pallas_call(
        join_body,
        out_shape=jax.ShapeDtypeStruct((8, PIECE, QKV), BF16),
        in_specs=[VM] * 4,
        out_specs=VM,
        compiler_params=pltpu.CompilerParams(vmem_limit_bytes=4 << 20),
        name="join",
    )(*parts)


def finish_body(parts, out):
    total = sum(parts[i].astype(F32) for i in range(8)).astype(BF16)
    for i in range(16):
        out[i] = total


def finish(parts):
    return pl.pallas_call(
        finish_body,
        out_shape=jax.ShapeDtypeStruct((16, PIECE, QKV), BF16),
        in_specs=[VM],
        out_specs=VM,
        compiler_params=pltpu.CompilerParams(vmem_limit_bytes=4 << 20),
        name="finish",
    )(parts)


def squares_body(got, out):
    total = jnp.zeros((PIECE, 128), F32)
    for i in range(16):
        value = got[i].astype(F32)
        value = value * value
        for k in range(0, QKV, 128):
            total = total + value[:, k : k + 128]
    out[...] = jnp.broadcast_to((total[:8] + total[8:])[None], (16, 8, 128))


def squares(got):
    return pl.pallas_call(
        squares_body,
        out_shape=jax.ShapeDtypeStruct((16, 8, 128), F32),
        in_specs=[VM],
        out_specs=VM,
        compiler_params=pltpu.CompilerParams(vmem_limit_bytes=4 << 20),
        name="squares",
    )(got)


def rescale_body(parts, mine, theirs, out, held, sems):
    total = sum(parts[i] for i in range(16))
    total = jnp.sum(jnp.sum(total, axis=1, keepdims=True), axis=0, keepdims=True)
    factor = target_rms * lax.rsqrt(total * (1.0 / (D * QKV)) + 1e-06)
    c = lax.axis_index("core")
    copies = []
    for side, half in ((c, mine), (1 - c, theirs)):
        for k in range(2):
            i = len(copies)
            part = half[8 * k : 8 * (k + 1)].reshape(QUART, QKV)
            held[i] = (part.astype(F32) * factor).astype(BF16)
            rows = aligned(side * HALF + k * QUART, QUART)
            copies.append(pltpu.make_async_copy(held.at[i], out.at[rows, :], sems.at[i]))
            copies[-1].start()
    for copy in copies:
        copy.wait()


def rescale(parts, mine, theirs):
    return pl.pallas_call(
        rescale_body,
        out_shape=jax.ShapeDtypeStruct((BLK, QKV), BF16),
        in_specs=[VM] * 3,
        out_specs=pl.BlockSpec(memory_space=pl.ANY),
        scratch_shapes=[pltpu.VMEM((4, QUART, QKV), BF16), pltpu.SemaphoreType.DMA((4,))],
        compiler_params=pltpu.CompilerParams(vmem_limit_bytes=8 << 20),
        name="rescale",
    )(parts, mine, theirs)


def tables():
    freq = np.exp(-np.log(rope_base) * 2.0 * np.arange(HD // 2) / HD)
    angle = np.arange(TOK)[:, None] * freq[None, :]
    cos, sin = np.cos(angle), np.sin(angle)
    return np.concatenate([cos, cos], 1).astype(np.float32), np.concatenate([-sin, sin], 1).astype(np.float32)


TABLES = tables()

def on_device(tokens, grad_attended, doc_ids, w_own):
    start = lax.axis_index("core") * HALF
    w00 = [lax.dynamic_slice_in_dim(w_own, start + k, QUART, 0) for k in (0, QUART)]
    w00, tokens = lax.optimization_barrier((w00, tokens))
    round_one = [lax.optimization_barrier((swap(part, gather_x1), swap(part, flip_y))) for part in w00]
    wa0, w01 = zip(*round_one)
    wb0, wo0, wa1 = zip(*[(swap(part, pair_z), swap(part, gather_x2), swap(part, flip_y)) for part in wa0])
    scale_r, own, send_low, send_high = norm(tokens)
    other = [swap(send, other_core) for send in (send_low, send_high)]
    both = (own, *other)
    wb1 = [swap(part, pair_z) for part in wa1]
    wo1 = [swap(wo0[0], flip_y), swap(wa1[1], gather_x2)]
    early, early_spots = [*w00, *w01, *wa0], [("0", 0), ("0", 1), ("a", 0)]
    middle, middle_spots = [*wo0, *wa1, *wb0], [("o", 0), ("a", 1), ("b", 0)]
    part_own, part_other = project(early_spots + middle_spots, both, early + middle)
    feats = transpose(*both)
    wo1, wb1, part_own, part_other = lax.optimization_barrier((wo1, wb1, part_own, part_other))
    late, late_spots = [*wo1, *wb1], [("o", 1), ("b", 1)]
    late_other = project_late(late_spots, other, late, part_other, BF16)
    came = swap(late_other, other_core)
    late_other, part_own = lax.optimization_barrier((late_other, part_own))
    qkv = project_late(late_spots, [own], late, part_own, F32)
    d_low, rest, d_key, d_val = attend_low(qkv, came, grad_attended, doc_ids)

    low_other = swap(d_low, other_core)
    d_high = attend_high(rest, d_key, d_val, grad_attended, doc_ids)
    low_other, d_high = lax.optimization_barrier((low_other, d_high))
    high_other = swap(d_high, other_core)
    lows, highs = (feats, d_low, low_other), (feats, d_high, high_other)
    came_x = swap(terms(True, 1, lows), x_1)
    sent_y = terms(False, 1, highs)
    came_y = swap(sent_y, y_1)
    spots, pieces = early_spots + middle_spots + late_spots, early + middle + late
    sent_y, lows, highs = lax.optimization_barrier((sent_y, lows, highs))
    sum_x, sum_y = terms(True, 0, lows), terms(False, 0, highs)
    normed_own, normed_send = normed_grad(spots, (*lows[1:], *highs[1:]), pieces)
    normed_came = swap(normed_send, other_core)
    normed_came, sum_x, sum_y = lax.optimization_barrier((normed_came, sum_x, sum_y))
    d_tokens = tokens_grad(normed_own, normed_came, tokens, scale_r)
    came_x, sum_x, sum_y, d_tokens = lax.optimization_barrier((came_x, sum_x, sum_y, d_tokens))
    first, second = add([(sum_x, 4, 4), (came_x, 4, 4)], [(2, 2), (0, 2)])
    pass_x, keep_x = swap(first, x_2), swap(second, x_2)
    first, second = add([(sum_y, 4, 4), (came_y, 4, 4)], [(2, 2), (0, 2)])
    pass_y, keep_y = swap(first, y_2), swap(second, y_2)
    (sent,) = add([(sum_x, 2, 2), (came_x, 2, 2), (pass_x, 0, 2)], [(0, 2)])
    pass_x = swap(sent, y_1)
    (sent,) = add([(sum_y, 2, 2), (came_y, 2, 2), (pass_y, 0, 2)], [(0, 2)])
    pass_y = swap(sent, x_1)
    sum_x, sent = add([(sum_x, 0, 2), (came_x, 0, 2), (keep_x, 0, 2), (pass_x, 0, 2)], [(0, 1), (1, 1)])
    came_x = swap(sent, y_2)
    sum_y, sent = add([(sum_y, 0, 2), (came_y, 0, 2), (keep_y, 0, 2), (pass_y, 0, 2)], [(0, 1), (1, 1)])
    came_y = swap(sent, x_2)

    total = join(sum_x, came_x, sum_y, came_y)
    got = finish(lax.all_to_all(total, "z", 0, 0))
    got = lax.all_to_all(got, ("y_hi", "z"), 0, 0)

    theirs = swap(got, other_core)
    parts = lax.all_to_all(squares(got), ("x", "y_lo", "core"), 0, 0)
    return d_tokens, rescale(parts, got, theirs)


def solution(mesh):
    mesh = Mesh(mesh.devices.reshape(SIZES), AXES)
    spread, rows = P(AXES, None), P(AXES[:2], None)
    return jax.shard_map(
        on_device,
        mesh=mesh,
        in_specs=(spread, spread, spread, rows),
        out_specs=(spread, rows),
        check_vma=False,
    )
```
